32 devices in a mesh: fsdp: 16 (over z, x, core), rep: 2 (over y).
Axes of the slice: x: 2, y: 2, z: 4, core: 2. Of those that a mesh axis runs over, the one named last changes fastest.
Arguments:
- pixels: bfloat16 [32768, 768], P(('fsdp', 'rep')), may hold values from -6 to 6
- image_tokens: int32 [32, 4], P(('fsdp', 'rep')), may hold values from 0 to 900, as said below
- patch_class: int32 [32, 4], P(('fsdp', 'rep')), may hold values from 0 to 1, as said below
- resize_coarse: bfloat16 [768, 3072], replicated, may hold values from -0.21875 to 0.21875
- resize_fine: bfloat16 [192, 3072], replicated, may hold values from -0.4375 to 0.4375
- w_base: float32 [3072, 768], P('fsdp'), may hold values from -0.109375 to 0.109375
- w_qkv: float32 [768, 2304], P('fsdp'), may hold values from -0.21875 to 0.21875
- w_proj: float32 [768, 768], P('fsdp'), may hold values from -0.4375 to 0.4375
- w_fc1: float32 [768, 3072], P('fsdp'), may hold values from -0.21875 to 0.21875
- w_fc2: float32 [3072, 768], P('fsdp'), may hold values from -0.109375 to 0.109375
- small_params: float32 [11, 768], P(None, 'fsdp')
- first_base: float32 [3072, 768], P('fsdp'), may hold values from -0.00048828125 to 0.00048828125
- first_qkv: float32 [768, 2304], P('fsdp'), may hold values from -0.00048828125 to 0.00048828125
- first_proj: float32 [768, 768], P('fsdp'), may hold values from -0.00048828125 to 0.00048828125
- first_fc1: float32 [768, 3072], P('fsdp'), may hold values from -0.00048828125 to 0.00048828125
- first_fc2: float32 [3072, 768], P('fsdp'), may hold values from -0.00048828125 to 0.00048828125
- first_small: float32 [11, 768], P(None, 'fsdp'), may hold values from -0.00048828125 to 0.00048828125
- second_base: float32 [3072, 768], P('fsdp'), may hold values from 5.611059e-09 to 2.2232499e-08
- second_qkv: float32 [768, 2304], P('fsdp'), may hold values from 5.611059e-09 to 2.2232499e-08
- second_proj: float32 [768, 768], P('fsdp'), may hold values from 5.611059e-09 to 2.2232499e-08
- second_fc1: float32 [768, 3072], P('fsdp'), may hold values from 5.611059e-09 to 2.2232499e-08
- second_fc2: float32 [3072, 768], P('fsdp'), may hold values from 5.611059e-09 to 2.2232499e-08
- second_small: float32 [11, 768], P(None, 'fsdp'), may hold values from 5.611059e-09 to 2.2232499e-08
- cotangent: bfloat16 [32768, 768], P(('fsdp', 'rep')), may hold values from -6 to 6
Outputs:
- activations: bfloat16 [32768, 768], P(('fsdp', 'rep'))
- pixel_grad: bfloat16 [32768, 768], P(('fsdp', 'rep'))
- grad_norm: float32 [], replicated
- base_new: float32 [3072, 768], P('fsdp')
- qkv_new: float32 [768, 2304], P('fsdp')
- proj_new: float32 [768, 768], P('fsdp')
- fc1_new: float32 [768, 3072], P('fsdp')
- fc2_new: float32 [3072, 768], P('fsdp')
- small_new: float32 [11, 768], P(None, 'fsdp')
- first_base_new: float32 [3072, 768], P('fsdp')
- first_qkv_new: float32 [768, 2304], P('fsdp')
- first_proj_new: float32 [768, 768], P('fsdp')
- first_fc1_new: float32 [768, 3072], P('fsdp')
- first_fc2_new: float32 [3072, 768], P('fsdp')
- first_small_new: float32 [11, 768], P(None, 'fsdp')
- second_base_new: float32 [3072, 768], P('fsdp')
- second_qkv_new: float32 [768, 2304], P('fsdp')
- second_proj_new: float32 [768, 768], P('fsdp')
- second_fc1_new: float32 [768, 3072], P('fsdp')
- second_fc2_new: float32 [3072, 768], P('fsdp')
- second_small_new: float32 [11, 768], P(None, 'fsdp')
The draws below stay inside these ranges and needn't reach their ends.
Inputs may be any that keep to these rules, and one draw needn't show every extreme that they name: `image_tokens`: each row holds either one image of 900 tokens with class 1 in slot 0 and empty slots after it, or one to 4 images of 225 tokens with class 0 in the first slots and empty slots (0 tokens) after them; every draw has at least one fine image. `patch_class`: 1 only in slot 0 of a row holding a fine image.
All inputs are finite; a program needn't handle non-finite values.
Results may differ from the reference program's by a relative error of at most 0.019.
Values may be sent and summed in bfloat16 or wider, within the bound.
No kernel may reach another device: no remote copies, remote signals or barrier semaphores. Data moves between devices by JAX's collectives and lax.ppermute only.
A program may use at most 256 MiB of HBM per device.

```python
import math
import jax
import jax.numpy as jnp
from jax import lax

D = 768
HEADS = 12
HEAD_DIM = 64
FF = 3072
PIXB = 3072
PIXC = 768
PIXF = 192
TOK_DEV = 1024
FINE_LEN = 900
COARSE_LEN = 225
STEP = 10
IMG_DEV = 4
DEVICES_ROWS = 32
TOKENS = 32768
PARAMS = 9445632


def image_plan(key):
    key_roll, key_pick, key_count = jax.random.split(key, 3)
    roll = jax.random.randint(key_roll, (DEVICES_ROWS,), 0, 8)
    pick = jax.random.randint(key_pick, (), 0, DEVICES_ROWS)
    index = jnp.arange(DEVICES_ROWS, dtype=jnp.int32)
    has_fine = (roll == 0) | (index == pick)
    count = jax.random.randint(key_count, (DEVICES_ROWS,), 1, IMG_DEV + 1)
    slots = jnp.arange(IMG_DEV, dtype=jnp.int32)
    coarse_lengths = jnp.where(slots[None, :] < count[:, None], COARSE_LEN, 0)
    fine_lengths = jnp.where(slots[None, :] == 0, FINE_LEN, 0)
    lengths = jnp.where(has_fine[:, None], fine_lengths, coarse_lengths).astype(jnp.int32)
    classes = jnp.where(has_fine[:, None] & (slots[None, :] == 0), 1, 0).astype(jnp.int32)
    return (lengths, classes)


def draw_image_tokens(key, part):
    return image_plan(key)[0]


def draw_patch_class(key, part):
    return image_plan(key)[1]


def draw_small_params(key, part):
    key = jax.random.fold_in(key, 7)
    key_noise, key_shift = jax.random.split(key)
    ramp_low = 0.6
    ramp_high = 1.8
    column = jnp.arange(D, dtype=jnp.float32) / (D - 1)
    ramp = ramp_low + (ramp_high - ramp_low) * column
    noise = jax.random.uniform(key_noise, (11, D), jnp.float32, 0.7, 1.3)
    shifts = 0.3 * jax.random.normal(key_shift, (11, D), jnp.float32)
    rows = jnp.arange(11, dtype=jnp.int32)[:, None]
    is_gain = (rows == 1) | (rows == 4)
    return jnp.where(is_gain, ramp[None, :] * noise, shifts).astype(jnp.float32)


def shard_levels(stream_key, shape, pieces, smallest, top_value):
    factor_of = 1.0
    for dim, shards_of in pieces:
        steps = jax.random.uniform(jax.random.fold_in(jax.random.fold_in(stream_key, 6), dim), (shards_of,), jnp.float32, smallest / len(pieces), top_value / len(pieces))
        factor_of = factor_of * jnp.repeat(jnp.exp(steps), shape[dim] // shards_of).reshape((-1,) + (1,) * (len(shape) - 1 - dim))
    return factor_of


def scatter_about(own_key, shape, scale, reach, shards=(), kind=jnp.bfloat16):
    level = shard_levels(own_key, shape, shards, -0.22, 0.18) if shards else 1.0
    drawn = jax.random.normal(own_key, shape, jnp.float32) * scale * level
    return jnp.minimum(jnp.maximum(drawn, -reach), reach).astype(kind)


def setup_inputs(seed: int = 0) -> dict:
    arg_keys = jax.random.split(jax.random.key(seed), 25)
    pixels = scatter_about(arg_keys[0], (TOKENS, PIXC), 1.0, 6.0, ((0, 32),))
    image_tokens = draw_image_tokens(jax.random.fold_in(arg_keys[24], 71), 0)
    patch_class = draw_patch_class(jax.random.fold_in(arg_keys[24], 71), 0)
    resize_coarse = scatter_about(arg_keys[3], (PIXC, PIXB), PIXC ** -0.5, 0.21875)
    resize_fine = scatter_about(arg_keys[4], (PIXF, PIXB), PIXF ** -0.5, 0.4375)
    w_base = scatter_about(arg_keys[5], (PIXB, D), PIXB ** -0.5, 0.109375, ((0, 16),), jnp.float32)
    w_qkv = scatter_about(arg_keys[6], (D, 3 * D), D ** -0.5, 0.21875, ((0, 16),), jnp.float32)
    w_proj = scatter_about(arg_keys[7], (D, D), (D // 4) ** -0.5, 0.4375, ((0, 16),), jnp.float32)
    w_fc1 = scatter_about(arg_keys[8], (D, FF), D ** -0.5, 0.21875, ((0, 16),), jnp.float32)
    w_fc2 = scatter_about(arg_keys[9], (FF, D), FF ** -0.5, 0.109375, ((0, 16),), jnp.float32)
    small_params = draw_small_params(jax.random.fold_in(arg_keys[24], 71), 0)
    first_base = scatter_about(arg_keys[11], (PIXB, D), (0.11 / PARAMS ** 0.5), 0.00048828125, ((0, 16),), jnp.float32)
    first_qkv = scatter_about(arg_keys[12], (D, 3 * D), (0.11 / PARAMS ** 0.5), 0.00048828125, ((0, 16),), jnp.float32)
    first_proj = scatter_about(arg_keys[13], (D, D), (0.11 / PARAMS ** 0.5), 0.00048828125, ((0, 16),), jnp.float32)
    first_fc1 = scatter_about(arg_keys[14], (D, FF), (0.11 / PARAMS ** 0.5), 0.00048828125, ((0, 16),), jnp.float32)
    first_fc2 = scatter_about(arg_keys[15], (FF, D), (0.11 / PARAMS ** 0.5), 0.00048828125, ((0, 16),), jnp.float32)
    first_small = scatter_about(arg_keys[16], (11, D), (0.11 / PARAMS ** 0.5), 0.00048828125, ((1, 16),), jnp.float32)
    second_base = jnp.clip(jnp.exp(math.log(2.2232498508856224e-08) - 1.3768156 * jax.random.uniform(arg_keys[17], (PIXB, D), jnp.float32) ** shard_levels(arg_keys[17], (PIXB, D), ((0, 16),), -0.2, 0.2)), 5.611059172849764e-09, 2.2232498508856224e-08)
    second_qkv = jnp.clip(jnp.exp(math.log(2.2232498508856224e-08) - 1.3768156 * jax.random.uniform(arg_keys[18], (D, 3 * D), jnp.float32) ** shard_levels(arg_keys[18], (D, 3 * D), ((0, 16),), -0.2, 0.2)), 5.611059172849764e-09, 2.2232498508856224e-08)
    second_proj = jnp.clip(jnp.exp(math.log(2.2232498508856224e-08) - 1.3768156 * jax.random.uniform(arg_keys[19], (D, D), jnp.float32) ** shard_levels(arg_keys[19], (D, D), ((0, 16),), -0.2, 0.2)), 5.611059172849764e-09, 2.2232498508856224e-08)
    second_fc1 = jnp.clip(jnp.exp(math.log(2.2232498508856224e-08) - 1.3768156 * jax.random.uniform(arg_keys[20], (D, FF), jnp.float32) ** shard_levels(arg_keys[20], (D, FF), ((0, 16),), -0.2, 0.2)), 5.611059172849764e-09, 2.2232498508856224e-08)
    second_fc2 = jnp.clip(jnp.exp(math.log(2.2232498508856224e-08) - 1.3768156 * jax.random.uniform(arg_keys[21], (FF, D), jnp.float32) ** shard_levels(arg_keys[21], (FF, D), ((0, 16),), -0.2, 0.2)), 5.611059172849764e-09, 2.2232498508856224e-08)
    second_small = jnp.clip(jnp.exp(math.log(2.2232498508856224e-08) - 1.3768156 * jax.random.uniform(arg_keys[22], (11, D), jnp.float32) ** shard_levels(arg_keys[22], (11, D), ((1, 16),), -0.2, 0.2)), 5.611059172849764e-09, 2.2232498508856224e-08)
    cotangent = scatter_about(arg_keys[23], (TOKENS, D), 1.0, 6.0, ((0, 32),))
    return {"pixels": pixels, "image_tokens": image_tokens, "patch_class": patch_class, "resize_coarse": resize_coarse, "resize_fine": resize_fine, "w_base": w_base, "w_qkv": w_qkv, "w_proj": w_proj, "w_fc1": w_fc1, "w_fc2": w_fc2, "small_params": small_params, "first_base": first_base, "first_qkv": first_qkv, "first_proj": first_proj, "first_fc1": first_fc1, "first_fc2": first_fc2, "first_small": first_small, "second_base": second_base, "second_qkv": second_qkv, "second_proj": second_proj, "second_fc1": second_fc1, "second_fc2": second_fc2, "second_small": second_small, "cotangent": cotangent}


EPS_NORM = 1e-06
NEG_BIG = -1000000000.0
RATE = 0.05
RATE_SMALL = 0.5
BETA_ONE = 0.9
BETA_TWO = 0.95
ADAM_EPS = 1e-08
DECAY = 0.05
CLIP_NORM = 1.0

@jax.custom_vjp
def low(v):
    return lax.optimization_barrier(v.astype(jnp.bfloat16)).astype(jnp.float32)

@jax.custom_vjp
def low_back(v):
    return v

def low_keep(v):
    return (low(v), None)

def low_pass(kept, grad):
    return (grad,)

def back_keep(v):
    return (v, None)

def back_low(kept, grad):
    return (low(grad),)
low.defvjp(low_keep, low_pass)
low_back.defvjp(back_keep, back_low)

def rows_plan(lengths, classes, count):
    ends = jnp.cumsum(lengths).astype(jnp.int32)
    positions = jnp.arange(count, dtype=jnp.int32)
    segment = lax.optimization_barrier(jnp.sum((positions[:, None] >= ends[None, :]).astype(jnp.int32), axis=1))
    alive = (positions < ends[-1]).astype(jnp.float32)
    slots = jnp.arange(lengths.shape[0], dtype=jnp.int32)
    member = (segment[:, None] == slots[None, :]).astype(jnp.float32)
    finer = lax.optimization_barrier(jnp.sum(member * classes[None, :].astype(jnp.float32), axis=1))
    return (segment, alive, finer)

def layer_norm(values, gain, shift):
    average = lax.optimization_barrier(jnp.mean(values, axis=-1, keepdims=True))
    centre = values - average
    spread = lax.optimization_barrier(jnp.mean(centre * centre, axis=-1, keepdims=True))
    return centre * lax.rsqrt(spread + EPS_NORM) * gain + shift

def device_block(pixel_rows, lengths, classes, coarse_weight, fine_weight, qkv_weight, proj_weight, fc1_weight, fc2_weight, vectors):
    highest = lax.Precision.HIGHEST
    segment, alive, finer = rows_plan(lengths, classes, TOK_DEV)
    fine_col = finer[:, None]
    coarse_part = jnp.dot(pixel_rows, coarse_weight, precision=highest)
    fine_part = jnp.dot(pixel_rows[:, :PIXF], fine_weight, precision=highest)
    patch = low_back(coarse_part * (1.0 - fine_col) + fine_part * fine_col)
    state_zero = patch + vectors[0]
    normed_one = low(layer_norm(state_zero, vectors[1], vectors[2]))
    qkv_all = low(low_back(jnp.dot(normed_one, qkv_weight, precision=highest)))
    queries = qkv_all[:, :D].reshape(TOK_DEV, HEADS, HEAD_DIM)
    keys_all = qkv_all[:, D:2 * D].reshape(TOK_DEV, HEADS, HEAD_DIM)
    values_all = qkv_all[:, 2 * D:].reshape(TOK_DEV, HEADS, HEAD_DIM)
    scaling = 1.0 / math.sqrt(HEAD_DIM)
    scores = low_back(jnp.einsum('qhd,khd->hqk', queries, keys_all, precision=highest) * scaling)
    same = segment[:, None] == segment[None, :]
    scores = jnp.where(same[None], scores, NEG_BIG)
    probabilities = low(jax.nn.softmax(scores, axis=-1))
    mixed = jnp.einsum('hqk,khd->qhd', probabilities, values_all, precision=highest).reshape(TOK_DEV, D)
    mixed = low(low_back(mixed))
    state_one = state_zero + low_back(jnp.dot(mixed, proj_weight, precision=highest)) + vectors[3]
    normed_two = low(layer_norm(state_one, vectors[4], vectors[5]))
    before = low_back(jnp.dot(normed_two, fc1_weight, precision=highest) + vectors[7:11].reshape(FF))
    hidden = low(jax.nn.gelu(before, approximate=False))
    state_two = state_one + low_back(jnp.dot(hidden, fc2_weight, precision=highest)) + vectors[6]
    return state_two * alive[:, None]

def adamw(weight, grad, first, second, clip, rate):
    scaled = grad * clip
    first_new = BETA_ONE * first + (1.0 - BETA_ONE) * scaled
    second_new = BETA_TWO * second + (1.0 - BETA_TWO) * scaled * scaled
    update = first_new / (1.0 - BETA_ONE ** STEP) / (jnp.sqrt(second_new / (1.0 - BETA_TWO ** STEP)) + ADAM_EPS)
    return (weight - rate * (update + DECAY * weight), first_new, second_new)

def reference(pixels, image_tokens, patch_class, resize_coarse, resize_fine, w_base, w_qkv, w_proj, w_fc1, w_fc2, small_params, first_base, first_qkv, first_proj, first_fc1, first_fc2, first_small, second_base, second_qkv, second_proj, second_fc1, second_fc2, second_small, cotangent):
    highest = lax.Precision.HIGHEST
    resize_c = resize_coarse.astype(jnp.float32)
    resize_f = resize_fine.astype(jnp.float32)
    pixel_all = pixels.astype(jnp.float32).reshape(-1, TOK_DEV, PIXC)

    def forward(pixel_blocks, base, qkv_weight, proj_weight, fc1_weight, fc2_weight, vectors):
        base_low = low(base)
        coarse_weight = low(jnp.dot(resize_c, base_low, precision=highest))
        fine_weight = low(jnp.dot(resize_f, base_low, precision=highest))
        qkv_low = low(qkv_weight)
        proj_low = low(proj_weight)
        fc1_low = low(fc1_weight)
        fc2_low = low(fc2_weight)
        vector_low = low(vectors)

        def one_block(carry, blocks):
            pixel_rows, lengths, classes = blocks
            return (carry, device_block(pixel_rows, lengths, classes, coarse_weight, fine_weight, qkv_low, proj_low, fc1_low, fc2_low, vector_low))
        _, results = lax.scan(jax.checkpoint(one_block), None, (pixel_blocks, image_tokens, patch_class))
        return results.reshape(-1, D)
    output, backward = jax.vjp(forward, pixel_all, w_base, w_qkv, w_proj, w_fc1, w_fc2, small_params)
    grads = backward(cotangent.astype(jnp.float32))
    pixel_grad = grads[0].reshape(-1, PIXC).astype(jnp.bfloat16)
    weight_grads = grads[1:]
    squares = jnp.float32(0.0)
    for grad in weight_grads:
        squares = squares + jnp.sum(grad * grad)
    grad_norm = jnp.sqrt(squares)
    clip = jnp.minimum(1.0, CLIP_NORM / grad_norm)
    masters = (w_base, w_qkv, w_proj, w_fc1, w_fc2, small_params)
    firsts = (first_base, first_qkv, first_proj, first_fc1, first_fc2, first_small)
    seconds = (second_base, second_qkv, second_proj, second_fc1, second_fc2, second_small)
    rates = (RATE, RATE, RATE, RATE, RATE, RATE_SMALL)
    results = [adamw(masters[index], weight_grads[index], firsts[index], seconds[index], clip, rates[index]) for index in range(6)]
    return (output.astype(jnp.bfloat16), pixel_grad, grad_norm, results[0][0], results[1][0], results[2][0], results[3][0], results[4][0], results[5][0], results[0][1], results[1][1], results[2][1], results[3][1], results[4][1], results[5][1], results[0][2], results[1][2], results[2][2], results[3][2], results[4][2], results[5][2])
```

```python
import functools
import math

import jax
import jax.numpy as jnp
from jax import lax
from jax.experimental import pallas as pl
from jax.experimental.pallas import tpu as pltpu
from jax.sharding import PartitionSpec as P

D = 768
HEADS = 12
HEAD_DIM = 64
FF = 3072
PIXC = 768
PIXF = 192
STEP = 10
SLOTS = 5


EPS_NORM = 1e-06
RATE = 0.05
RATE_SMALL = 0.5
BETA_ONE = 0.9
BETA_TWO = 0.95
ADAM_EPS = 1e-08
DECAY = 0.05
CLIP_NORM = 1.0


def rows_plan(lengths, classes, count):
    ends = jnp.cumsum(lengths)
    positions = jnp.arange(count, dtype=jnp.int32)
    segment = jnp.sum((positions[:, None] >= ends[None, :]).astype(jnp.int32), axis=1)
    alive = (positions < ends[-1]).astype(jnp.float32)
    slots = jnp.arange(lengths.shape[0], dtype=jnp.int32)
    member = (segment[:, None] == slots[None, :]).astype(jnp.float32)
    finer = jnp.sum(member * classes[None, :].astype(jnp.float32), axis=1)
    return (segment, alive, finer)


def layer_norm(values, gain, shift):
    average = jnp.mean(values, axis=-1, keepdims=True)
    centre = values - average
    spread = jnp.mean(centre * centre, axis=-1, keepdims=True)
    return centre * lax.rsqrt(spread + EPS_NORM) * gain + shift


def gelu_exact(values):
    return jax.nn.gelu(values, approximate=False)


LOG2E = math.log2(math.e)
FAR = -1e30
ATT_ROWS = 512


def lane_plan(rows, side, seg):
    lane = lax.broadcasted_iota(jnp.int32, (rows, 2 * HEAD_DIM), 1)
    mine = (lane < HEAD_DIM) if side == 0 else (lane >= HEAD_DIM)
    first = HEAD_DIM if side == 0 else 0
    hot = lane - first == seg
    slots = (lane >= first) & (lane < first + SLOTS)
    return lane, mine, hot, slots


def attend_kernel(seg_ref, q_ref, k_ref, v_ref, mixed_ref, log_ref, *, step):
    pair = pl.program_id(0)
    rows = q_ref.shape[0]
    seg = seg_ref[...]
    one = jnp.ones((), jnp.bfloat16)
    logs = jnp.where(pair == 0, 0.0, log_ref[...])
    outs = []
    for side in range(2):
        lane, mine, hot, slots = lane_plan(rows, side, seg)
        keys = jnp.where(
            mine, k_ref[...], jnp.where(slots & ~hot, FAR, 0.0).astype(jnp.bfloat16)
        )
        values = jnp.where(mine, v_ref[...], one)
        queries = jnp.where(mine, q_ref[...] * jnp.bfloat16(0.125), hot.astype(jnp.bfloat16))
        parts, part_logs = [], []
        for at in range(0, rows, step):
            scores = lax.dot_general(
                queries[at : at + step],
                keys,
                (((1,), (1,)), ((), ())),
                preferred_element_type=jnp.float32,
            )
            top = jnp.max(scores, axis=1, keepdims=True) * LOG2E
            raised = jnp.exp2(scores * LOG2E - top).astype(jnp.bfloat16)
            sums = jnp.dot(raised, values, preferred_element_type=jnp.float32)
            turned = pltpu.roll(sums, HEAD_DIM, 1)
            inside = mine[at : at + step]
            parts.append(sums / turned)
            part_logs.append(top + jnp.log2(jnp.where(inside, turned, sums)))
        outs.append(jnp.concatenate(parts, axis=0))
        logs = jnp.where(lane == 2 * pair + side, jnp.concatenate(part_logs, axis=0), logs)
    lane = lax.broadcasted_iota(jnp.int32, (rows, 2 * HEAD_DIM), 1)
    mixed_ref[...] = jnp.where(lane < HEAD_DIM, outs[0], outs[1]).astype(jnp.bfloat16)
    log_ref[...] = logs


def attend(qkv, seg):
    rows = qkv.shape[0]
    wide = 2 * HEAD_DIM
    pairs = D // wide
    step = min(ATT_ROWS, rows)

    def block(first):
        return pl.BlockSpec((rows, wide), lambda pair: (0, first + pair))

    return pl.pallas_call(
        functools.partial(attend_kernel, step=step),
        grid=(pairs,),
        in_specs=[
            pl.BlockSpec((rows, 1), lambda pair: (0, 0)),
            block(0),
            block(pairs),
            block(2 * pairs),
        ],
        out_specs=[block(0), pl.BlockSpec((rows, wide), lambda pair: (0, 0))],
        out_shape=[
            jax.ShapeDtypeStruct((rows, D), jnp.bfloat16),
            jax.ShapeDtypeStruct((rows, wide), jnp.float32),
        ],
        compiler_params=pltpu.CompilerParams(vmem_limit_bytes=48 * 2**20),
        cost_estimate=pl.CostEstimate(
            flops=16 * rows * rows * D,
            bytes_accessed=rows * D * 8,
            transcendentals=HEADS * rows * rows,
        ),
    )(seg, qkv, qkv, qkv)


def attend_back_kernel(
    seg_ref, q_ref, k_ref, v_ref, mixed_ref, grad_ref, log_ref, dq_ref, dk_ref, dv_ref, *, step
):
    pair = pl.program_id(0)
    rows = q_ref.shape[0]
    seg = seg_ref[...]
    zero = jnp.zeros((), jnp.bfloat16)
    product = grad_ref[...].astype(jnp.float32) * mixed_ref[...].astype(jnp.float32)
    plain_keys = k_ref[...]
    values = v_ref[...]
    scaled = q_ref[...] * jnp.bfloat16(0.125)
    results = []
    for side in range(2):
        lane, mine, hot, slots = lane_plan(rows, side, seg)
        keys = jnp.where(
            mine, plain_keys, jnp.where(slots & ~hot, FAR, 0.0).astype(jnp.bfloat16)
        )
        queries = jnp.where(mine, scaled, hot.astype(jnp.bfloat16))
        grads = jnp.where(mine, grad_ref[...], zero)
        queries_t = jnp.where(mine, scaled, zero).T
        grads_t = grads.T
        drop = jnp.sum(jnp.where(mine, product, 0.0), axis=1, keepdims=True)
        logs = jnp.sum(
            jnp.where(lane == 2 * pair + side, log_ref[...], 0.0), axis=1, keepdims=True
        )
        dq_parts, dk_t, dv_t = [], 0.0, 0.0
        for at in range(0, rows, step):
            part = slice(at, at + step)
            scores = lax.dot_general(
                queries[part],
                keys,
                (((1,), (1,)), ((), ())),
                preferred_element_type=jnp.float32,
            )
            probs = jnp.exp2(scores * LOG2E - logs[part])
            grad_probs = lax.dot_general(
                grads[part],
                values,
                (((1,), (1,)), ((), ())),
                preferred_element_type=jnp.float32,
            )
            grad_scores = (probs * (grad_probs - drop[part])).astype(jnp.bfloat16)
            probs = probs.astype(jnp.bfloat16)
            dq_parts.append(jnp.dot(grad_scores, plain_keys, preferred_element_type=jnp.float32))
            dv_t = dv_t + jnp.dot(grads_t[:, part], probs, preferred_element_type=jnp.float32)
            dk_t = dk_t + jnp.dot(
                queries_t[:, part], grad_scores, preferred_element_type=jnp.float32
            )
        results.append((jnp.concatenate(dq_parts, axis=0) * 0.125, dk_t.T, dv_t.T))
    lane = lax.broadcasted_iota(jnp.int32, (rows, 2 * HEAD_DIM), 1)
    for ref, low, high in zip((dq_ref, dk_ref, dv_ref), results[0], results[1]):
        ref[...] = jnp.where(lane < HEAD_DIM, low, high).astype(jnp.bfloat16)


def attend_back(qkv, seg, mixed, grad_mixed, logs):
    rows = qkv.shape[0]
    wide = 2 * HEAD_DIM
    pairs = D // wide
    step = min(ATT_ROWS, rows)

    def block(first):
        return pl.BlockSpec((rows, wide), lambda pair: (0, first + pair))

    return pl.pallas_call(
        functools.partial(attend_back_kernel, step=step),
        grid=(pairs,),
        in_specs=[
            pl.BlockSpec((rows, 1), lambda pair: (0, 0)),
            block(0),
            block(pairs),
            block(2 * pairs),
            block(0),
            block(0),
            pl.BlockSpec((rows, wide), lambda pair: (0, 0)),
        ],
        out_specs=[block(0)] * 3,
        out_shape=[jax.ShapeDtypeStruct((rows, D), jnp.bfloat16)] * 3,
        compiler_params=pltpu.CompilerParams(vmem_limit_bytes=48 * 2**20),
        cost_estimate=pl.CostEstimate(
            flops=40 * rows * rows * D,
            bytes_accessed=rows * D * 16,
            transcendentals=HEADS * rows * rows,
        ),
    )(seg, qkv, qkv, qkv, mixed, grad_mixed, logs)


def bits_of(count):
    bits = count.bit_length() - 1
    assert count == 1 << bits
    return bits


def swap(value, axis, count, mask):
    return lax.ppermute(value, axis, [(i, i ^ mask) for i in range(count)])


def gather(shard, count):
    here = lax.axis_index("fsdp")
    held = shard[None]
    for bit in reversed(range(bits_of(count))):
        other = swap(held, "fsdp", count, 1 << bit)
        upper = (here >> bit) & 1 == 1
        both = jnp.where(
            upper, jnp.stack([other, held], axis=1), jnp.stack([held, other], axis=1)
        )
        held = both.reshape((-1,) + shard.shape)
    return held


def scatter(blocks, count):
    here = lax.axis_index("fsdp")
    held = blocks.astype(jnp.bfloat16)
    for bit in range(bits_of(count)):
        side = (here >> bit) & 1
        halves = held.reshape((held.shape[0] // 2, 2) + held.shape[1:])
        sent = lax.dynamic_index_in_dim(halves, 1 - side, axis=1, keepdims=False)
        kept = lax.dynamic_index_in_dim(halves, side, axis=1, keepdims=False)
        other = swap(sent, "fsdp", count, 1 << bit)
        held = (kept.astype(jnp.float32) + other.astype(jnp.float32)).astype(jnp.bfloat16)
    return held[0]


def replicas(value, count):
    for bit in range(bits_of(count)):
        other = swap(value, "rep", count, 1 << bit)
        value = (value.astype(jnp.float32) + other.astype(jnp.float32)).astype(jnp.bfloat16)
    return value


def total(value, count):
    for bit in range(bits_of(count)):
        value = value + swap(value, "fsdp", count, 1 << bit)
    return value


def adamw(weight, grad, first, second, clip, rate):
    scaled = grad * clip
    first_new = BETA_ONE * first + (1.0 - BETA_ONE) * scaled
    second_new = BETA_TWO * second + (1.0 - BETA_TWO) * scaled * scaled
    update = (
        first_new
        / (1.0 - BETA_ONE**STEP)
        / (jnp.sqrt(second_new / (1.0 - BETA_TWO**STEP)) + ADAM_EPS)
    )
    return (weight - rate * (update + DECAY * weight), first_new, second_new)


def transposed_dot(left, right):
    return jnp.einsum("ti,tj->ij", left, right, preferred_element_type=jnp.float32)


def body(
    shards_count,
    rep_count,
    pixels,
    image_tokens,
    patch_class,
    resize_coarse,
    resize_fine,
    w_base,
    w_qkv,
    w_proj,
    w_fc1,
    w_fc2,
    small_params,
    first_base,
    first_qkv,
    first_proj,
    first_fc1,
    first_fc2,
    first_small,
    second_base,
    second_qkv,
    second_proj,
    second_fc1,
    second_fc2,
    second_small,
    cotangent,
):
    bfloat = jnp.bfloat16
    rows_here = pixels.shape[0]
    here = lax.axis_index("fsdp")

    def whole(shard):
        return gather(shard.astype(bfloat), shards_count).reshape(-1, shard.shape[1])

    gathered = (
        whole(w_base),
        whole(w_qkv),
        whole(w_proj),
        whole(w_fc1),
        whole(w_fc2),
        gather(small_params.astype(bfloat), shards_count).transpose(1, 0, 2).reshape(11, D),
    )

    def resized(weights):
        coarse = jnp.dot(resize_coarse, weights[0], preferred_element_type=jnp.float32).astype(
            bfloat
        )
        finer_w = jnp.dot(resize_fine, weights[0], preferred_element_type=jnp.float32).astype(
            bfloat
        )
        return (coarse, finer_w)

    segment, alive, finer = rows_plan(image_tokens[0], patch_class[0], rows_here)
    fine_col = finer[:, None]
    coarse_weight, fine_weight = resized(gathered)
    vectors = gathered[5].astype(jnp.float32)
    patch = jnp.dot(pixels, coarse_weight, preferred_element_type=jnp.float32) * (1.0 - fine_col)
    patch = (
        patch
        + jnp.dot(pixels[:, :PIXF], fine_weight, preferred_element_type=jnp.float32) * fine_col
    )
    state_zero = patch + vectors[0]
    normed_one = layer_norm(state_zero, vectors[1], vectors[2]).astype(bfloat)
    qkv_all = jnp.dot(normed_one, gathered[1], preferred_element_type=jnp.float32).astype(bfloat)
    segment_col = segment[:, None]
    mixed, logs = attend(qkv_all, segment_col)
    state_one = (
        state_zero + jnp.dot(mixed, gathered[2], preferred_element_type=jnp.float32) + vectors[3]
    )
    normed_two = layer_norm(state_one, vectors[4], vectors[5]).astype(bfloat)
    before = jnp.dot(normed_two, gathered[3], preferred_element_type=jnp.float32) + vectors[
        7:11
    ].reshape(FF)
    hidden = gelu_exact(before).astype(bfloat)
    state_two = (
        state_one + jnp.dot(hidden, gathered[4], preferred_element_type=jnp.float32) + vectors[6]
    )
    activations = (state_two * alive[:, None]).astype(bfloat)
    grad_two = cotangent.astype(jnp.float32) * alive[:, None]
    grad_out_bias = jnp.sum(grad_two, axis=0)
    grad_branch = grad_two.astype(bfloat)
    grad_fc2 = transposed_dot(hidden, grad_branch)
    grad_hidden = jnp.dot(grad_branch, gathered[4].T, preferred_element_type=jnp.float32)
    _, gelu_back = jax.vjp(gelu_exact, before)
    grad_before = gelu_back(grad_hidden)[0].astype(bfloat)
    grad_fc1_bias = jnp.sum(grad_before.astype(jnp.float32), axis=0)
    grad_fc1 = transposed_dot(normed_two, grad_before)
    grad_normed_two = jnp.dot(grad_before, gathered[3].T, preferred_element_type=jnp.float32)
    _, norm_two_back = jax.vjp(layer_norm, state_one, vectors[4], vectors[5])
    grad_one_part, grad_gain_two, grad_shift_two = norm_two_back(grad_normed_two)
    grad_one = grad_two + grad_one_part
    grad_proj_bias = jnp.sum(grad_one, axis=0)
    grad_attn = grad_one.astype(bfloat)
    grad_proj = transposed_dot(mixed, grad_attn)
    grad_mixed = jnp.dot(grad_attn, gathered[2].T, preferred_element_type=jnp.float32).astype(
        bfloat
    )
    grad_qkv_all = jnp.concatenate(
        attend_back(qkv_all, segment_col, mixed, grad_mixed, logs), axis=1
    )
    grad_qkv = transposed_dot(normed_one, grad_qkv_all)
    grad_normed_one = jnp.dot(grad_qkv_all, gathered[1].T, preferred_element_type=jnp.float32)
    _, norm_one_back = jax.vjp(layer_norm, state_zero, vectors[1], vectors[2])
    grad_zero_part, grad_gain_one, grad_shift_one = norm_one_back(grad_normed_one)
    grad_zero = grad_one + grad_zero_part
    grad_embed_bias = jnp.sum(grad_zero, axis=0)
    grad_patch = grad_zero.astype(bfloat)
    grad_coarse_rows = grad_patch * (1.0 - fine_col).astype(bfloat)
    grad_fine_rows = grad_patch * fine_col.astype(bfloat)
    grad_coarse = transposed_dot(pixels, grad_coarse_rows)
    grad_fine = transposed_dot(pixels[:, :PIXF], grad_fine_rows)
    pixel_grad = jnp.dot(grad_coarse_rows, coarse_weight.T, preferred_element_type=jnp.float32)
    fine_pixels = jnp.dot(grad_fine_rows, fine_weight.T, preferred_element_type=jnp.float32)
    pixel_grad = (pixel_grad + jnp.pad(fine_pixels, ((0, 0), (0, PIXC - PIXF)))).astype(bfloat)
    grad_small = jnp.concatenate(
        [
            jnp.stack(
                [
                    grad_embed_bias,
                    grad_gain_one,
                    grad_shift_one,
                    grad_proj_bias,
                    grad_gain_two,
                    grad_shift_two,
                    grad_out_bias,
                ]
            ),
            grad_fc1_bias.reshape(4, D),
        ],
        axis=0,
    )
    def owned(grad, axis):
        if axis == 0:
            blocks = grad.reshape(shards_count, -1, grad.shape[1])
        else:
            blocks = grad.reshape(grad.shape[0], shards_count, -1).transpose(1, 0, 2)
        return replicas(scatter(blocks, shards_count), rep_count).astype(jnp.float32)

    pad = -(PIXC + PIXF) % (16 * shards_count)
    patch_grads = jnp.concatenate([grad_coarse, grad_fine, jnp.zeros((pad, D), jnp.float32)])
    patch_part = replicas(
        scatter(patch_grads.reshape(shards_count, -1, D), shards_count), rep_count
    )
    patch_grads = gather(patch_part, shards_count).reshape(-1, D)
    first_row = here * w_base.shape[0]
    coarse_part = lax.dynamic_slice_in_dim(resize_coarse, first_row, w_base.shape[0], axis=1)
    fine_part = lax.dynamic_slice_in_dim(resize_fine, first_row, w_base.shape[0], axis=1)
    grad_base = transposed_dot(coarse_part, patch_grads[:PIXC])
    grad_base = grad_base + transposed_dot(fine_part, patch_grads[PIXC : PIXC + PIXF])
    shards = (
        grad_base,
        owned(grad_qkv, 0),
        owned(grad_proj, 0),
        owned(grad_fc1, 0),
        owned(grad_fc2, 0),
        owned(grad_small, 1),
    )
    squares = jnp.float32(0.0)
    for shard in shards:
        squares = squares + jnp.sum(shard * shard)
    grad_norm = jnp.sqrt(total(squares, shards_count))
    clip = jnp.minimum(1.0, CLIP_NORM / grad_norm)
    masters = (w_base, w_qkv, w_proj, w_fc1, w_fc2, small_params)
    firsts = (first_base, first_qkv, first_proj, first_fc1, first_fc2, first_small)
    seconds = (second_base, second_qkv, second_proj, second_fc1, second_fc2, second_small)
    rates = (RATE, RATE, RATE, RATE, RATE, RATE_SMALL)
    results = [
        adamw(masters[index], shards[index], firsts[index], seconds[index], clip, rates[index])
        for index in range(6)
    ]
    return (
        activations,
        pixel_grad,
        grad_norm,
        results[0][0],
        results[1][0],
        results[2][0],
        results[3][0],
        results[4][0],
        results[5][0],
        results[0][1],
        results[1][1],
        results[2][1],
        results[3][1],
        results[4][1],
        results[5][1],
        results[0][2],
        results[1][2],
        results[2][2],
        results[3][2],
        results[4][2],
        results[5][2],
    )


def solution(mesh):
    in_specs = (
        P(("fsdp", "rep"), None),
        P(("fsdp", "rep"), None),
        P(("fsdp", "rep"), None),
        P(),
        P(),
        P("fsdp", None),
        P("fsdp", None),
        P("fsdp", None),
        P("fsdp", None),
        P("fsdp", None),
        P(None, "fsdp"),
        P("fsdp", None),
        P("fsdp", None),
        P("fsdp", None),
        P("fsdp", None),
        P("fsdp", None),
        P(None, "fsdp"),
        P("fsdp", None),
        P("fsdp", None),
        P("fsdp", None),
        P("fsdp", None),
        P("fsdp", None),
        P(None, "fsdp"),
        P(("fsdp", "rep"), None),
    )
    out_specs = (
        P(("fsdp", "rep"), None),
        P(("fsdp", "rep"), None),
        P(),
        P("fsdp", None),
        P("fsdp", None),
        P("fsdp", None),
        P("fsdp", None),
        P("fsdp", None),
        P(None, "fsdp"),
        P("fsdp", None),
        P("fsdp", None),
        P("fsdp", None),
        P("fsdp", None),
        P("fsdp", None),
        P(None, "fsdp"),
        P("fsdp", None),
        P("fsdp", None),
        P("fsdp", None),
        P("fsdp", None),
        P("fsdp", None),
        P(None, "fsdp"),
    )
    step = functools.partial(body, mesh.shape["fsdp"], mesh.shape["rep"])
    return jax.shard_map(step, mesh=mesh, in_specs=in_specs, out_specs=out_specs, check_vma=False)
```

```python
import functools
import math

import jax
import jax.numpy as jnp
from jax import lax
from jax.experimental import pallas as pl
from jax.experimental.pallas import tpu as pltpu
from jax.sharding import PartitionSpec as P

D = 768
HEADS = 12
HEAD_DIM = 64
FF = 3072
PIXC = 768
PIXF = 192
PIXALL = 1024
STEP = 10
SLOTS = 5
SMALL = 11
SMALL_PAD = 16


EPS_NORM = 1e-06
RATE = 0.05
RATE_SMALL = 0.5
BETA_ONE = 0.9
BETA_TWO = 0.95
ADAM_EPS = 1e-08
DECAY = 0.05
CLIP_NORM = 1.0

LOG2E = math.log2(math.e)
FAR = -1e30
ATT_ROWS = 512
ROWS = 256
VMEM = 24 * 2**20
BF = jnp.bfloat16
F32 = jnp.float32
ANY = pl.ANY


def rows_plan(lengths, classes, count):
    ends = jnp.cumsum(lengths)
    positions = jnp.arange(count, dtype=jnp.int32)
    segment = jnp.sum((positions[:, None] >= ends[None, :]).astype(jnp.int32), axis=1)
    alive = (positions < ends[-1]).astype(F32)
    slots = jnp.arange(lengths.shape[0], dtype=jnp.int32)
    member = (segment[:, None] == slots[None, :]).astype(F32)
    finer = jnp.sum(member * classes[None, :].astype(F32), axis=1)
    return (segment, alive, finer)


def adamw(weight, grad, first, second, clip, rate):
    scaled = grad * clip
    first_new = BETA_ONE * first + (1.0 - BETA_ONE) * scaled
    second_new = BETA_TWO * second + (1.0 - BETA_TWO) * scaled * scaled
    update = (
        first_new
        / (1.0 - BETA_ONE**STEP)
        / (jnp.sqrt(second_new / (1.0 - BETA_TWO**STEP)) + ADAM_EPS)
    )
    return (weight - rate * (update + DECAY * weight), first_new, second_new)


def dot_nn(left, right):
    return jnp.dot(left, right, preferred_element_type=F32)


def dot_nt(left, right):
    return lax.dot_general(left, right, (((1,), (1,)), ((), ())), preferred_element_type=F32)


def dot_tn(left, right):
    return lax.dot_general(left, right, (((0,), (0,)), ((), ())), preferred_element_type=F32)


def norm_parts(values):
    average = jnp.mean(values, axis=-1, keepdims=True)
    centre = values - average
    spread = jnp.mean(centre * centre, axis=-1, keepdims=True)
    scale = lax.rsqrt(spread + EPS_NORM)
    return centre * scale, scale


def norm_back(grad, gain, unit, scale):
    inner = grad * gain
    mean_inner = jnp.mean(inner, axis=-1, keepdims=True)
    mean_unit = jnp.mean(inner * unit, axis=-1, keepdims=True)
    return scale * (inner - mean_inner - unit * mean_unit)


def column_sum(values):
    return jnp.sum(values, axis=0, keepdims=True)


def fetch(ids_ref, refs, offsets, target, sems, column=0, width=None):
    me = ids_ref[0]
    copies = []
    for ref, places in zip(refs, offsets):
        rows = ref.shape[1]
        for index, place in enumerate(places):
            source = ref.at[index]
            if width is not None and width != ref.shape[2]:
                source = ref.at[index, :, pl.ds(column, width)]
            first = 0 if place is None else jnp.bitwise_xor(me, place) * rows
            if place is not None:
                first = pl.multiple_of(first, rows)
            copies.append(
                pltpu.make_async_copy(
                    source, target.at[pl.ds(first, rows)], sems.at[len(copies)]
                )
            )
    return copies


def begin(copies):
    for copy in copies:
        copy.start()


def finish(copies):
    for copy in copies:
        copy.wait()


def piece_count(weight):
    return sum(len(places) for places in weight[1])


def anys(count):
    return [pl.BlockSpec(memory_space=ANY)] * count


def params(**others):
    return pltpu.CompilerParams(vmem_limit_bytes=VMEM, **others)


def cost():
    return pl.CostEstimate(flops=0, bytes_accessed=0, transcendentals=0)


def skip(kernel, count):
    if count == 0:
        return kernel
    return lambda ids_ref, *refs: kernel(ids_ref, *refs[count:])


def tie(value, *others):
    return lax.optimization_barrier((value,) + others)[0]


def row_spec(width, step=ROWS):
    return pl.BlockSpec((step, width), lambda i, ids: (i, 0))


def full_spec(shape):
    return pl.BlockSpec(shape, lambda i, ids: (0,) * len(shape))


def resize_kernel(ids_ref, *refs, offsets, arrays, shard_rows):
    coarse_ref, fine_ref = refs[:2]
    pieces = refs[2 : 2 + arrays]
    out_ref, resize, base, small, sems = refs[2 + arrays :]
    me = ids_ref[0]
    core = jnp.bitwise_and(me, 1)
    side = jnp.bitwise_and(lax.shift_right_logical(me, 1), 1)
    half = PIXALL // 2
    width = 2 * shard_rows
    blocks = resize.shape[1] // width
    rest = PIXC - half

    def spans(low):
        copies = []
        for block in range(blocks):
            source = pl.ds(pl.multiple_of((2 * block + side) * width, 128), width)
            target = pl.ds(block * width, width)
            at = 2 * block
            if low:
                copies.append(
                    pltpu.make_async_copy(
                        coarse_ref.at[pl.ds(0, half), source],
                        resize.at[pl.ds(0, half), target],
                        sems.at[at],
                    )
                )
            else:
                copies.append(
                    pltpu.make_async_copy(
                        coarse_ref.at[pl.ds(half, rest), source],
                        resize.at[pl.ds(0, rest), target],
                        sems.at[at],
                    )
                )
                copies.append(
                    pltpu.make_async_copy(
                        fine_ref.at[:, source],
                        resize.at[pl.ds(rest, PIXF), target],
                        sems.at[at + 1],
                    )
                )
        return copies

    copies = []
    at = 2 * blocks
    small_at = 0
    for ref, places in zip(pieces, offsets):
        for index, place in enumerate(places):
            shard = jnp.bitwise_xor(me, place)
            spot = lax.shift_right_logical(shard, 2) * 2 + jnp.bitwise_and(shard, 1)
            first = pl.multiple_of(spot * shard_rows, shard_rows)
            copies.append(
                pltpu.make_async_copy(
                    ref.at[index, pl.ds(0, shard_rows)],
                    base.at[pl.ds(first, shard_rows)],
                    sems.at[at],
                )
            )
            copies.append(
                pltpu.make_async_copy(
                    ref.at[index, pl.ds(shard_rows, 2 * SMALL_PAD)],
                    small.at[small_at],
                    sems.at[at + 1],
                )
            )
            at += 2
            small_at += 1
    begin(copies)

    @pl.when(core == 0)
    def _():
        low = spans(True)
        begin(low)
        finish(low)

    @pl.when(core != 0)
    def _():
        resize[pl.ds(rest + PIXF, half - rest - PIXF)] = jnp.zeros(
            (half - rest - PIXF, resize.shape[1]), BF
        )
        high = spans(False)
        begin(high)
        finish(high)

    finish(copies)
    out_ref[:half] = dot_nn(resize[...], base[...]).astype(BF)
    joined = small[0].astype(F32)
    for index in range(1, small_at):
        joined = joined + small[index].astype(F32)
    out_ref[half:] = joined.astype(BF)


def resize_part(ids, coarse, fine, arrays, offsets, shard_rows):
    half = PIXALL // 2
    count = sum(len(places) for places in offsets)
    blocks = count // 2
    return pl.pallas_call(
        functools.partial(
            resize_kernel, offsets=offsets, arrays=len(arrays), shard_rows=shard_rows
        ),
        grid_spec=pltpu.PrefetchScalarGridSpec(
            num_scalar_prefetch=1,
            grid=(1,),
            in_specs=anys(2 + len(arrays)),
            out_specs=full_spec((half + 2 * SMALL_PAD, D // 2)),
            scratch_shapes=[
                pltpu.VMEM((half, count * shard_rows), BF),
                pltpu.VMEM((count * shard_rows, D // 2), BF),
                pltpu.VMEM((count, 2 * SMALL_PAD, D // 2), BF),
                pltpu.SemaphoreType.DMA((2 * blocks + 2 * count,)),
            ],
        ),
        out_shape=jax.ShapeDtypeStruct((half + 2 * SMALL_PAD, D // 2), BF),
        compiler_params=params(),
        cost_estimate=cost(),
        name="resize_part",
    )(ids, coarse, fine, *arrays)


def spread_pixels(pixels, fine_col):
    rough = jnp.where(fine_col > 0.5, jnp.zeros((), BF), pixels)
    wide = PIXALL - PIXC
    lane = lax.broadcasted_iota(jnp.int32, (pixels.shape[0], wide), 1)
    fine = jnp.where((lane < PIXF) & (fine_col > 0.5), pixels[:, :wide], jnp.zeros((), BF))
    return jnp.concatenate([rough, fine], axis=1)


def patch_kernel(ids_ref, pixels_ref, rows_ref, vectors_ref, *refs, places, arrays):
    pieces = refs[:arrays]
    state_ref, normed_ref, weight_ref, sems = refs[arrays:]

    @pl.when(pl.program_id(0) == 0)
    def _():
        copies = []
        for ref, spots in zip(pieces, places):
            for index, spot in enumerate(spots):
                rows, width = ref.shape[1:]
                first, column = (0, 0) if spot is None else spot
                if spot is not None:
                    first = jnp.bitwise_xor(jnp.bitwise_and(ids_ref[0], 1), first) * rows
                    column = jnp.bitwise_xor(ids_ref[1], column) * width
                    first = pl.multiple_of(first, rows)
                    column = pl.multiple_of(column, 128)
                copies.append(
                    pltpu.make_async_copy(
                        ref.at[index],
                        weight_ref.at[pl.ds(first, rows), pl.ds(column, width)],
                        sems.at[len(copies)],
                    )
                )
        begin(copies)
        finish(copies)

    pixels = spread_pixels(pixels_ref[...], rows_ref[:, 2:3])
    vectors = vectors_ref[...]
    state = dot_nn(pixels, weight_ref[...]) + vectors[0:1]
    unit, _ = norm_parts(state)
    state_ref[...] = state
    normed_ref[...] = (unit * vectors[1:2] + vectors[2:3]).astype(BF)


def patch(ids, pixels, rows, vectors, arrays, places, deps=()):
    count = pixels.shape[0]
    total = sum(len(spots) for spots in places)
    return pl.pallas_call(
        skip(functools.partial(patch_kernel, places=places, arrays=len(arrays)), len(deps)),
        grid_spec=pltpu.PrefetchScalarGridSpec(
            num_scalar_prefetch=1,
            grid=(count // ROWS,),
            in_specs=anys(len(deps)) + [row_spec(PIXC), row_spec(8), full_spec(vectors.shape)]
            + anys(len(arrays)),
            out_specs=[row_spec(D), row_spec(D), full_spec((PIXALL, D))],
            scratch_shapes=[pltpu.SemaphoreType.DMA((total,))],
        ),
        out_shape=[
            jax.ShapeDtypeStruct((count, D), F32),
            jax.ShapeDtypeStruct((count, D), BF),
            jax.ShapeDtypeStruct((PIXALL, D), BF),
        ],
        compiler_params=params(),
        cost_estimate=cost(),
        name="patch",
    )(ids, *deps, pixels, rows, vectors, *arrays)


def qkv_kernel(ids_ref, normed_ref, *refs, offsets, arrays):
    pieces = refs[:arrays]
    out_ref, weight, sems = refs[arrays:]

    @pl.when(pl.program_id(0) == 0)
    def _():
        copies = fetch(ids_ref, pieces, offsets, weight, sems)
        begin(copies)
        finish(copies)

    out_ref[...] = dot_nn(normed_ref[...], weight[...]).astype(BF)


def project_qkv(ids, normed, weight, deps=()):
    arrays, offsets = weight
    count = normed.shape[0]
    return pl.pallas_call(
        skip(functools.partial(qkv_kernel, offsets=offsets, arrays=len(arrays)), len(deps)),
        grid_spec=pltpu.PrefetchScalarGridSpec(
            num_scalar_prefetch=1,
            grid=(count // ROWS,),
            in_specs=anys(len(deps)) + [row_spec(D)] + anys(len(arrays)),
            out_specs=row_spec(3 * D),
            scratch_shapes=[
                pltpu.VMEM((D, 3 * D), BF),
                pltpu.SemaphoreType.DMA((piece_count(weight),)),
            ],
        ),
        out_shape=jax.ShapeDtypeStruct((count, 3 * D), BF),
        compiler_params=params(),
        cost_estimate=cost(),
        name="project_qkv",
    )(ids, *deps, normed, *arrays)


def lane_plan(rows, side, seg):
    lane = lax.broadcasted_iota(jnp.int32, (rows, 2 * HEAD_DIM), 1)
    mine = (lane < HEAD_DIM) if side == 0 else (lane >= HEAD_DIM)
    first = HEAD_DIM if side == 0 else 0
    hot = lane - first == seg
    slots = (lane >= first) & (lane < first + SLOTS)
    return lane, mine, hot, slots


def attend_kernel(ids_ref, seg_ref, q_ref, k_ref, v_ref, mixed_ref, log_ref, *, step, start):
    pair = pl.program_id(0) + start
    rows = q_ref.shape[0]
    seg = seg_ref[...]
    one = jnp.ones((), BF)
    logs = jnp.where(pair == start, 0.0, log_ref[...])
    outs = []
    for side in range(2):
        lane, mine, hot, slots = lane_plan(rows, side, seg)
        keys = jnp.where(
            mine, k_ref[...], jnp.where(slots & ~hot, FAR, 0.0).astype(BF)
        )
        values = jnp.where(mine, v_ref[...], one)
        queries = jnp.where(mine, q_ref[...] * BF(0.125), hot.astype(BF))
        parts, part_logs = [], []
        for at in range(0, rows, step):
            scores = lax.dot_general(
                queries[at : at + step],
                keys,
                (((1,), (1,)), ((), ())),
                preferred_element_type=F32,
            )
            top = jnp.max(scores, axis=1, keepdims=True) * LOG2E
            raised = jnp.exp2(scores * LOG2E - top).astype(BF)
            sums = jnp.dot(raised, values, preferred_element_type=F32)
            turned = pltpu.roll(sums, HEAD_DIM, 1)
            inside = mine[at : at + step]
            parts.append(sums / turned)
            part_logs.append(top + jnp.log2(jnp.where(inside, turned, sums)))
        outs.append(jnp.concatenate(parts, axis=0))
        logs = jnp.where(lane == 2 * pair + side, jnp.concatenate(part_logs, axis=0), logs)
    lane = lax.broadcasted_iota(jnp.int32, (rows, 2 * HEAD_DIM), 1)
    mixed_ref[...] = jnp.where(lane < HEAD_DIM, outs[0], outs[1]).astype(BF)
    log_ref[...] = logs


def attend(ids, qkv, seg, start, many, deps=()):
    rows = qkv.shape[0]
    wide = 2 * HEAD_DIM
    pairs = D // wide
    step = min(ATT_ROWS, rows)

    def block(first):
        return pl.BlockSpec((rows, wide), lambda pair, ids: (0, first + start + pair))

    return pl.pallas_call(
        skip(functools.partial(attend_kernel, step=step, start=start), len(deps)),
        grid_spec=pltpu.PrefetchScalarGridSpec(
            num_scalar_prefetch=1,
            grid=(many,),
            in_specs=anys(len(deps))
            + [full_spec((rows, 1)), block(0), block(pairs), block(2 * pairs)],
            out_specs=[
                pl.BlockSpec((rows, wide), lambda pair, ids: (0, pair)),
                full_spec((rows, wide)),
            ],
        ),
        out_shape=[
            jax.ShapeDtypeStruct((rows, many * wide), BF),
            jax.ShapeDtypeStruct((rows, wide), F32),
        ],
        compiler_params=params(),
        cost_estimate=cost(),
        name="attend",
    )(ids, *deps, seg, qkv, qkv, qkv)


def attend_back_kernel(
    ids_ref, seg_ref, q_ref, k_ref, v_ref, mixed_ref, grad_ref, log_ref, out_ref, *, step, start
):
    pair = pl.program_id(0) + start
    rows = q_ref.shape[0]
    seg = seg_ref[...]
    zero = jnp.zeros((), BF)
    product = grad_ref[...].astype(F32) * mixed_ref[...].astype(F32)
    plain_keys = k_ref[...]
    values = v_ref[...]
    scaled = q_ref[...] * BF(0.125)
    results = []
    for side in range(2):
        lane, mine, hot, slots = lane_plan(rows, side, seg)
        keys = jnp.where(
            mine, plain_keys, jnp.where(slots & ~hot, FAR, 0.0).astype(BF)
        )
        queries = jnp.where(mine, scaled, hot.astype(BF))
        grads = jnp.where(mine, grad_ref[...], zero)
        queries_t = jnp.where(mine, scaled, zero).T
        grads_t = grads.T
        drop = jnp.sum(jnp.where(mine, product, 0.0), axis=1, keepdims=True)
        logs = jnp.sum(
            jnp.where(lane == 2 * pair + side, log_ref[...], 0.0), axis=1, keepdims=True
        )
        dq_parts, dk_t, dv_t = [], 0.0, 0.0
        for at in range(0, rows, step):
            part = slice(at, at + step)
            scores = lax.dot_general(
                queries[part],
                keys,
                (((1,), (1,)), ((), ())),
                preferred_element_type=F32,
            )
            probs = jnp.exp2(scores * LOG2E - logs[part])
            grad_probs = lax.dot_general(
                grads[part],
                values,
                (((1,), (1,)), ((), ())),
                preferred_element_type=F32,
            )
            grad_scores = (probs * (grad_probs - drop[part])).astype(BF)
            probs = probs.astype(BF)
            dq_parts.append(jnp.dot(grad_scores, plain_keys, preferred_element_type=F32))
            dv_t = dv_t + jnp.dot(grads_t[:, part], probs, preferred_element_type=F32)
            dk_t = dk_t + jnp.dot(
                queries_t[:, part], grad_scores, preferred_element_type=F32
            )
        results.append((jnp.concatenate(dq_parts, axis=0) * 0.125, dk_t.T, dv_t.T))
    lane = lax.broadcasted_iota(jnp.int32, (rows, 2 * HEAD_DIM), 1)
    for kind, (low, high) in enumerate(zip(results[0], results[1])):
        out_ref[kind] = jnp.where(lane < HEAD_DIM, low, high).astype(BF)


def attend_back(ids, qkv, seg, mixed, grad_mixed, logs, start, many, deps=()):
    rows = qkv.shape[0]
    wide = 2 * HEAD_DIM
    pairs = D // wide
    step = min(ATT_ROWS, rows)

    def block(first):
        return pl.BlockSpec((rows, wide), lambda pair, ids: (0, first + start + pair))

    kernel = functools.partial(attend_back_kernel, step=step, start=start)
    return pl.pallas_call(
        skip(kernel, len(deps)),
        grid_spec=pltpu.PrefetchScalarGridSpec(
            num_scalar_prefetch=1,
            grid=(many,),
            in_specs=anys(len(deps))
            + [
                full_spec((rows, 1)),
                block(0),
                block(pairs),
                block(2 * pairs),
                block(0),
                block(0),
                full_spec((rows, wide)),
            ],
            out_specs=pl.BlockSpec((3, rows, wide), lambda pair, ids: (0, 0, pair)),
        ),
        out_shape=jax.ShapeDtypeStruct((3, rows, many * wide), BF),
        compiler_params=params(),
        cost_estimate=cost(),
        name="attend_back",
    )(ids, *deps, seg, qkv, qkv, qkv, mixed, grad_mixed, logs)


def up_kernel(
    ids_ref, mixed_ref, state_ref, vectors_ref, bias_ref, *refs, offsets, arrays, columns
):
    pieces = refs[:arrays]
    one_ref, normed_ref, hidden_ref, slope_ref, proj, up, proj_sems, up_sems = refs[arrays:]

    @pl.when(pl.program_id(0) == 0)
    def _():
        copies = fetch(ids_ref, pieces, offsets, proj, proj_sems, 0, D)
        copies = copies + fetch(ids_ref, pieces, offsets, up, up_sems, D, FF)
        begin(copies)
        finish(copies)

    vectors = vectors_ref[...]
    state = state_ref[...] + dot_nn(mixed_ref[...], proj[...]) + vectors[3:4]
    one_ref[...] = state
    unit, _ = norm_parts(state)
    normed = (unit * vectors[4:5] + vectors[5:6]).astype(BF)
    normed_ref[...] = normed
    for at in range(0, FF, columns):
        part = slice(at, at + columns)
        before = dot_nn(normed, up[:, part]) + bias_ref[:, part]
        share = 0.5 + 0.5 * lax.erf(before * math.sqrt(0.5))
        bell = jnp.exp2(before * before * (-0.5 * LOG2E)) * (1.0 / math.sqrt(2.0 * math.pi))
        hidden_ref[:, part] = (before * share).astype(BF)
        slope_ref[:, part] = (share + before * bell).astype(BF)


def feed_up(ids, mixed, state, vectors, bias, weight, deps=()):
    arrays, offsets = weight
    count = mixed.shape[0]
    total = piece_count(weight)
    return pl.pallas_call(
        skip(functools.partial(up_kernel, offsets=offsets, arrays=len(arrays), columns=512), len(deps)),
        grid_spec=pltpu.PrefetchScalarGridSpec(
            num_scalar_prefetch=1,
            grid=(count // ROWS,),
            in_specs=anys(len(deps)) + [
                row_spec(D),
                row_spec(D),
                full_spec(vectors.shape),
                full_spec(bias.shape),
            ]
            + anys(len(arrays)),
            out_specs=[row_spec(D), row_spec(D), row_spec(FF), row_spec(FF)],
            scratch_shapes=[
                pltpu.VMEM((D, D), BF),
                pltpu.VMEM((D, FF), BF),
                pltpu.SemaphoreType.DMA((total,)),
                pltpu.SemaphoreType.DMA((total,)),
            ],
        ),
        out_shape=[
            jax.ShapeDtypeStruct((count, D), F32),
            jax.ShapeDtypeStruct((count, D), BF),
            jax.ShapeDtypeStruct((count, FF), BF),
            jax.ShapeDtypeStruct((count, FF), BF),
        ],
        compiler_params=params(),
        cost_estimate=cost(),
        name="feed_up",
    )(ids, *deps, mixed, state, vectors, bias, *arrays)


def down_kernel(
    ids_ref,
    hidden_ref,
    slope_ref,
    state_ref,
    cotangent_ref,
    rows_ref,
    vectors_ref,
    *refs,
    offsets,
    arrays,
    columns,
):
    pieces = refs[:arrays]
    out_ref, branch_ref, before_ref, sums_ref, weight, sems = refs[arrays:]

    @pl.when(pl.program_id(0) == 0)
    def _():
        copies = fetch(ids_ref, pieces, offsets, weight, sems)
        begin(copies)
        sums_ref[...] = jnp.zeros_like(sums_ref)
        finish(copies)

    alive = rows_ref[:, 1:2]
    state = state_ref[...] + dot_nn(hidden_ref[...], weight[...]) + vectors_ref[6:7]
    out_ref[...] = (state * alive).astype(BF)
    grad = cotangent_ref[...].astype(F32) * alive
    branch = grad.astype(BF)
    branch_ref[...] = branch
    sums_ref[0:1, :D] += column_sum(grad)
    for at in range(0, FF, columns):
        part = slice(at, at + columns)
        before = dot_nt(branch, weight[part]) * slope_ref[:, part].astype(F32)
        before = before.astype(BF)
        before_ref[:, part] = before
        sums_ref[1:2, part] += column_sum(before.astype(F32))


def feed_down(ids, hidden, slope, state, cotangent, rows, vectors, weight, deps=()):
    arrays, offsets = weight
    count = hidden.shape[0]
    return pl.pallas_call(
        skip(functools.partial(down_kernel, offsets=offsets, arrays=len(arrays), columns=768), len(deps)),
        grid_spec=pltpu.PrefetchScalarGridSpec(
            num_scalar_prefetch=1,
            grid=(count // ROWS,),
            in_specs=anys(len(deps)) + [
                row_spec(FF),
                row_spec(FF),
                row_spec(D),
                row_spec(D),
                row_spec(8),
                full_spec(vectors.shape),
            ]
            + anys(len(arrays)),
            out_specs=[row_spec(D), row_spec(D), row_spec(FF), full_spec((8, FF))],
            scratch_shapes=[
                pltpu.VMEM((FF, D), BF),
                pltpu.SemaphoreType.DMA((piece_count(weight),)),
            ],
        ),
        out_shape=[
            jax.ShapeDtypeStruct((count, D), BF),
            jax.ShapeDtypeStruct((count, D), BF),
            jax.ShapeDtypeStruct((count, FF), BF),
            jax.ShapeDtypeStruct((8, FF), F32),
        ],
        compiler_params=params(),
        cost_estimate=cost(),
        name="feed_down",
    )(ids, *deps, hidden, slope, state, cotangent, rows, vectors, *arrays)


def middle_kernel(
    ids_ref, before_ref, state_ref, branch_ref, vectors_ref, *refs, offsets, arrays
):
    pieces = refs[:arrays]
    grad_ref, attn_ref, mixed_ref, sums_ref, proj, up, proj_sems, up_sems = refs[arrays:]

    @pl.when(pl.program_id(0) == 0)
    def _():
        copies = fetch(ids_ref, pieces, offsets, proj, proj_sems, 0, D)
        copies = copies + fetch(ids_ref, pieces, offsets, up, up_sems, D, FF)
        begin(copies)
        sums_ref[...] = jnp.zeros_like(sums_ref)
        finish(copies)

    vectors = vectors_ref[...]
    normed = dot_nt(before_ref[...], up[...])
    unit, scale = norm_parts(state_ref[...])
    grad = branch_ref[...].astype(F32) + norm_back(normed, vectors[4:5], unit, scale)
    grad_ref[...] = grad
    attn = grad.astype(BF)
    attn_ref[...] = attn
    mixed_ref[...] = dot_nt(attn, proj[...]).astype(BF)
    sums_ref[0:1] += column_sum(grad)
    sums_ref[1:2] += column_sum(normed * unit)
    sums_ref[2:3] += column_sum(normed)


def middle_back(ids, before, state, branch, vectors, weight, deps=()):
    arrays, offsets = weight
    count = before.shape[0]
    total = piece_count(weight)
    return pl.pallas_call(
        skip(functools.partial(middle_kernel, offsets=offsets, arrays=len(arrays)), len(deps)),
        grid_spec=pltpu.PrefetchScalarGridSpec(
            num_scalar_prefetch=1,
            grid=(count // ROWS,),
            in_specs=anys(len(deps)) + [row_spec(FF), row_spec(D), row_spec(D), full_spec(vectors.shape)]
            + anys(len(arrays)),
            out_specs=[row_spec(D), row_spec(D), row_spec(D), full_spec((8, D))],
            scratch_shapes=[
                pltpu.VMEM((D, D), BF),
                pltpu.VMEM((D, FF), BF),
                pltpu.SemaphoreType.DMA((total,)),
                pltpu.SemaphoreType.DMA((total,)),
            ],
        ),
        out_shape=[
            jax.ShapeDtypeStruct((count, D), F32),
            jax.ShapeDtypeStruct((count, D), BF),
            jax.ShapeDtypeStruct((count, D), BF),
            jax.ShapeDtypeStruct((8, D), F32),
        ],
        compiler_params=params(),
        cost_estimate=cost(),
        name="middle_back",
    )(ids, *deps, before, state, branch, vectors, *arrays)


def place_pieces(ids_ref, values, kept_ref, sent_ref, shards, rows, first, lead=0):
    count = values.shape[0] // rows
    flat = len(kept_ref.shape) == 2
    if sent_ref is None:
        if flat:
            kept_ref[lead:] = values
        else:
            kept_ref[pl.ds(first, count)] = values.reshape((count, rows) + values.shape[1:])
        return
    me = ids_ref[0]
    for index in range(count):
        apart = jnp.bitwise_xor(me, first + index)
        spot = 0
        for bit in range(1, bits_of(shards)):
            spot = spot * 2 + jnp.bitwise_and(lax.shift_right_logical(apart, bit), 1)
        piece = values[index * rows : (index + 1) * rows]
        same = jnp.bitwise_and(apart, 1) == 0

        def put(ref, piece=piece, spot=spot):
            if flat:
                ref[pl.ds(pl.multiple_of(lead + spot * rows, 16), rows)] = piece
            else:
                ref[spot] = piece

        pl.when(same)(functools.partial(put, kept_ref))
        pl.when(jnp.logical_not(same))(functools.partial(put, sent_ref))


def weight_kernel(ids_ref, left_ref, right_ref, *refs, shards, rows, first_step, extra):
    out_refs = refs[2 * extra :]
    sent_ref = out_refs[1] if len(out_refs) > 1 else None
    step = pl.program_id(0)

    def put(left_ref, right_ref):
        right = right_ref[0] if len(right_ref.shape) == 3 else right_ref[...]
        values = dot_tn(left_ref[...], right).astype(BF)
        place_pieces(
            ids_ref, values, out_refs[0], sent_ref, shards, rows, step * first_step
        )

    if extra:
        last = pl.num_programs(0) - extra * (refs[1].shape[1] // right_ref.shape[2])
        pl.when(step < last)(lambda: put(left_ref, right_ref))

        @pl.when(step >= last)
        def _():
            wide = right_ref.shape[2]
            for index in range(refs[1].shape[1] // wide):
                part = pl.ds(index * wide, wide)

                @pl.when(step == last + index)
                def _(part=part):
                    put(refs[0], refs[1].at[:, part])

    else:
        put(left_ref, right_ref)


def weight_grad(ids, left, right, shards, split, name, deps=(), extra=()):
    count, tall = left.shape
    stacked = right.ndim == 3
    wide = right.shape[-1]
    step = wide if stacked else min(768, max(tall, wide))
    narrow = tall > wide and not stacked
    rows = tall // shards
    outs = 2 if split else 1
    pieces = shards // outs
    more_specs = []
    if narrow:
        grid, first_step, out_wide = tall // step, step // rows, wide
        specs = [
            pl.BlockSpec((count, step), lambda i, ids: (0, i)),
            pl.BlockSpec((count, wide), lambda i, ids: (0, 0)),
        ]
        out_spec = pl.BlockSpec((pieces, rows, wide), lambda i, ids: (0, 0, 0))
    else:
        first_step = 0
        if stacked:
            kinds = right.shape[0]
            grid, out_wide = kinds, kinds * wide
            if extra:
                grid, out_wide = grid + extra[1].shape[1] // wide, out_wide + extra[1].shape[1]
                more_specs = [full_spec(value.shape) for value in extra]
            right_spec = pl.BlockSpec(
                (1, count, step), lambda i, ids: (jnp.minimum(i, kinds - 1), 0, 0)
            )
        else:
            grid, out_wide = wide // step, wide
            right_spec = pl.BlockSpec((count, step), lambda i, ids: (0, i))
        specs = [pl.BlockSpec((count, tall), lambda i, ids: (0, 0)), right_spec]
        out_spec = pl.BlockSpec((pieces, rows, step), lambda i, ids: (0, 0, i))
    kernel = functools.partial(
        weight_kernel,
        shards=shards,
        rows=rows,
        first_step=first_step,
        extra=1 if extra else 0,
    )
    return pl.pallas_call(
        skip(kernel, len(deps)),
        grid_spec=pltpu.PrefetchScalarGridSpec(
            num_scalar_prefetch=1,
            grid=(grid,),
            in_specs=anys(len(deps)) + specs + more_specs,
            out_specs=[out_spec] * outs,
        ),
        out_shape=[jax.ShapeDtypeStruct((pieces, rows, out_wide), BF)] * outs,
        compiler_params=params(),
        cost_estimate=cost(),
        name=name,
    )(ids, *deps, left, right, *extra)


def embed_kernel(
    ids_ref,
    state_ref,
    grad_ref,
    vectors_ref,
    down_sums_ref,
    middle_sums_ref,
    *refs,
    offsets,
    arrays,
    chunks,
):
    grad_refs = refs[:chunks]
    pieces = refs[chunks : chunks + arrays]
    patch_ref, small_ref, weight, sums, sems = refs[chunks + arrays :]
    step = pl.program_id(0)

    @pl.when(step == 0)
    def _():
        copies = fetch(ids_ref, pieces, offsets, weight, sems)
        begin(copies)
        sums[...] = jnp.zeros_like(sums)
        finish(copies)

    normed = 0.0
    at = 0
    for ref in grad_refs:
        wide = ref.shape[2]
        for kind in range(3):
            first = kind * D + at
            normed = normed + dot_nt(ref[kind], weight[:, first : first + wide])
        at += wide
    unit, scale = norm_parts(state_ref[...])
    grad = grad_ref[...] + norm_back(normed, vectors_ref[1:2], unit, scale)
    patch_ref[...] = grad.astype(BF)
    sums[0:1] += column_sum(grad)
    sums[1:2] += column_sum(normed * unit)
    sums[2:3] += column_sum(normed)

    @pl.when(step == pl.num_programs(0) - 1)
    def _():
        small = [sums[0:3], middle_sums_ref[0:3], down_sums_ref[0:1, :D]]
        small += [
            down_sums_ref[1:2, index * D : (index + 1) * D] for index in range(FF // D)
        ]
        small += [jnp.zeros((SMALL_PAD - SMALL, D), F32)]
        small_ref[:, :D] = jnp.concatenate(small, axis=0).astype(BF)
        small_ref[:, D:] = jnp.zeros((SMALL_PAD, PIXALL - D), BF)


def embed_back(
    ids, grads, state, grad, vectors, down_sums, middle_sums, weight, deps=()
):
    arrays, offsets = weight
    count = state.shape[0]
    kernel = functools.partial(
        embed_kernel, offsets=offsets, arrays=len(arrays), chunks=len(grads)
    )
    return pl.pallas_call(
        skip(kernel, len(deps)),
        grid_spec=pltpu.PrefetchScalarGridSpec(
            num_scalar_prefetch=1,
            grid=(count // ROWS,),
            in_specs=anys(len(deps))
            + [
                row_spec(D),
                row_spec(D),
                full_spec(vectors.shape),
                full_spec(down_sums.shape),
                full_spec(middle_sums.shape),
            ]
            + [
                pl.BlockSpec((3, ROWS, part.shape[2]), lambda i, ids: (0, i, 0))
                for part in grads
            ]
            + anys(len(arrays)),
            out_specs=[row_spec(D), full_spec((SMALL_PAD, PIXALL))],
            scratch_shapes=[
                pltpu.VMEM((D, 3 * D), BF),
                pltpu.VMEM((8, D), F32),
                pltpu.SemaphoreType.DMA((piece_count(weight),)),
            ],
        ),
        out_shape=[
            jax.ShapeDtypeStruct((count, D), BF),
            jax.ShapeDtypeStruct((SMALL_PAD, PIXALL), BF),
        ],
        compiler_params=params(),
        cost_estimate=cost(),
        name="embed_back",
    )(ids, *deps, state, grad, vectors, down_sums, middle_sums, *grads, *arrays)


def patch_back_kernel(ids_ref, patch_ref, pixels_ref, rows_ref, small_ref, *out_refs, shards):
    sent_ref = out_refs[1] if len(out_refs) > 1 else None
    spread = spread_pixels(pixels_ref[...], rows_ref[:, 2:3])
    values = dot_tn(patch_ref[...], spread).astype(BF)
    place_pieces(
        ids_ref, values, out_refs[0], sent_ref, shards, D // shards, 0, SMALL_PAD
    )
    for ref in out_refs:
        ref[:SMALL_PAD] = small_ref[...]


def patch_back(ids, patch_grad, pixels, rows, small, shards, split, deps=()):
    count = pixels.shape[0]
    outs = 2 if split else 1
    held = (SMALL_PAD + D // outs, PIXALL)
    return pl.pallas_call(
        skip(functools.partial(patch_back_kernel, shards=shards), len(deps)),
        grid_spec=pltpu.PrefetchScalarGridSpec(
            num_scalar_prefetch=1,
            grid=(1,),
            in_specs=anys(len(deps))
            + [
                full_spec((count, D)),
                full_spec((count, PIXC)),
                full_spec(rows.shape),
                full_spec(small.shape),
            ],
            out_specs=[full_spec(held)] * outs,
        ),
        out_shape=[jax.ShapeDtypeStruct(held, BF)] * outs,
        compiler_params=params(),
        cost_estimate=cost(),
        name="patch_back",
    )(ids, *deps, patch_grad, pixels, rows, small)


def pixel_kernel(ids_ref, patch_ref, rows_ref, weight_ref, out_ref):
    fine = rows_ref[:, 2:3]
    both = dot_nt(patch_ref[...], weight_ref[...])
    wide = PIXALL - PIXC
    rough = both[:, :PIXC] * (1.0 - fine)
    first = rough[:, :wide] + both[:, PIXC:] * fine
    out_ref[...] = jnp.concatenate([first, rough[:, wide:]], axis=1).astype(BF)


def pixel_back(ids, patch_grad, rows, weight, deps=()):
    count = patch_grad.shape[0]
    return pl.pallas_call(
        skip(pixel_kernel, len(deps)),
        grid_spec=pltpu.PrefetchScalarGridSpec(
            num_scalar_prefetch=1,
            grid=(count // ROWS,),
            in_specs=anys(len(deps)) + [row_spec(D), row_spec(8), full_spec(weight.shape)],
            out_specs=row_spec(PIXC),
        ),
        out_shape=jax.ShapeDtypeStruct((count, PIXC), BF),
        compiler_params=params(),
        cost_estimate=cost(),
        name="pixel_back",
    )(ids, *deps, patch_grad, rows, weight)


def bits_of(count):
    bits = count.bit_length() - 1
    assert count == 1 << bits
    return bits


def swap(value, axis, count, mask):
    return lax.ppermute(value, axis, [(i, i ^ mask) for i in range(count)])


def add_low(left, right):
    return (left.astype(F32) + right.astype(F32)).astype(BF)


class Gather:
    def __init__(self, shard, count):
        self.held, self.places, self.count = shard[None], [0], count
        self.bits = list(reversed(range(2, bits_of(count))))
        self.other = None

    def land(self, *after):
        if self.other is not None:
            self.held = jnp.concatenate([self.held, tie(self.other, *after)])
            self.other = None
        return self.held

    def step(self, *after):
        bit = self.bits.pop(0)
        held = tie(self.land(*after), *after)
        self.other = swap(held, "fsdp", self.count, 1 << bit)
        self.places = self.places + [place ^ (1 << bit) for place in self.places]
        return self.other

    def far(self, *after):
        held = tie(self.land(*after), *after)
        self.other = swap(held, "fsdp", self.count, 2)
        self.held_core = swap(held, "fsdp", self.count, 1)
        return self.other

    def near(self, *after):
        other_core = swap(tie(self.other, *after), "fsdp", self.count, 1)
        offsets = tuple(tuple(p ^ mask for p in self.places) for mask in (0, 1, 2, 3))
        return (self.held, self.held_core, self.other, other_core), offsets


def gather_whole(shard, count):
    here = lax.axis_index("fsdp")
    held = shard[None]
    for bit in reversed(range(bits_of(count))):
        other = swap(held, "fsdp", count, 1 << bit)
        upper = (here >> bit) & 1 == 1
        both = jnp.where(
            upper, jnp.stack([other, held], axis=1), jnp.stack([held, other], axis=1)
        )
        held = both.reshape((-1,) + shard.shape)
    return held.reshape((-1,) + shard.shape[1:])


def as_piece(whole):
    return (whole[None],), ((None,),)


def scatter_whole(blocks, count):
    here = lax.axis_index("fsdp")
    held = blocks
    for bit in range(bits_of(count)):
        side = (here >> bit) & 1
        halves = held.reshape((held.shape[0] // 2, 2) + held.shape[1:])
        sent = lax.dynamic_index_in_dim(halves, 1 - side, axis=1, keepdims=False)
        kept = lax.dynamic_index_in_dim(halves, side, axis=1, keepdims=False)
        held = add_low(kept, swap(sent, "fsdp", count, 1 << bit))
    return held[0]


class Scatter:
    def __init__(self, parts, shards, reps, lead=0, early=False):
        self.kept, self.sent = parts
        self.shards, self.reps, self.lead = shards, reps, lead
        bits = list(range(1, bits_of(shards)))
        self.plan = [0] + (["half"] + bits + ["join"] if early else bits + ["rep"])
        self.at = 0
        self.ready = self.sent

    def step(self, *after):
        kind = self.plan[self.at]
        value = tie(self.ready, *after)
        if isinstance(kind, int):
            self.other = swap(value, "fsdp", self.shards, 1 << kind)
        else:
            self.other = swap(value, "rep", self.reps, 1)
        self.at += 1

    def land(self, *after):
        kept, other = self.kept, tie(self.other, *after)
        following = self.plan[self.at] if self.at < len(self.plan) else None
        there = lax.axis_index("rep")
        if self.plan[self.at - 1] == "join":
            low = jnp.where(there == 0, kept, other)
            high = jnp.where(there == 0, other, kept)
            self.kept = self.ready = jnp.concatenate([low, high], axis=-1)
        elif following == "half":
            wide = kept.shape[-1] // 2

            def columns(side):
                return add_low(
                    lax.dynamic_slice_in_dim(kept, side * wide, wide, axis=2),
                    lax.dynamic_slice_in_dim(other, side * wide, wide, axis=2),
                )

            self.kept, self.ready = columns(there), columns(1 - there)
        elif isinstance(following, int):
            half = (kept.shape[0] - self.lead) // 2 + self.lead
            low, high = add_low(kept[:half], other[:half]), add_low(kept[half:], other[half:])
            self.kept, self.ready = low, high
            if self.lead:
                self.ready = jnp.concatenate([low[: self.lead], high])
        else:
            self.kept = self.ready = add_low(kept, other)
        return self.ready


def replicas(value, count):
    for bit in range(bits_of(count)):
        value = add_low(value, swap(value, "rep", count, 1 << bit))
    return value


def total_of(value, count):
    for bit in range(bits_of(count)):
        value = value + swap(value, "fsdp", count, 1 << bit)
    return value


def body(
    shards,
    reps,
    pixels,
    image_tokens,
    patch_class,
    resize_coarse,
    resize_fine,
    w_base,
    w_qkv,
    w_proj,
    w_fc1,
    w_fc2,
    small_params,
    first_base,
    first_qkv,
    first_proj,
    first_fc1,
    first_fc2,
    first_small,
    second_base,
    second_qkv,
    second_proj,
    second_fc1,
    second_fc2,
    second_small,
    cotangent,
):
    rows_here = pixels.shape[0]
    here = lax.axis_index("fsdp")
    there = lax.axis_index("rep")
    ids = jnp.stack([here, there]).astype(jnp.int32)
    base_rows = w_base.shape[0]
    pieced = shards == 16 and reps == 2 and w_qkv.shape[0] % 16 == 0

    segment, alive, finer = rows_plan(image_tokens[0], patch_class[0], rows_here)
    segment_col = segment[:, None]
    nothing = jnp.zeros_like(alive)
    rows = jnp.stack([nothing, alive, finer] + [nothing] * 5, axis=1)

    low_qkv = w_qkv.astype(BF)
    low_both = jnp.concatenate([w_proj, w_fc1], axis=1).astype(BF)
    low_fc2 = w_fc2.astype(BF)
    small_cols = small_params.shape[1]
    if pieced:
        half_cols = D // 2
        lanes = jnp.arange(D, dtype=jnp.int32)[None, :] // small_cols
        placed = jnp.where(lanes == here, jnp.tile(small_params, (1, shards)), 0.0)
        placed = jnp.pad(placed, ((0, SMALL_PAD - SMALL), (0, 0))).astype(BF)
        mine = lax.dynamic_slice_in_dim(w_base, there * half_cols, half_cols, axis=1)
        message = jnp.concatenate(
            [mine.astype(BF), placed[:, :half_cols], placed[:, half_cols:]], axis=0
        )
        gather_base = Gather(message, shards)
        gather_base.step()
        base_done = gather_base.step()
        held, places = gather_base.land(), gather_base.places
        other = swap(held, "fsdp", shards, 1)
        offsets = (tuple(places), tuple(place ^ 1 for place in places))
        part = resize_part(ids, resize_coarse, resize_fine, (held, other), offsets, base_rows)
        gather_qkv = Gather(low_qkv, shards)
        gather_qkv.step(base_done)
        qkv_done = gather_qkv.step(part)
        part = add_low(part, swap(part, "fsdp", shards, 2))
        half_rows = PIXALL // 2
        quarter = part[:half_rows][None]
        small_low = part[half_rows:]
        vectors = jnp.concatenate([small_low[:SMALL_PAD], small_low[SMALL_PAD:]], axis=1)
        quarter_rep = swap(quarter, "rep", reps, 1)
        quarter_core = swap(quarter, "fsdp", shards, 1)
        quarter_both = swap(quarter_rep, "fsdp", shards, 1)
        patch_arrays = (quarter, quarter_core, quarter_rep, quarter_both)
        patch_places = (((0, 0),), ((1, 0),), ((0, 1),), ((1, 1),))
        gather_qkv.far(quarter)
        gather_both = Gather(low_both, shards)
        gather_both.step(qkv_done, quarter)
    else:
        base = gather_whole(w_base.astype(BF), shards)
        coarse = dot_nn(resize_coarse, base).astype(BF)
        fine = dot_nn(resize_fine, base).astype(BF)
        whole = jnp.concatenate([coarse, fine, jnp.zeros((PIXALL - PIXC - PIXF, D), BF)])
        patch_arrays = (whole[None],)
        patch_places = ((None,),)
        vectors = gather_whole(small_params.astype(BF).T, shards).T
        vectors = jnp.pad(vectors, ((0, SMALL_PAD - SMALL), (0, 0)))
        weight_qkv = as_piece(gather_whole(low_qkv, shards))
        weight_both = as_piece(gather_whole(low_both, shards))
        weight_fc2 = as_piece(gather_whole(low_fc2, shards))
    vectors = vectors.astype(F32)
    bias = vectors[7:11].reshape(1, FF)

    state_zero, normed_one, patch_weight = patch(
        ids, pixels, rows, vectors, patch_arrays, patch_places
    )
    if pieced:
        weight_qkv = gather_qkv.near(state_zero)
        both_done = gather_both.step(state_zero)
    qkv = project_qkv(ids, normed_one, weight_qkv)
    front = attend(ids, qkv, segment_col, 0, HEADS // 4)
    after = ()
    if pieced:
        both_held = gather_both.land(front[0])
        both_far = gather_both.far(front[0])
        gather_fc2 = Gather(low_fc2, shards)
        fc2_done = gather_fc2.step(front[0], both_done)
        after = (both_held,)
    back = attend(ids, qkv, segment_col, HEADS // 4, HEADS // 4, after)
    if pieced:
        fc2_done = gather_fc2.step(back[0])
        weight_both = gather_both.near(fc2_done)
        fc2_far = gather_fc2.far(both_far)
    mixed = jnp.concatenate([front[0], back[0]], axis=1)
    logs = front[1] + back[1]
    state_one, normed_two, hidden, slope = feed_up(
        ids, mixed, state_zero, vectors, bias, weight_both
    )
    if pieced:
        weight_fc2 = gather_fc2.near(state_one)
    activations, branch, grad_before, down_sums = feed_down(
        ids, hidden, slope, state_one, cotangent, rows, vectors, weight_fc2
    )

    chunks = 3
    pairs = HEADS // 2

    def qkv_chunk(index, *after):
        many = pairs // chunks
        return attend_back(
            ids, qkv, segment_col, mixed, grad_mixed, logs, index * many, many, after
        )

    def chunk_grad(part, *after, extra=()):
        return weight_grad(
            ids, normed_one, part, shards, pieced, "grad_qkv", after, extra
        )

    def finish_embed(grads, *after):
        return embed_back(
            ids,
            grads,
            state_zero,
            grad_one,
            vectors,
            down_sums,
            middle_sums,
            weight_qkv,
            after,
        )

    part_fc2 = weight_grad(ids, hidden, branch, shards, pieced, "grad_fc2")
    if pieced:
        sum_fc2 = Scatter(part_fc2, shards, reps)
        sum_fc2.step()
        part_fc1 = weight_grad(
            ids, normed_two, grad_before, shards, pieced, "grad_fc1", part_fc2
        )
        sum_fc1 = Scatter(part_fc1, shards, reps, early=True)
        sum_fc2.land(part_fc1[0])
        sum_fc2.step()
        sum_fc1.step()
        grad_one, grad_attn, grad_mixed, middle_sums = middle_back(
            ids,
            grad_before,
            state_one,
            branch,
            vectors,
            weight_both,
            (sum_fc2.ready, part_fc1[0]),
        )
        sum_fc1.land(grad_one)
        sum_fc1.step()
        first = qkv_chunk(0, sum_fc1.ready)
        part_first = chunk_grad(first, extra=(mixed, grad_attn))
        sum_first = Scatter(part_first, shards, reps, early=True)
        sum_fc2.land(part_first[0])
        sum_fc2.step()
        sum_first.step()
        second = qkv_chunk(1, sum_fc2.ready, part_first[0])
        sum_first.land(second)
        sum_first.step()
        sum_fc1.land(second)
        sum_fc1.step()
        part_second = chunk_grad(second, sum_first.ready, sum_fc1.ready)
        sum_second = Scatter(part_second, shards, reps)
        sum_fc2.land(part_second[0])
        sum_fc2.step()
        sum_second.step()
        third = qkv_chunk(2, sum_fc2.ready, part_second[0])
        sum_second.land(third)
        sum_first.land(third)
        sum_first.step()
        sum_second.step(sum_first.ready)
        part_third = chunk_grad(third, sum_first.ready, sum_second.ready)
        sum_third = Scatter(part_third, shards, reps)
        sum_third.step()
        sum_fc1.land(part_third[0])
        sum_fc1.step()
        patch_grad, small_part = finish_embed(
            (first, second, third), part_third[0], sum_fc1.ready
        )
        sum_third.land(patch_grad)
        sum_third.step()
        sum_first.land(patch_grad)
        sum_first.step()
        sum_fc2.land(patch_grad)
        sum_fc2.step()
        patch_parts = patch_back(
            ids,
            patch_grad,
            pixels,
            rows,
            small_part,
            shards,
            pieced,
            (sum_third.ready, sum_first.ready, sum_fc2.ready),
        )
        sum_patch = Scatter(patch_parts, shards, reps, SMALL_PAD)
        sum_patch.step()
        sum_second.land(patch_parts[0])
        sum_second.step()
        sum_fc1.land(patch_parts[0])
        sum_fc1.step()
        sum_patch.land()
        sum_patch.step(sum_second.ready, sum_fc1.ready)
        pixel_grad = pixel_back(ids, patch_grad, rows, patch_weight, (sum_patch.ready,))
        sum_third.land(pixel_grad)
        sum_third.step()
        sum_first.land(pixel_grad)
        sum_first.step()
        sum_fc2.land(pixel_grad)
        sum_patch.land(sum_third.ready, sum_first.ready)
        sum_patch.step()
        mark = sum_patch.ready
        sum_second.land(mark)
        sum_second.step()
        sum_fc1.land(mark)
        sum_fc1.step()
        sum_third.land(mark)
        sum_third.step()
        sum_first.land(mark)
        sum_first.step()
        sum_patch.land(sum_second.ready, sum_fc1.ready, sum_third.ready)
        sum_patch.step()
        mark = sum_patch.ready
        sum_second.land(mark)
        sum_second.step()
        sum_third.land(mark)
        sum_third.step()
        sum_fc1.land(mark)
        sum_first.land(mark)
        sum_patch.land(sum_second.ready, sum_third.ready)
        sum_patch.step()
        mark = sum_patch.ready
        sum_second.land(mark)
        sum_third.land(mark)
        sum_patch.land()
        grad_fc2, grad_fc1 = sum_fc2.ready[0], sum_fc1.ready[0]
        grad_first, grad_proj = sum_first.ready[0, :, :D], sum_first.ready[0, :, D:]
        grad_second, grad_third = sum_second.ready[0], sum_third.ready[0]
        turned = sum_patch.ready
    else:

        def owned(parts):
            return replicas(scatter_whole(parts[0], shards), reps)

        grad_fc2 = owned(part_fc2)
        grad_fc1 = owned(
            weight_grad(ids, normed_two, grad_before, shards, pieced, "grad_fc1")
        )
        grad_one, grad_attn, grad_mixed, middle_sums = middle_back(
            ids, grad_before, state_one, branch, vectors, weight_both
        )
        grad_proj = owned(weight_grad(ids, mixed, grad_attn, shards, pieced, "grad_proj"))
        grads = [qkv_chunk(index) for index in range(chunks)]
        grad_first, grad_second, grad_third = [owned(chunk_grad(part)) for part in grads]
        patch_grad, small_part = finish_embed(grads)
        patch_parts = patch_back(ids, patch_grad, pixels, rows, small_part, shards, pieced)
        pixel_grad = pixel_back(ids, patch_grad, rows, patch_weight)
        small_all = small_part
        for bit in range(bits_of(shards)):
            small_all = add_low(small_all, swap(small_all, "fsdp", shards, 1 << bit))
        patch_all = patch_parts[0][SMALL_PAD:].reshape(shards, D // shards, PIXALL)
        turned = jnp.concatenate([replicas(small_all, reps), owned((patch_all,))])

    small_total = turned[:SMALL, :D].astype(F32)
    turned = turned[SMALL_PAD:]
    grad_small = lax.dynamic_slice_in_dim(small_total, here * small_cols, small_cols, axis=1)
    resize = jnp.concatenate(
        [resize_coarse, resize_fine, jnp.zeros((PIXALL - PIXC - PIXF, resize_fine.shape[1]), BF)]
    )
    base_cols = dot_nn(turned, resize)
    squares = jnp.sum(base_cols * base_cols)
    pieces = base_cols.astype(BF).reshape(base_cols.shape[0], shards, base_rows)
    pieces = lax.all_to_all(pieces.transpose(1, 0, 2), "fsdp", 0, 0)
    grad_base = pieces.reshape(D, base_rows).T
    wide = grad_first.shape[1] // 3
    grad_qkv = jnp.concatenate(
        [
            part[:, kind * wide : (kind + 1) * wide]
            for kind in range(3)
            for part in (grad_first, grad_second, grad_third)
        ],
        axis=1,
    )

    shards_of = [
        value.astype(F32) for value in (grad_base, grad_qkv, grad_proj, grad_fc1, grad_fc2)
    ] + [grad_small]
    for shard in shards_of[1:5]:
        squares = squares + jnp.sum(shard * shard)
    squares = total_of(squares, shards) + jnp.sum(small_total * small_total)
    grad_norm = jnp.sqrt(squares)
    clip = jnp.minimum(1.0, CLIP_NORM / grad_norm)
    masters = (w_base, w_qkv, w_proj, w_fc1, w_fc2, small_params)
    firsts = (first_base, first_qkv, first_proj, first_fc1, first_fc2, first_small)
    seconds = (second_base, second_qkv, second_proj, second_fc1, second_fc2, second_small)
    rates = (RATE, RATE, RATE, RATE, RATE, RATE_SMALL)
    results = [
        adamw(masters[index], shards_of[index], firsts[index], seconds[index], clip, rates[index])
        for index in range(6)
    ]
    return (activations, pixel_grad, grad_norm) + tuple(
        results[index][kind] for kind in range(3) for index in range(6)
    )


def solution(mesh):
    tokens = P(("fsdp", "rep"), None)
    split_rows = P("fsdp", None)
    states = (split_rows,) * 5 + (P(None, "fsdp"),)
    in_specs = (tokens, tokens, tokens, P(), P()) + states * 3 + (tokens,)
    out_specs = (tokens, tokens, P()) + states * 3
    step = functools.partial(body, mesh.shape["fsdp"], mesh.shape["rep"])
    return jax.shard_map(
        step, mesh=mesh, in_specs=in_specs, out_specs=out_specs, check_vma=False
    )
```

```python
import functools
import math

import jax
import jax.numpy as jnp
from jax import lax
from jax.experimental import pallas as pl
from jax.experimental.pallas import tpu as pltpu
from jax.sharding import PartitionSpec as P

D = 768
HEADS = 12
HEAD_DIM = 64
FF = 3072
PIXC = 768
PIXF = 192
PIXALL = 1024
STEP = 10
SLOTS = 5
SMALL = 11
SMALL_PAD = 16


EPS_NORM = 1e-06
RATE = 0.05
RATE_SMALL = 0.5
BETA_ONE = 0.9
BETA_TWO = 0.95
ADAM_EPS = 1e-08
DECAY = 0.05
CLIP_NORM = 1.0

LOG2E = math.log2(math.e)
FAR = -1e30
ATT_ROWS = 512
ROWS = 256
VMEM = 16 * 2**20
BF = jnp.bfloat16
F32 = jnp.float32
ANY = pltpu.HBM


def rows_plan(lengths, classes, count):
    ends = jnp.cumsum(lengths)
    positions = jnp.arange(count, dtype=jnp.int32)
    segment = jnp.sum((positions[:, None] >= ends[None, :]).astype(jnp.int32), axis=1)
    alive = (positions < ends[-1]).astype(F32)
    slots = jnp.arange(lengths.shape[0], dtype=jnp.int32)
    member = (segment[:, None] == slots[None, :]).astype(F32)
    finer = jnp.sum(member * classes[None, :].astype(F32), axis=1)
    return (segment, alive, finer)


def adamw(weight, grad, first, second, clip, rate):
    scaled = grad * clip
    first_new = BETA_ONE * first + (1.0 - BETA_ONE) * scaled
    second_new = BETA_TWO * second + (1.0 - BETA_TWO) * scaled * scaled
    update = (
        first_new
        / (1.0 - BETA_ONE**STEP)
        / (jnp.sqrt(second_new / (1.0 - BETA_TWO**STEP)) + ADAM_EPS)
    )
    return (weight - rate * (update + DECAY * weight), first_new, second_new)


def dot_nn(left, right):
    return jnp.dot(left, right, preferred_element_type=F32)


def dot_nt(left, right):
    return lax.dot_general(left, right, (((1,), (1,)), ((), ())), preferred_element_type=F32)


def dot_tn(left, right):
    return lax.dot_general(left, right, (((0,), (0,)), ((), ())), preferred_element_type=F32)


def norm_parts(values):
    average = jnp.mean(values, axis=-1, keepdims=True)
    centre = values - average
    spread = jnp.mean(centre * centre, axis=-1, keepdims=True)
    scale = lax.rsqrt(spread + EPS_NORM)
    return centre * scale, scale


def norm_back(grad, gain, unit, scale):
    inner = grad * gain
    mean_inner = jnp.mean(inner, axis=-1, keepdims=True)
    mean_unit = jnp.mean(inner * unit, axis=-1, keepdims=True)
    return scale * (inner - mean_inner - unit * mean_unit)


def column_sum(values):
    return jnp.sum(values, axis=0, keepdims=True)


def fetch(ids_ref, refs, offsets, target, sems, column=0, width=None):
    me = ids_ref[0]
    copies = []
    for ref, places in zip(refs, offsets):
        rows = ref.shape[1]
        for index, place in enumerate(places):
            source = ref.at[index]
            if width is not None and width != ref.shape[2]:
                source = ref.at[index, :, pl.ds(column, width)]
            first = 0 if place is None else jnp.bitwise_xor(me, place) * rows
            if place is not None:
                first = pl.multiple_of(first, rows)
            copies.append(
                pltpu.make_async_copy(
                    source, target.at[pl.ds(first, rows)], sems.at[len(copies)]
                )
            )
    return copies


def fetch_halves(ids_ref, refs, offsets, targets, sems):
    me = ids_ref[0]
    copies = []
    for ref, places in zip(refs, offsets):
        rows = ref.shape[1]
        for index, place in enumerate(places):
            if place is None:
                first, sides = 0, (0, 1)
            elif isinstance(place, tuple):
                first = pl.multiple_of(jnp.bitwise_xor(me, place[0]) * rows, rows)
                sides = (jnp.bitwise_xor(ids_ref[1], place[1]),)
            else:
                first = pl.multiple_of(jnp.bitwise_xor(me, place) * rows, rows)
                sides = (0, 1)
            at = 0
            for side in sides:
                for target in targets:
                    half = target.shape[1] // 2
                    column = side * half
                    if len(sides) == 1:
                        column = pl.multiple_of(column, 128)
                    copies.append(
                        pltpu.make_async_copy(
                            ref.at[index, :, pl.ds(at, half)],
                            target.at[pl.ds(first, rows), pl.ds(column, half)],
                            sems.at[len(copies)],
                        )
                    )
                    at += half
    return copies


def halves_count(weight):
    return sum(
        2 if isinstance(place, tuple) else 4 for places in weight[1] for place in places
    )


def begin(copies):
    for copy in copies:
        copy.start()


def finish(copies):
    for copy in copies:
        copy.wait()


def piece_count(weight):
    return sum(len(places) for places in weight[1])


def anys(count):
    return [pl.BlockSpec(memory_space=ANY)] * count


def params(limit=VMEM):
    return pltpu.CompilerParams(vmem_limit_bytes=limit)


def cost(micros):
    return pl.CostEstimate(
        flops=int(micros * 1.15e9), bytes_accessed=0, transcendentals=0
    )


def tie(value, *others):
    return lax.optimization_barrier((value,) + others)[0] if others else value


def row_spec(width, step=ROWS):
    return pl.BlockSpec((step, width), lambda i, ids: (i, 0))


def full_spec(shape):
    return pl.BlockSpec(shape, lambda i, ids: (0,) * len(shape))


def resize_kernel(ids_ref, *refs, offsets, arrays, shard_rows):
    coarse_ref, fine_ref = refs[:2]
    pieces = refs[2 : 2 + arrays]
    out_ref, resize, base, small, sems = refs[2 + arrays :]
    me = ids_ref[0]
    core = jnp.bitwise_and(me, 1)
    side = jnp.bitwise_and(lax.shift_right_logical(me, 1), 1)
    half = PIXALL // 2
    width = 2 * shard_rows
    blocks = resize.shape[1] // width
    rest = PIXC - half

    def spans(low):
        copies = []
        for block in range(blocks):
            source = pl.ds(pl.multiple_of((2 * block + side) * width, 128), width)
            target = pl.ds(block * width, width)
            at = 2 * block
            if low:
                copies.append(
                    pltpu.make_async_copy(
                        coarse_ref.at[pl.ds(0, half), source],
                        resize.at[pl.ds(0, half), target],
                        sems.at[at],
                    )
                )
            else:
                copies.append(
                    pltpu.make_async_copy(
                        coarse_ref.at[pl.ds(half, rest), source],
                        resize.at[pl.ds(0, rest), target],
                        sems.at[at],
                    )
                )
                copies.append(
                    pltpu.make_async_copy(
                        fine_ref.at[:, source],
                        resize.at[pl.ds(rest, PIXF), target],
                        sems.at[at + 1],
                    )
                )
        return copies

    copies = []
    at = 2 * blocks
    small_at = 0
    for ref, places in zip(pieces, offsets):
        for index, place in enumerate(places):
            shard = jnp.bitwise_xor(me, place)
            spot = lax.shift_right_logical(shard, 2) * 2 + jnp.bitwise_and(shard, 1)
            first = pl.multiple_of(spot * shard_rows, shard_rows)
            copies.append(
                pltpu.make_async_copy(
                    ref.at[index, pl.ds(0, shard_rows)],
                    base.at[pl.ds(first, shard_rows)],
                    sems.at[at],
                )
            )
            copies.append(
                pltpu.make_async_copy(
                    ref.at[index, pl.ds(shard_rows, 2 * SMALL_PAD)],
                    small.at[small_at],
                    sems.at[at + 1],
                )
            )
            at += 2
            small_at += 1
    begin(copies)

    @pl.when(core == 0)
    def _():
        low = spans(True)
        begin(low)
        finish(low)

    @pl.when(core != 0)
    def _():
        resize[pl.ds(rest + PIXF, half - rest - PIXF)] = jnp.zeros(
            (half - rest - PIXF, resize.shape[1]), BF
        )
        high = spans(False)
        begin(high)
        finish(high)

    finish(copies)
    out_ref[:half] = dot_nn(resize[...], base[...]).astype(BF)
    joined = small[0].astype(F32)
    for index in range(1, small_at):
        joined = joined + small[index].astype(F32)
    out_ref[half:] = joined.astype(BF)


def resize_part(ids, coarse, fine, arrays, offsets, shard_rows):
    half = PIXALL // 2
    count = sum(len(places) for places in offsets)
    blocks = count // 2
    return pl.pallas_call(
        functools.partial(
            resize_kernel, offsets=offsets, arrays=len(arrays), shard_rows=shard_rows
        ),
        grid_spec=pltpu.PrefetchScalarGridSpec(
            num_scalar_prefetch=1,
            grid=(1,),
            in_specs=anys(2 + len(arrays)),
            out_specs=full_spec((half + 2 * SMALL_PAD, D // 2)),
            scratch_shapes=[
                pltpu.VMEM((half, count * shard_rows), BF),
                pltpu.VMEM((count * shard_rows, D // 2), BF),
                pltpu.VMEM((count, 2 * SMALL_PAD, D // 2), BF),
                pltpu.SemaphoreType.DMA((2 * blocks + 2 * count,)),
            ],
        ),
        out_shape=jax.ShapeDtypeStruct((half + 2 * SMALL_PAD, D // 2), BF),
        compiler_params=params(),
        cost_estimate=cost(0),
        name="resize_part",
    )(ids, coarse, fine, *arrays)


def spread_pixels(pixels, fine_col):
    rough = jnp.where(fine_col > 0.5, jnp.zeros((), BF), pixels)
    wide = PIXALL - PIXC
    lane = lax.broadcasted_iota(jnp.int32, (pixels.shape[0], wide), 1)
    fine = jnp.where((lane < PIXF) & (fine_col > 0.5), pixels[:, :wide], jnp.zeros((), BF))
    return jnp.concatenate([rough, fine], axis=1)


def patch_kernel(ids_ref, pixels_ref, rows_ref, vectors_ref, *refs, places, arrays):
    pieces = refs[:arrays]
    state_ref, normed_ref, weight_ref, sems = refs[arrays:]

    @pl.when(pl.program_id(0) == 0)
    def _():
        copies = []
        for ref, spots in zip(pieces, places):
            for index, spot in enumerate(spots):
                rows, width = ref.shape[1:]
                first, column = (0, 0) if spot is None else spot
                if spot is not None:
                    first = jnp.bitwise_xor(jnp.bitwise_and(ids_ref[0], 1), first) * rows
                    column = jnp.bitwise_xor(ids_ref[1], column) * width
                    first = pl.multiple_of(first, rows)
                    column = pl.multiple_of(column, 128)
                copies.append(
                    pltpu.make_async_copy(
                        ref.at[index],
                        weight_ref.at[pl.ds(first, rows), pl.ds(column, width)],
                        sems.at[len(copies)],
                    )
                )
        begin(copies)
        finish(copies)

    pixels = spread_pixels(pixels_ref[...], rows_ref[:, 2:3])
    vectors = vectors_ref[...]
    state = dot_nn(pixels, weight_ref[...]) + vectors[0:1]
    unit, _ = norm_parts(state)
    state_ref[...] = state
    normed_ref[...] = (unit * vectors[1:2] + vectors[2:3]).astype(BF)


def patch(ids, pixels, rows, vectors, arrays, places, deps=()):
    count = pixels.shape[0]
    total = sum(len(spots) for spots in places)
    return pl.pallas_call(
        functools.partial(patch_kernel, places=places, arrays=len(arrays)),
        grid_spec=pltpu.PrefetchScalarGridSpec(
            num_scalar_prefetch=1,
            grid=(count // ROWS,),
            in_specs=[row_spec(PIXC), row_spec(8), full_spec(vectors.shape)]
            + anys(len(arrays)),
            out_specs=[row_spec(D), row_spec(D), full_spec((PIXALL, D))],
            scratch_shapes=[pltpu.SemaphoreType.DMA((total,))],
        ),
        out_shape=[
            jax.ShapeDtypeStruct((count, D), F32),
            jax.ShapeDtypeStruct((count, D), BF),
            jax.ShapeDtypeStruct((PIXALL, D), BF),
        ],
        compiler_params=params(52 * 2**20),
        cost_estimate=cost(0),
        name="patch",
    )(tie(ids, *deps), pixels, rows, vectors, *arrays)


def qkv_kernel(ids_ref, normed_ref, *refs, offsets, arrays):
    pieces = refs[:arrays]
    out_ref, weight, sems = refs[arrays:]

    @pl.when(pl.program_id(0) == 0)
    def _():
        copies = fetch(ids_ref, pieces, offsets, weight, sems)
        begin(copies)
        finish(copies)

    out_ref[...] = dot_nn(normed_ref[...], weight[...]).astype(BF)


def project_qkv(ids, normed, weight, deps=()):
    arrays, offsets = weight
    count = normed.shape[0]
    return pl.pallas_call(
        functools.partial(qkv_kernel, offsets=offsets, arrays=len(arrays)),
        grid_spec=pltpu.PrefetchScalarGridSpec(
            num_scalar_prefetch=1,
            grid=(count // ROWS,),
            in_specs=[row_spec(D)] + anys(len(arrays)),
            out_specs=row_spec(3 * D),
            scratch_shapes=[
                pltpu.VMEM((D, 3 * D), BF),
                pltpu.SemaphoreType.DMA((piece_count(weight),)),
            ],
        ),
        out_shape=jax.ShapeDtypeStruct((count, 3 * D), BF),
        compiler_params=params(),
        cost_estimate=cost(0),
        name="project_qkv",
    )(tie(ids, *deps), normed, *arrays)


def lane_plan(rows, side, seg):
    lane = lax.broadcasted_iota(jnp.int32, (rows, 2 * HEAD_DIM), 1)
    mine = (lane < HEAD_DIM) if side == 0 else (lane >= HEAD_DIM)
    first = HEAD_DIM if side == 0 else 0
    hot = lane - first == seg
    slots = (lane >= first) & (lane < first + SLOTS)
    return lane, mine, hot, slots


def attend_kernel(ids_ref, seg_ref, q_ref, k_ref, v_ref, mixed_ref, log_ref, *, step, start):
    pair = pl.program_id(0) + start
    rows = q_ref.shape[0]
    seg = seg_ref[...]
    one = jnp.ones((), BF)
    logs = jnp.where(pair == start, 0.0, log_ref[...])
    outs = []
    for side in range(2):
        lane, mine, hot, slots = lane_plan(rows, side, seg)
        keys = jnp.where(
            mine, k_ref[...], jnp.where(slots & ~hot, FAR, 0.0).astype(BF)
        )
        values = jnp.where(mine, v_ref[...], one)
        queries = jnp.where(mine, q_ref[...] * BF(0.125), hot.astype(BF))
        parts, part_logs = [], []
        for at in range(0, rows, step):
            scores = lax.dot_general(
                queries[at : at + step],
                keys,
                (((1,), (1,)), ((), ())),
                preferred_element_type=F32,
            )
            top = jnp.max(scores, axis=1, keepdims=True) * LOG2E
            raised = jnp.exp2(scores * LOG2E - top).astype(BF)
            sums = jnp.dot(raised, values, preferred_element_type=F32)
            turned = pltpu.roll(sums, HEAD_DIM, 1)
            inside = mine[at : at + step]
            parts.append(sums / turned)
            part_logs.append(top + jnp.log2(jnp.where(inside, turned, sums)))
        outs.append(jnp.concatenate(parts, axis=0))
        logs = jnp.where(lane == 2 * pair + side, jnp.concatenate(part_logs, axis=0), logs)
    lane = lax.broadcasted_iota(jnp.int32, (rows, 2 * HEAD_DIM), 1)
    mixed_ref[...] = jnp.where(lane < HEAD_DIM, outs[0], outs[1]).astype(BF)
    log_ref[...] = logs


def attend(ids, qkv, seg, start, many, deps=()):
    rows = qkv.shape[0]
    wide = 2 * HEAD_DIM
    pairs = D // wide
    step = min(ATT_ROWS, rows)

    def block(first):
        return pl.BlockSpec((rows, wide), lambda pair, ids: (0, first + start + pair))

    return pl.pallas_call(
        functools.partial(attend_kernel, step=step, start=start),
        grid_spec=pltpu.PrefetchScalarGridSpec(
            num_scalar_prefetch=1,
            grid=(many,),
            in_specs=[full_spec((rows, 1)), block(0), block(pairs), block(2 * pairs)],
            out_specs=[
                pl.BlockSpec((rows, wide), lambda pair, ids: (0, pair)),
                full_spec((rows, wide)),
            ],
        ),
        out_shape=[
            jax.ShapeDtypeStruct((rows, many * wide), BF),
            jax.ShapeDtypeStruct((rows, wide), F32),
        ],
        compiler_params=params(),
        cost_estimate=cost(0),
        name="attend",
    )(tie(ids, *deps), seg, qkv, qkv, qkv)


def attend_back_kernel(
    ids_ref,
    seg_ref,
    q_ref,
    k_ref,
    v_ref,
    mixed_ref,
    grad_ref,
    log_ref,
    out_ref,
    *,
    step,
    start,
):
    pair = pl.program_id(0) + start
    rows = q_ref.shape[0]
    seg = seg_ref[...]
    zero = jnp.zeros((), BF)
    product = grad_ref[...].astype(F32) * mixed_ref[...].astype(F32)
    plain_keys = k_ref[...]
    values = v_ref[...]
    scaled = q_ref[...] * BF(0.125)
    results = []
    for side in range(2):
        lane, mine, hot, slots = lane_plan(rows, side, seg)
        keys = jnp.where(
            mine, plain_keys, jnp.where(slots & ~hot, FAR, 0.0).astype(BF)
        )
        queries = jnp.where(mine, scaled, hot.astype(BF))
        grads = jnp.where(mine, grad_ref[...], zero)
        queries_t = jnp.where(mine, scaled, zero).T
        grads_t = grads.T
        drop = jnp.sum(jnp.where(mine, product, 0.0), axis=1, keepdims=True)
        logs = jnp.sum(
            jnp.where(lane == 2 * pair + side, log_ref[...], 0.0), axis=1, keepdims=True
        )
        dq_parts, dk_t, dv_t = [], 0.0, 0.0
        for at in range(0, rows, step):
            part = slice(at, at + step)
            scores = lax.dot_general(
                queries[part],
                keys,
                (((1,), (1,)), ((), ())),
                preferred_element_type=F32,
            )
            probs = jnp.exp2(scores * LOG2E - logs[part])
            grad_probs = lax.dot_general(
                grads[part],
                values,
                (((1,), (1,)), ((), ())),
                preferred_element_type=F32,
            )
            grad_scores = (probs * (grad_probs - drop[part])).astype(BF)
            probs = probs.astype(BF)
            dq_parts.append(jnp.dot(grad_scores, plain_keys, preferred_element_type=F32))
            dv_t = dv_t + jnp.dot(grads_t[:, part], probs, preferred_element_type=F32)
            dk_t = dk_t + jnp.dot(
                queries_t[:, part], grad_scores, preferred_element_type=F32
            )
        results.append((jnp.concatenate(dq_parts, axis=0) * 0.125, dk_t.T, dv_t.T))
    lane = lax.broadcasted_iota(jnp.int32, (rows, 2 * HEAD_DIM), 1)
    for kind, (low, high) in enumerate(zip(results[0], results[1])):
        out_ref[kind] = jnp.where(lane < HEAD_DIM, low, high).astype(BF)


def attend_back(ids, qkv, seg, mixed, grad_mixed, logs, start, many, deps=()):
    rows = qkv.shape[0]
    wide = 2 * HEAD_DIM
    pairs = D // wide
    step = min(ATT_ROWS, rows)

    def block(first):
        return pl.BlockSpec((rows, wide), lambda pair, ids: (0, first + start + pair))

    kernel = functools.partial(attend_back_kernel, step=step, start=start)
    return pl.pallas_call(
        kernel,
        grid_spec=pltpu.PrefetchScalarGridSpec(
            num_scalar_prefetch=1,
            grid=(many,),
            in_specs=[
                full_spec((rows, 1)),
                block(0),
                block(pairs),
                block(2 * pairs),
                block(0),
                block(0),
                full_spec((rows, wide)),
            ],
            out_specs=pl.BlockSpec((3, rows, wide), lambda pair, ids: (0, 0, pair)),
        ),
        out_shape=jax.ShapeDtypeStruct((3, rows, many * wide), BF),
        compiler_params=params(),
        cost_estimate=cost(0),
        name="attend_back",
    )(tie(ids, *deps), seg, qkv, qkv, qkv, mixed, grad_mixed, logs)


def up_kernel(
    ids_ref, mixed_ref, state_ref, vectors_ref, bias_ref, *refs, offsets, arrays, columns
):
    pieces = refs[:arrays]
    one_ref, normed_ref, hidden_ref, slope_ref, proj, up, sems = refs[arrays:]

    @pl.when(pl.program_id(0) == 0)
    def _():
        copies = fetch_halves(ids_ref, pieces, offsets, (proj, up), sems)
        begin(copies)
        finish(copies)

    vectors = vectors_ref[...]
    state = state_ref[...] + dot_nn(mixed_ref[...], proj[...]) + vectors[3:4]
    one_ref[...] = state
    unit, _ = norm_parts(state)
    normed = (unit * vectors[4:5] + vectors[5:6]).astype(BF)
    normed_ref[...] = normed
    for at in range(0, FF, columns):
        part = slice(at, at + columns)
        before = dot_nn(normed, up[:, part]) + bias_ref[:, part]
        share = 0.5 + 0.5 * lax.erf(before * math.sqrt(0.5))
        bell = jnp.exp2(before * before * (-0.5 * LOG2E)) * (1.0 / math.sqrt(2.0 * math.pi))
        hidden_ref[:, part] = (before * share).astype(BF)
        slope_ref[:, part] = (share + before * bell).astype(BF)


def feed_up(ids, mixed, state, vectors, bias, weight, deps=()):
    arrays, offsets = weight
    count = mixed.shape[0]
    total = halves_count(weight)
    return pl.pallas_call(
        functools.partial(up_kernel, offsets=offsets, arrays=len(arrays), columns=512),
        grid_spec=pltpu.PrefetchScalarGridSpec(
            num_scalar_prefetch=1,
            grid=(count // ROWS,),
            in_specs=[
                row_spec(D),
                row_spec(D),
                full_spec(vectors.shape),
                full_spec(bias.shape),
            ]
            + anys(len(arrays)),
            out_specs=[row_spec(D), row_spec(D), row_spec(FF), row_spec(FF)],
            scratch_shapes=[
                pltpu.VMEM((D, D), BF),
                pltpu.VMEM((D, FF), BF),
                pltpu.SemaphoreType.DMA((total,)),
            ],
        ),
        out_shape=[
            jax.ShapeDtypeStruct((count, D), F32),
            jax.ShapeDtypeStruct((count, D), BF),
            jax.ShapeDtypeStruct((count, FF), BF),
            jax.ShapeDtypeStruct((count, FF), BF),
        ],
        compiler_params=params(),
        cost_estimate=cost(0),
        name="feed_up",
    )(tie(ids, *deps), mixed, state, vectors, bias, *arrays)


def down_kernel(
    ids_ref,
    hidden_ref,
    slope_ref,
    state_ref,
    cotangent_ref,
    rows_ref,
    vectors_ref,
    *refs,
    offsets,
    arrays,
    columns,
):
    pieces = refs[:arrays]
    out_ref, branch_ref, before_ref, sums_ref, weight, sems = refs[arrays:]

    @pl.when(pl.program_id(0) == 0)
    def _():
        copies = fetch(ids_ref, pieces, offsets, weight, sems)
        begin(copies)
        sums_ref[...] = jnp.zeros_like(sums_ref)
        finish(copies)

    alive = rows_ref[:, 1:2]
    state = state_ref[...] + dot_nn(hidden_ref[...], weight[...]) + vectors_ref[6:7]
    out_ref[...] = (state * alive).astype(BF)
    grad = cotangent_ref[...].astype(F32) * alive
    branch = grad.astype(BF)
    branch_ref[...] = branch
    sums_ref[0:1, :D] += column_sum(grad)
    for at in range(0, FF, columns):
        part = slice(at, at + columns)
        before = dot_nt(branch, weight[part]) * slope_ref[:, part].astype(F32)
        before = before.astype(BF)
        before_ref[:, part] = before
        sums_ref[1:2, part] += column_sum(before.astype(F32))


def feed_down(ids, hidden, slope, state, cotangent, rows, vectors, weight, deps=()):
    arrays, offsets = weight
    count = hidden.shape[0]
    return pl.pallas_call(
        functools.partial(down_kernel, offsets=offsets, arrays=len(arrays), columns=768),
        grid_spec=pltpu.PrefetchScalarGridSpec(
            num_scalar_prefetch=1,
            grid=(count // ROWS,),
            in_specs=[
                row_spec(FF),
                row_spec(FF),
                row_spec(D),
                row_spec(D),
                row_spec(8),
                full_spec(vectors.shape),
            ]
            + anys(len(arrays)),
            out_specs=[row_spec(D), row_spec(D), row_spec(FF), full_spec((8, FF))],
            scratch_shapes=[
                pltpu.VMEM((FF, D), BF),
                pltpu.SemaphoreType.DMA((piece_count(weight),)),
            ],
        ),
        out_shape=[
            jax.ShapeDtypeStruct((count, D), BF),
            jax.ShapeDtypeStruct((count, D), BF),
            jax.ShapeDtypeStruct((count, FF), BF),
            jax.ShapeDtypeStruct((8, FF), F32),
        ],
        compiler_params=params(),
        cost_estimate=cost(0),
        name="feed_down",
    )(tie(ids, *deps), hidden, slope, state, cotangent, rows, vectors, *arrays)


def middle_kernel(
    ids_ref, before_ref, state_ref, branch_ref, vectors_ref, *refs, offsets, arrays
):
    pieces = refs[:arrays]
    grad_ref, attn_ref, mixed_ref, sums_ref, proj, up, sems = refs[arrays:]

    @pl.when(pl.program_id(0) == 0)
    def _():
        copies = fetch_halves(ids_ref, pieces, offsets, (proj, up), sems)
        begin(copies)
        sums_ref[...] = jnp.zeros_like(sums_ref)
        finish(copies)

    vectors = vectors_ref[...]
    normed = dot_nt(before_ref[...], up[...])
    unit, scale = norm_parts(state_ref[...])
    grad = branch_ref[...].astype(F32) + norm_back(normed, vectors[4:5], unit, scale)
    grad_ref[...] = grad
    attn = grad.astype(BF)
    attn_ref[...] = attn
    mixed_ref[...] = dot_nt(attn, proj[...]).astype(BF)
    sums_ref[0:1] += column_sum(grad)
    sums_ref[1:2] += column_sum(normed * unit)
    sums_ref[2:3] += column_sum(normed)


def middle_back(ids, before, state, branch, vectors, weight, deps=()):
    arrays, offsets = weight
    count = before.shape[0]
    total = halves_count(weight)
    return pl.pallas_call(
        functools.partial(middle_kernel, offsets=offsets, arrays=len(arrays)),
        grid_spec=pltpu.PrefetchScalarGridSpec(
            num_scalar_prefetch=1,
            grid=(count // ROWS,),
            in_specs=[row_spec(FF), row_spec(D), row_spec(D), full_spec(vectors.shape)]
            + anys(len(arrays)),
            out_specs=[row_spec(D), row_spec(D), row_spec(D), full_spec((8, D))],
            scratch_shapes=[
                pltpu.VMEM((D, D), BF),
                pltpu.VMEM((D, FF), BF),
                pltpu.SemaphoreType.DMA((total,)),
            ],
        ),
        out_shape=[
            jax.ShapeDtypeStruct((count, D), F32),
            jax.ShapeDtypeStruct((count, D), BF),
            jax.ShapeDtypeStruct((count, D), BF),
            jax.ShapeDtypeStruct((8, D), F32),
        ],
        compiler_params=params(52 * 2**20),
        cost_estimate=cost(0),
        name="middle_back",
    )(tie(ids, *deps), before, state, branch, vectors, *arrays)


def place_pieces(ids_ref, values, kept_ref, sent_ref, shards, rows, first, lead=0):
    count = values.shape[0] // rows
    flat = len(kept_ref.shape) == 2
    if sent_ref is None:
        if flat:
            kept_ref[lead:] = values
        else:
            kept_ref[pl.ds(first, count)] = values.reshape((count, rows) + values.shape[1:])
        return
    me = ids_ref[0]
    for index in range(count):
        apart = jnp.bitwise_xor(me, first + index)
        spot = 0
        for bit in range(1, bits_of(shards)):
            spot = spot * 2 + jnp.bitwise_and(lax.shift_right_logical(apart, bit), 1)
        piece = values[index * rows : (index + 1) * rows]
        same = jnp.bitwise_and(apart, 1) == 0

        def put(ref, piece=piece, spot=spot):
            if flat:
                ref[pl.ds(pl.multiple_of(lead + spot * rows, 16), rows)] = piece
            else:
                ref[spot] = piece

        pl.when(same)(functools.partial(put, kept_ref))
        pl.when(jnp.logical_not(same))(functools.partial(put, sent_ref))


def weight_kernel(ids_ref, left_ref, right_ref, *refs, shards, rows, first_step, extra):
    out_refs = refs[2 * extra :]
    sent_ref = out_refs[1] if len(out_refs) > 1 else None
    step = pl.program_id(0)

    def put(left_ref, right_ref):
        right = right_ref[0] if len(right_ref.shape) == 3 else right_ref[...]
        values = dot_tn(left_ref[...], right).astype(BF)
        place_pieces(
            ids_ref, values, out_refs[0], sent_ref, shards, rows, step * first_step
        )

    if extra:
        last = pl.num_programs(0) - extra * (refs[1].shape[1] // right_ref.shape[2])
        pl.when(step < last)(lambda: put(left_ref, right_ref))

        @pl.when(step >= last)
        def _():
            wide = right_ref.shape[2]
            for index in range(refs[1].shape[1] // wide):
                part = pl.ds(index * wide, wide)

                @pl.when(step == last + index)
                def _(part=part):
                    put(refs[0], refs[1].at[:, part])

    else:
        put(left_ref, right_ref)


def weight_grad(ids, left, right, shards, split, name, deps=(), extra=()):
    count, tall = left.shape
    stacked = right.ndim == 3
    wide = right.shape[-1]
    step = wide if stacked else min(768, max(tall, wide))
    narrow = tall > wide and not stacked
    rows = tall // shards
    outs = 2 if split else 1
    pieces = shards // outs
    more_specs = []
    if narrow:
        grid, first_step, out_wide = tall // step, step // rows, wide
        specs = [
            pl.BlockSpec((count, step), lambda i, ids: (0, i)),
            pl.BlockSpec((count, wide), lambda i, ids: (0, 0)),
        ]
        out_spec = pl.BlockSpec((pieces, rows, wide), lambda i, ids: (0, 0, 0))
    else:
        first_step = 0
        if stacked:
            kinds = right.shape[0]
            grid, out_wide = kinds, kinds * wide
            if extra:
                grid, out_wide = grid + extra[1].shape[1] // wide, out_wide + extra[1].shape[1]
                more_specs = [full_spec(value.shape) for value in extra]
            right_spec = pl.BlockSpec(
                (1, count, step), lambda i, ids: (jnp.minimum(i, kinds - 1), 0, 0)
            )
        else:
            grid, out_wide = wide // step, wide
            right_spec = pl.BlockSpec((count, step), lambda i, ids: (0, i))
        specs = [pl.BlockSpec((count, tall), lambda i, ids: (0, 0)), right_spec]
        out_spec = pl.BlockSpec((pieces, rows, step), lambda i, ids: (0, 0, i))
    kernel = functools.partial(
        weight_kernel,
        shards=shards,
        rows=rows,
        first_step=first_step,
        extra=1 if extra else 0,
    )
    return pl.pallas_call(
        kernel,
        grid_spec=pltpu.PrefetchScalarGridSpec(
            num_scalar_prefetch=1,
            grid=(grid,),
            in_specs=specs + more_specs,
            out_specs=[out_spec] * outs,
        ),
        out_shape=[jax.ShapeDtypeStruct((pieces, rows, out_wide), BF)] * outs,
        compiler_params=params(),
        cost_estimate=cost(0),
        name=name,
    )(tie(ids, *deps), left, right, *extra)


def embed_kernel(
    ids_ref,
    state_ref,
    grad_ref,
    vectors_ref,
    down_sums_ref,
    middle_sums_ref,
    *refs,
    offsets,
    arrays,
    chunks,
):
    grad_refs = refs[:chunks]
    pieces = refs[chunks : chunks + arrays]
    patch_ref, small_ref, weight, sums, sems = refs[chunks + arrays :]
    step = pl.program_id(0)

    @pl.when(step == 0)
    def _():
        copies = fetch(ids_ref, pieces, offsets, weight, sems)
        begin(copies)
        sums[...] = jnp.zeros_like(sums)
        finish(copies)

    normed = 0.0
    at = 0
    for ref in grad_refs:
        wide = ref.shape[2]
        for kind in range(3):
            first = kind * D + at
            normed = normed + dot_nt(ref[kind], weight[:, first : first + wide])
        at += wide
    unit, scale = norm_parts(state_ref[...])
    grad = grad_ref[...] + norm_back(normed, vectors_ref[1:2], unit, scale)
    patch_ref[...] = grad.astype(BF)
    sums[0:1] += column_sum(grad)
    sums[1:2] += column_sum(normed * unit)
    sums[2:3] += column_sum(normed)

    @pl.when(step == pl.num_programs(0) - 1)
    def _():
        small = [sums[0:3], middle_sums_ref[0:3], down_sums_ref[0:1, :D]]
        small += [
            down_sums_ref[1:2, index * D : (index + 1) * D] for index in range(FF // D)
        ]
        small += [jnp.zeros((SMALL_PAD - SMALL, D), F32)]
        small_ref[:, :D] = jnp.concatenate(small, axis=0).astype(BF)
        small_ref[:, D:] = jnp.zeros((SMALL_PAD, PIXALL - D), BF)


def embed_back(
    ids, grads, state, grad, vectors, down_sums, middle_sums, weight, deps=()
):
    arrays, offsets = weight
    count = state.shape[0]
    kernel = functools.partial(
        embed_kernel, offsets=offsets, arrays=len(arrays), chunks=len(grads)
    )
    return pl.pallas_call(
        kernel,
        grid_spec=pltpu.PrefetchScalarGridSpec(
            num_scalar_prefetch=1,
            grid=(count // ROWS,),
            in_specs=[
                row_spec(D),
                row_spec(D),
                full_spec(vectors.shape),
                full_spec(down_sums.shape),
                full_spec(middle_sums.shape),
            ]
            + [
                pl.BlockSpec((3, ROWS, part.shape[2]), lambda i, ids: (0, i, 0))
                for part in grads
            ]
            + anys(len(arrays)),
            out_specs=[row_spec(D), full_spec((SMALL_PAD, PIXALL))],
            scratch_shapes=[
                pltpu.VMEM((D, 3 * D), BF),
                pltpu.VMEM((8, D), F32),
                pltpu.SemaphoreType.DMA((piece_count(weight),)),
            ],
        ),
        out_shape=[
            jax.ShapeDtypeStruct((count, D), BF),
            jax.ShapeDtypeStruct((SMALL_PAD, PIXALL), BF),
        ],
        compiler_params=params(),
        cost_estimate=cost(0),
        name="embed_back",
    )(tie(ids, *deps), state, grad, vectors, down_sums, middle_sums, *grads, *arrays)


def patch_back_kernel(ids_ref, patch_ref, pixels_ref, rows_ref, small_ref, *out_refs, shards):
    sent_ref = out_refs[1] if len(out_refs) > 1 else None
    spread = spread_pixels(pixels_ref[...], rows_ref[:, 2:3])
    values = dot_tn(patch_ref[...], spread).astype(BF)
    place_pieces(
        ids_ref, values, out_refs[0], sent_ref, shards, D // shards, 0, SMALL_PAD
    )
    for ref in out_refs:
        ref[:SMALL_PAD] = small_ref[...]


def patch_back(ids, patch_grad, pixels, rows, small, shards, split, deps=()):
    count = pixels.shape[0]
    outs = 2 if split else 1
    held = (SMALL_PAD + D // outs, PIXALL)
    return pl.pallas_call(
        functools.partial(patch_back_kernel, shards=shards),
        grid_spec=pltpu.PrefetchScalarGridSpec(
            num_scalar_prefetch=1,
            grid=(1,),
            in_specs=[
                full_spec((count, D)),
                full_spec((count, PIXC)),
                full_spec(rows.shape),
                full_spec(small.shape),
            ],
            out_specs=[full_spec(held)] * outs,
        ),
        out_shape=[jax.ShapeDtypeStruct(held, BF)] * outs,
        compiler_params=params(),
        cost_estimate=cost(0),
        name="patch_back",
    )(tie(ids, *deps), patch_grad, pixels, rows, small)


def pixel_kernel(ids_ref, patch_ref, rows_ref, weight_ref, out_ref):
    fine = rows_ref[:, 2:3]
    both = dot_nt(patch_ref[...], weight_ref[...])
    wide = PIXALL - PIXC
    rough = both[:, :PIXC] * (1.0 - fine)
    first = rough[:, :wide] + both[:, PIXC:] * fine
    out_ref[...] = jnp.concatenate([first, rough[:, wide:]], axis=1).astype(BF)


def pixel_back(ids, patch_grad, rows, weight, deps=()):
    count = patch_grad.shape[0]
    return pl.pallas_call(
        pixel_kernel,
        grid_spec=pltpu.PrefetchScalarGridSpec(
            num_scalar_prefetch=1,
            grid=(count // ROWS,),
            in_specs=[row_spec(D), row_spec(8), full_spec(weight.shape)],
            out_specs=row_spec(PIXC),
        ),
        out_shape=jax.ShapeDtypeStruct((count, PIXC), BF),
        compiler_params=params(),
        cost_estimate=cost(4),
        name="pixel_back",
    )(tie(ids, *deps), patch_grad, rows, weight)


def base_kernel(ids_ref, turned_ref, coarse_ref, fine_ref, out_ref, square_ref):
    turned = turned_ref[...]
    grad = dot_nn(turned[:, :PIXC], coarse_ref[...])
    grad = grad + dot_nn(turned[:, PIXC : PIXC + PIXF], fine_ref[...])

    @pl.when(pl.program_id(0) == 0)
    def _():
        square_ref[...] = jnp.zeros_like(square_ref)

    square_ref[...] += jnp.sum(grad * grad, axis=0, keepdims=True)
    low = grad.astype(BF)
    rows = out_ref.shape[2]
    for index in range(out_ref.shape[0]):
        out_ref[index] = low[:, index * rows : (index + 1) * rows]


def base_back(ids, turned, coarse, fine, shards, deps=()):
    count, wide = turned.shape[0], coarse.shape[1]
    step = 768
    rows = wide // shards
    return pl.pallas_call(
        base_kernel,
        grid_spec=pltpu.PrefetchScalarGridSpec(
            num_scalar_prefetch=1,
            grid=(wide // step,),
            in_specs=[
                full_spec(turned.shape),
                pl.BlockSpec((PIXC, step), lambda i, ids: (0, i)),
                pl.BlockSpec((PIXF, step), lambda i, ids: (0, i)),
            ],
            out_specs=[
                pl.BlockSpec((step // rows, count, rows), lambda i, ids: (i, 0, 0)),
                full_spec((1, step)),
            ],
        ),
        out_shape=[
            jax.ShapeDtypeStruct((shards, count, rows), BF),
            jax.ShapeDtypeStruct((1, step), F32),
        ],
        compiler_params=params(),
        cost_estimate=cost(0),
        name="base_back",
    )(tie(ids, *deps), turned, coarse, fine)


def bits_of(count):
    bits = count.bit_length() - 1
    assert count == 1 << bits
    return bits


def swap(value, axis, count, mask):
    return lax.ppermute(value, axis, [(i, i ^ mask) for i in range(count)])


def add_low(left, right):
    return (left.astype(F32) + right.astype(F32)).astype(BF)


class Gather:
    def __init__(self, shard, count):
        self.held, self.places, self.count = shard[None], [0], count
        self.bits = list(reversed(range(2, bits_of(count))))
        self.other = None

    def land(self, *after):
        if self.other is not None:
            self.held = jnp.concatenate([self.held, tie(self.other, *after)])
            self.other = None
        return self.held

    def step(self, *after):
        bit = self.bits.pop(0)
        held = tie(self.land(*after), *after)
        self.other = swap(held, "fsdp", self.count, 1 << bit)
        self.places = self.places + [place ^ (1 << bit) for place in self.places]
        return self.other

    def high(self, *after):
        held = tie(self.held, *after)
        masks = [0]
        while self.bits:
            masks = masks + [mask ^ (1 << self.bits[0]) for mask in masks]
            self.bits.pop(0)
        self.rest = [swap(held, "fsdp", self.count, mask) for mask in masks[1:]]
        self.places = masks
        return self.rest

    def join(self, *after):
        self.held = jnp.concatenate([self.held] + [tie(part, *after) for part in self.rest])

    def far(self, *after):
        held = tie(self.land(*after), *after)
        self.other = swap(held, "fsdp", self.count, 2)
        self.held_core = swap(held, "fsdp", self.count, 1)
        return self.other

    def far_halves(self, there, *after):
        held = tie(self.land(*after), *after)
        half = held.shape[2] // 2
        sent = lax.dynamic_slice_in_dim(held, there * half, half, axis=2)
        self.mine = swap(sent, "fsdp", self.count, 2)
        self.held_core = swap(held, "fsdp", self.count, 1)
        return self.mine

    def near_halves(self, *after):
        mine = tie(self.mine, *after)
        rest = swap(mine, "rep", 2, 1)
        mine_core = swap(mine, "fsdp", self.count, 1)
        rest_core = swap(rest, "fsdp", self.count, 1)
        arrays = (self.held, self.held_core, self.mine, mine_core, rest, rest_core)
        offsets = [tuple(p ^ mask for p in self.places) for mask in (0, 1)]
        offsets += [
            tuple((p ^ mask, side) for p in self.places) for side in (0, 1) for mask in (2, 3)
        ]
        return (arrays, tuple(offsets)), rest

    def near(self, *after):
        other_core = swap(tie(self.other, *after), "fsdp", self.count, 1)
        offsets = tuple(tuple(p ^ mask for p in self.places) for mask in (0, 1, 2, 3))
        return (self.held, self.held_core, self.other, other_core), offsets


def halves_of(value, side):
    wide = value.shape[1] // 2
    return value[:, side * wide : (side + 1) * wide]


def gather_whole(shard, count):
    here = lax.axis_index("fsdp")
    held = shard[None]
    for bit in reversed(range(bits_of(count))):
        other = swap(held, "fsdp", count, 1 << bit)
        upper = (here >> bit) & 1 == 1
        both = jnp.where(
            upper, jnp.stack([other, held], axis=1), jnp.stack([held, other], axis=1)
        )
        held = both.reshape((-1,) + shard.shape)
    return held.reshape((-1,) + shard.shape[1:])


def as_piece(whole):
    return (whole[None],), ((None,),)


def scatter_whole(blocks, count):
    here = lax.axis_index("fsdp")
    held = blocks
    for bit in range(bits_of(count)):
        side = (here >> bit) & 1
        halves = held.reshape((held.shape[0] // 2, 2) + held.shape[1:])
        sent = lax.dynamic_index_in_dim(halves, 1 - side, axis=1, keepdims=False)
        kept = lax.dynamic_index_in_dim(halves, side, axis=1, keepdims=False)
        held = add_low(kept, swap(sent, "fsdp", count, 1 << bit))
    return held[0]


class Scatter:
    def __init__(self, parts, shards, reps, plan, lead=0):
        self.kept, self.ready = parts
        self.shards, self.reps, self.lead = shards, reps, lead
        self.plan = plan
        self.at = 0

    def step(self, *after):
        kind = self.plan[self.at]
        value = tie(self.ready, *after)
        if isinstance(kind, int):
            self.other = swap(value, "fsdp", self.shards, 1 << kind)
        else:
            self.other = swap(value, "rep", self.reps, 1)
        self.at += 1

    def land(self, *after):
        kept, other = self.kept, tie(self.other, *after)
        following = self.plan[self.at] if self.at < len(self.plan) else None
        there = lax.axis_index("rep")
        if following == "half":
            wide = kept.shape[-1] // 2

            def columns(side):
                return add_low(
                    lax.dynamic_slice_in_dim(kept, side * wide, wide, axis=2),
                    lax.dynamic_slice_in_dim(other, side * wide, wide, axis=2),
                )

            self.kept, self.ready = columns(there), columns(1 - there)
        elif isinstance(following, int):
            half = (kept.shape[0] - self.lead) // 2 + self.lead
            low, high = add_low(kept[:half], other[:half]), add_low(kept[half:], other[half:])
            self.kept, self.ready = low, high
            if self.lead:
                self.ready = jnp.concatenate([low[: self.lead], high])
        else:
            self.kept = self.ready = add_low(kept, other)
        return self.ready


def merged(parts, more, shards, reps, plan):
    kept = jnp.concatenate([part.kept for part in (parts, more)], axis=2)
    ready = jnp.concatenate([part.ready for part in (parts, more)], axis=2)
    return Scatter((kept, ready), shards, reps, plan)


def rows_of(value):
    return [value[:, at : at + D] for at in range(0, value.shape[1], D)]


def replicas(value, count):
    for bit in range(bits_of(count)):
        value = add_low(value, swap(value, "rep", count, 1 << bit))
    return value


def total_of(value, count):
    bits = list(range(bits_of(count)))
    while bits:
        low = 1 << bits.pop(0)
        near = swap(value, "fsdp", count, low)
        if len(bits) == 1:
            high = 1 << bits.pop(0)
            far = swap(value, "fsdp", count, high)
            both = swap(value, "fsdp", count, high | low)
            value = (value + near) + (far + both)
        else:
            value = value + near
    return value


def body(
    shards,
    reps,
    pixels,
    image_tokens,
    patch_class,
    resize_coarse,
    resize_fine,
    w_base,
    w_qkv,
    w_proj,
    w_fc1,
    w_fc2,
    small_params,
    first_base,
    first_qkv,
    first_proj,
    first_fc1,
    first_fc2,
    first_small,
    second_base,
    second_qkv,
    second_proj,
    second_fc1,
    second_fc2,
    second_small,
    cotangent,
):
    rows_here = pixels.shape[0]
    here = lax.axis_index("fsdp")
    there = lax.axis_index("rep")
    ids = jnp.stack([here, there]).astype(jnp.int32)
    base_rows = w_base.shape[0]
    pieced = shards == 16 and reps == 2 and w_qkv.shape[0] % 16 == 0

    segment, alive, finer = rows_plan(image_tokens[0], patch_class[0], rows_here)
    segment_col = segment[:, None]
    nothing = jnp.zeros_like(alive)
    rows = jnp.stack([nothing, alive, finer] + [nothing] * 5, axis=1)

    low_qkv = w_qkv.astype(BF)
    low_both = jnp.concatenate(
        [part for side in (0, 1) for part in (halves_of(w_proj, side), halves_of(w_fc1, side))],
        axis=1,
    ).astype(BF)
    low_fc2 = w_fc2.astype(BF)
    small_cols = small_params.shape[1]
    if pieced:
        half_cols = D // 2
        lanes = jnp.arange(D, dtype=jnp.int32)[None, :] // small_cols
        placed = jnp.where(lanes == here, jnp.tile(small_params, (1, shards)), 0.0)
        placed = jnp.pad(placed, ((0, SMALL_PAD - SMALL), (0, 0))).astype(BF)
        mine = lax.dynamic_slice_in_dim(w_base, there * half_cols, half_cols, axis=1)
        message = jnp.concatenate(
            [mine.astype(BF), placed[:, :half_cols], placed[:, half_cols:]], axis=0
        )
        gather_base = Gather(message, shards)
        gather_base.step()
        base_done = gather_base.step()
        held, places = gather_base.land(), gather_base.places
        other = swap(held, "fsdp", shards, 1)
        offsets = (tuple(places), tuple(place ^ 1 for place in places))
        part = resize_part(ids, resize_coarse, resize_fine, (held, other), offsets, base_rows)
        gather_qkv = Gather(low_qkv, shards)
        gather_qkv.step(base_done)
        qkv_done = gather_qkv.step(part)
        part = add_low(part, swap(part, "fsdp", shards, 2))
        half_rows = PIXALL // 2
        quarter = part[:half_rows][None]
        small_low = part[half_rows:]
        vectors = jnp.concatenate([small_low[:SMALL_PAD], small_low[SMALL_PAD:]], axis=1)
        quarter_rep = swap(quarter, "rep", reps, 1)
        quarter_core = swap(quarter, "fsdp", shards, 1)
        quarter_both = swap(quarter_rep, "fsdp", shards, 1)
        patch_arrays = (quarter, quarter_core, quarter_rep, quarter_both)
        patch_places = (((0, 0),), ((1, 0),), ((0, 1),), ((1, 1),))
        gather_qkv.far(quarter)
        gather_both = Gather(low_both, shards)
        gather_both.step(qkv_done, quarter)
    else:
        base = gather_whole(w_base.astype(BF), shards)
        coarse = dot_nn(resize_coarse, base).astype(BF)
        fine = dot_nn(resize_fine, base).astype(BF)
        whole = jnp.concatenate([coarse, fine, jnp.zeros((PIXALL - PIXC - PIXF, D), BF)])
        patch_arrays = (whole[None],)
        patch_places = ((None,),)
        vectors = gather_whole(small_params.astype(BF).T, shards).T
        vectors = jnp.pad(vectors, ((0, SMALL_PAD - SMALL), (0, 0)))
        weight_qkv = as_piece(gather_whole(low_qkv, shards))
        weight_both = as_piece(gather_whole(low_both, shards))
        weight_fc2 = as_piece(gather_whole(low_fc2, shards))
    vectors = vectors.astype(F32)
    bias = vectors[7:11].reshape(1, FF)

    state_zero, normed_one, patch_weight = patch(
        ids, pixels, rows, vectors, patch_arrays, patch_places
    )
    if pieced:
        weight_qkv = gather_qkv.near(state_zero)
        both_done = gather_both.step(state_zero)
    qkv = project_qkv(ids, normed_one, weight_qkv)
    chunks = 3
    pairs = HEADS // 2
    many = pairs // chunks
    if pieced:
        gather_fc2 = Gather(low_fc2, shards)
        gather_fc2.high(qkv)
    outs = [attend(ids, qkv, segment_col, 0, many)]
    after = ()
    if pieced:
        both_held = gather_both.land(outs[0][0])
        both_mine = gather_both.far_halves(there, both_held)
        after = (both_held,)
    for index in range(1, chunks):
        outs.append(attend(ids, qkv, segment_col, index * many, many, after))
        after = (outs[-1][0],)
    if pieced:
        weight_both, both_rest = gather_both.near_halves(outs[-1][0])
        gather_fc2.join(both_mine, outs[-1][0])
        gather_fc2.far()
    mixed = jnp.concatenate([out[0] for out in outs], axis=1)
    logs = [out[1] for out in outs]
    state_one, normed_two, hidden, slope = feed_up(
        ids, mixed, state_zero, vectors, bias, weight_both
    )
    if pieced:
        weight_fc2 = gather_fc2.near(state_one)
    activations, branch, grad_before, down_sums = feed_down(
        ids, hidden, slope, state_one, cotangent, rows, vectors, weight_fc2
    )

    def qkv_chunk(index, *after):
        many = pairs // chunks
        return attend_back(
            ids, qkv, segment_col, mixed, grad_mixed, logs[index], index * many, many, after
        )

    def chunk_grad(part, *after, extra=()):
        return weight_grad(
            ids, normed_one, part, shards, pieced, "grad_qkv", after, extra
        )

    def finish_embed(grads, *after):
        return embed_back(
            ids,
            grads,
            state_zero,
            grad_one,
            vectors,
            down_sums,
            middle_sums,
            weight_qkv,
            after,
        )

    part_fc2 = weight_grad(ids, hidden, branch, shards, pieced, "grad_fc2")
    if pieced:
        every = list(range(bits_of(shards)))
        near, far = every[:2], every[2:]
        sum_fc2 = Scatter(part_fc2, shards, reps, every)
        sum_fc2.step()
        part_fc1 = weight_grad(
            ids, normed_two, grad_before, shards, pieced, "grad_fc1", part_fc2
        )
        sum_fc1 = Scatter(part_fc1, shards, reps, [0, "half"] + every[1:])
        sum_fc2.land(part_fc1[0])
        sum_fc2.step()
        sum_fc1.step()
        grad_one, grad_attn, grad_mixed, middle_sums = middle_back(
            ids,
            grad_before,
            state_one,
            branch,
            vectors,
            weight_both,
            (sum_fc2.ready, part_fc1[0]),
        )
        sum_fc1.land(grad_one)
        sum_fc1.step()
        first = qkv_chunk(0, sum_fc1.ready)
        part_first = chunk_grad(first, extra=(mixed, grad_attn))
        sum_first = Scatter(part_first, shards, reps, [0, "half"] + every[1:])
        sum_fc2.land(part_first[0])
        sum_fc2.step()
        sum_first.step()
        second = qkv_chunk(1, sum_fc2.ready, part_first[0])
        sum_first.land(second)
        sum_first.step()
        sum_fc1.land(second)
        sum_fc1.step(sum_first.ready)
        part_second = chunk_grad(second, sum_first.ready, sum_fc1.ready)
        sum_second = Scatter(part_second, shards, reps, every)
        sum_fc2.land(part_second[0])
        sum_fc2.step()
        sum_second.step()
        third = qkv_chunk(2, sum_fc2.ready, part_second[0])
        sum_first.land(third)
        sum_first.step()
        sum_second.land(third)
        sum_second.step(sum_first.ready)
        part_third = chunk_grad(third, sum_second.ready, sum_first.ready)
        sum_third = Scatter(part_third, shards, reps, every)
        sum_third.step()
        sum_fc1.land(part_third[0])
        sum_fc1.step()
        patch_grad, small_part = finish_embed(
            (first, second, third), part_third[0], sum_fc1.ready
        )
        sum_third.land(patch_grad)
        sum_third.step()
        sum_first.land(patch_grad)
        sum_second.land(patch_grad)
        sum_both = merged(sum_first, sum_second, shards, reps, far)
        sum_both.step(sum_third.ready)
        patch_parts = patch_back(
            ids,
            patch_grad,
            pixels,
            rows,
            small_part,
            shards,
            pieced,
            (sum_third.ready, sum_both.ready),
        )
        sum_patch = Scatter(patch_parts, shards, reps, every, SMALL_PAD)
        sum_patch.step()
        sum_fc1.land(patch_parts[0])
        sum_fc1.step()
        sum_fc2.land(patch_parts[0])
        fc2_other = swap(sum_fc2.kept, "rep", reps, 1)
        sum_patch.land(sum_fc1.ready, sum_fc2.kept)
        sum_patch.step()
        mark = sum_patch.ready
        pixel_grad = pixel_back(ids, patch_grad, rows, patch_weight, (mark,))
        sum_third.land(pixel_grad)
        sum_third.step()
        sum_both.land(sum_third.ready)
        sum_both.step()
        sum_patch.land(sum_both.ready)
        sum_patch.step()
        mark = sum_patch.ready
        sum_fc1.land(mark)
        sum_third.land(mark)
        sum_third.step()
        sum_patch.land(sum_third.ready, sum_fc1.ready)
        sum_patch.step()
        mark = sum_patch.ready
        sum_both.land(mark)
        ends = jnp.concatenate([*rows_of(sum_fc1.kept[0]), *rows_of(sum_both.kept[0])])
        ends_other = swap(ends, "rep", reps, 1)
        sum_third.land(ends)
        grad_fc2 = add_low(sum_fc2.kept[0], tie(fc2_other, ends)[0])
        sum_patch.land(sum_third.kept)
        tail = jnp.pad(sum_third.kept[0], ((0, 0), (0, PIXALL - D)))
        tail = jnp.concatenate([sum_patch.kept, tail])
        tail = add_low(tail, swap(tail, "rep", reps, 1))
        few = w_qkv.shape[0]
        parts = [ends[at * few :][:few] for at in range(4)]
        others = [ends_other[at * few :][:few] for at in range(4)]
        low = [jnp.where(there == 0, a, b) for a, b in zip(parts, others)]
        high = [jnp.where(there == 0, b, a) for a, b in zip(parts, others)]
        grad_fc1 = jnp.concatenate(low[:2] + high[:2], axis=1)
        grad_first, grad_proj = low[2], high[2]
        grad_second = add_low(parts[3], others[3])
        split_at = SMALL_PAD + D // shards
        turned, grad_third = tail[:split_at], tail[split_at:, :D]
    else:

        def owned(parts):
            return replicas(scatter_whole(parts[0], shards), reps)

        grad_fc2 = owned(part_fc2)
        grad_fc1 = owned(
            weight_grad(ids, normed_two, grad_before, shards, pieced, "grad_fc1")
        )
        grad_one, grad_attn, grad_mixed, middle_sums = middle_back(
            ids, grad_before, state_one, branch, vectors, weight_both
        )
        grad_proj = owned(weight_grad(ids, mixed, grad_attn, shards, pieced, "grad_proj"))
        grads = [qkv_chunk(index) for index in range(chunks)]
        grad_first, grad_second, grad_third = [owned(chunk_grad(part)) for part in grads]
        patch_grad, small_part = finish_embed(grads)
        patch_parts = patch_back(ids, patch_grad, pixels, rows, small_part, shards, pieced)
        pixel_grad = pixel_back(ids, patch_grad, rows, patch_weight)
        small_all = small_part
        for bit in range(bits_of(shards)):
            small_all = add_low(small_all, swap(small_all, "fsdp", shards, 1 << bit))
        patch_all = patch_parts[0][SMALL_PAD:].reshape(shards, D // shards, PIXALL)
        turned = jnp.concatenate([replicas(small_all, reps), owned((patch_all,))])

    small_total = turned[:SMALL, :D].astype(F32)
    turned = turned[SMALL_PAD:]
    grad_small = lax.dynamic_slice_in_dim(small_total, here * small_cols, small_cols, axis=1)
    if pieced:
        pieces, square_parts = base_back(ids, turned, resize_coarse, resize_fine, shards)
        squares = jnp.sum(square_parts)
    else:
        base_cols = dot_nn(turned[:, :PIXC], resize_coarse)
        base_cols = base_cols + dot_nn(turned[:, PIXC : PIXC + PIXF], resize_fine)
        squares = jnp.sum(base_cols * base_cols)
        pieces = base_cols.astype(BF).reshape(base_cols.shape[0], shards, base_rows)
        pieces = pieces.transpose(1, 0, 2)
    pieces = lax.all_to_all(pieces, "fsdp", 0, 0)
    grad_base = pieces.reshape(D, base_rows).T
    wide = grad_first.shape[1] // 3
    grad_qkv = jnp.concatenate(
        [
            part[:, kind * wide : (kind + 1) * wide]
            for kind in range(3)
            for part in (grad_first, grad_second, grad_third)
        ],
        axis=1,
    )

    shards_of = [
        value.astype(F32) for value in (grad_base, grad_qkv, grad_proj, grad_fc1, grad_fc2)
    ] + [grad_small]
    for shard in shards_of[1:5]:
        squares = squares + jnp.sum(shard * shard)
    squares = total_of(squares, shards) + jnp.sum(small_total * small_total)
    grad_norm = jnp.sqrt(squares)
    clip = jnp.minimum(1.0, CLIP_NORM / grad_norm)
    masters = (w_base, w_qkv, w_proj, w_fc1, w_fc2, small_params)
    firsts = (first_base, first_qkv, first_proj, first_fc1, first_fc2, first_small)
    seconds = (second_base, second_qkv, second_proj, second_fc1, second_fc2, second_small)
    rates = (RATE, RATE, RATE, RATE, RATE, RATE_SMALL)
    results = [
        adamw(masters[index], shards_of[index], firsts[index], seconds[index], clip, rates[index])
        for index in range(6)
    ]
    return (activations, pixel_grad, grad_norm) + tuple(
        results[index][kind] for kind in range(3) for index in range(6)
    )


def solution(mesh):
    tokens = P(("fsdp", "rep"), None)
    split_rows = P("fsdp", None)
    states = (split_rows,) * 5 + (P(None, "fsdp"),)
    in_specs = (tokens, tokens, tokens, P(), P()) + states * 3 + (tokens,)
    out_specs = (tokens, tokens, P()) + states * 3
    step = functools.partial(body, mesh.shape["fsdp"], mesh.shape["rep"])
    return jax.shard_map(
        step, mesh=mesh, in_specs=in_specs, out_specs=out_specs, check_vma=False
    )
```

```python
import functools
import math

import jax
import jax.numpy as jnp
from jax import lax
from jax.experimental import pallas as pl
from jax.experimental.pallas import tpu as pltpu
from jax.sharding import PartitionSpec as P

D = 768
HEADS = 12
HEAD_DIM = 64
FF = 3072
PIXC = 768
PIXF = 192
PIXALL = 1024
STEP = 10
SLOTS = 5
SMALL = 11
SMALL_PAD = 16


EPS_NORM = 1e-06
RATE = 0.05
RATE_SMALL = 0.5
BETA_ONE = 0.9
BETA_TWO = 0.95
ADAM_EPS = 1e-08
DECAY = 0.05
CLIP_NORM = 1.0

LOG2E = math.log2(math.e)
FAR = -1e30
ATT_ROWS = 512
ROWS = 256
VMEM = 16 * 2**20
BF = jnp.bfloat16
F32 = jnp.float32
ANY = pltpu.HBM


def rows_plan(lengths, classes, count):
    ends = jnp.cumsum(lengths)
    positions = jnp.arange(count, dtype=jnp.int32)
    segment = jnp.sum((positions[:, None] >= ends[None, :]).astype(jnp.int32), axis=1)
    alive = (positions < ends[-1]).astype(F32)
    slots = jnp.arange(lengths.shape[0], dtype=jnp.int32)
    member = (segment[:, None] == slots[None, :]).astype(F32)
    finer = jnp.sum(member * classes[None, :].astype(F32), axis=1)
    return (segment, alive, finer)


def adamw(weight, grad, first, second, clip, rate):
    scaled = grad * clip
    first_new = BETA_ONE * first + (1.0 - BETA_ONE) * scaled
    second_new = BETA_TWO * second + (1.0 - BETA_TWO) * scaled * scaled
    update = (
        first_new
        / (1.0 - BETA_ONE**STEP)
        / (jnp.sqrt(second_new / (1.0 - BETA_TWO**STEP)) + ADAM_EPS)
    )
    return (weight - rate * (update + DECAY * weight), first_new, second_new)


def dot_nn(left, right):
    return jnp.dot(left, right, preferred_element_type=F32)


def dot_nt(left, right):
    return lax.dot_general(left, right, (((1,), (1,)), ((), ())), preferred_element_type=F32)


def dot_tn(left, right):
    return lax.dot_general(left, right, (((0,), (0,)), ((), ())), preferred_element_type=F32)


def norm_parts(values):
    average = jnp.mean(values, axis=-1, keepdims=True)
    centre = values - average
    spread = jnp.mean(centre * centre, axis=-1, keepdims=True)
    scale = lax.rsqrt(spread + EPS_NORM)
    return centre * scale, scale


def norm_back(grad, gain, unit, scale):
    inner = grad * gain
    mean_inner = jnp.mean(inner, axis=-1, keepdims=True)
    mean_unit = jnp.mean(inner * unit, axis=-1, keepdims=True)
    return scale * (inner - mean_inner - unit * mean_unit)


def column_sum(values):
    return jnp.sum(values, axis=0, keepdims=True)


def fetch(ids_ref, refs, offsets, target, sems, column=0, width=None):
    me = ids_ref[0]
    copies = []
    for ref, places in zip(refs, offsets):
        rows = ref.shape[1]
        for index, place in enumerate(places):
            source = ref.at[index]
            if width is not None and width != ref.shape[2]:
                source = ref.at[index, :, pl.ds(column, width)]
            first = 0 if place is None else jnp.bitwise_xor(me, place) * rows
            if place is not None:
                first = pl.multiple_of(first, rows)
            copies.append(
                pltpu.make_async_copy(
                    source, target.at[pl.ds(first, rows)], sems.at[len(copies)]
                )
            )
    return copies


def fetch_halves(ids_ref, refs, offsets, targets, sems):
    me = ids_ref[0]
    copies = []
    for ref, places in zip(refs, offsets):
        rows = ref.shape[1]
        for index, place in enumerate(places):
            if place is None:
                first, sides = 0, (0, 1)
            elif isinstance(place, tuple):
                first = pl.multiple_of(jnp.bitwise_xor(me, place[0]) * rows, rows)
                sides = (jnp.bitwise_xor(ids_ref[1], place[1]),)
            else:
                first = pl.multiple_of(jnp.bitwise_xor(me, place) * rows, rows)
                sides = (0, 1)
            at = 0
            for side in sides:
                for target in targets:
                    half = target.shape[1] // 2
                    column = side * half
                    if len(sides) == 1:
                        column = pl.multiple_of(column, 128)
                    copies.append(
                        pltpu.make_async_copy(
                            ref.at[index, :, pl.ds(at, half)],
                            target.at[pl.ds(first, rows), pl.ds(column, half)],
                            sems.at[len(copies)],
                        )
                    )
                    at += half
    return copies


def halves_count(weight):
    return sum(
        2 if isinstance(place, tuple) else 4 for places in weight[1] for place in places
    )


def begin(copies):
    for copy in copies:
        copy.start()


def finish(copies):
    for copy in copies:
        copy.wait()


def piece_count(weight):
    return sum(len(places) for places in weight[1])


def anys(count):
    return [pl.BlockSpec(memory_space=ANY)] * count


def params(limit=VMEM):
    return pltpu.CompilerParams(vmem_limit_bytes=limit)


def cost(micros):
    return pl.CostEstimate(
        flops=int(micros * 1.15e9), bytes_accessed=0, transcendentals=0
    )


def tie(value, *others):
    return lax.optimization_barrier((value,) + others)[0] if others else value


def row_spec(width, step=ROWS):
    return pl.BlockSpec((step, width), lambda i, ids: (i, 0))


def full_spec(shape):
    return pl.BlockSpec(shape, lambda i, ids: (0,) * len(shape))


def resize_kernel(ids_ref, *refs, offsets, arrays, shard_rows):
    coarse_ref, fine_ref = refs[:2]
    pieces = refs[2 : 2 + arrays]
    out_ref, resize, base, small, sems = refs[2 + arrays :]
    me = ids_ref[0]
    core = jnp.bitwise_and(me, 1)
    side = jnp.bitwise_and(lax.shift_right_logical(me, 1), 1)
    half = PIXALL // 2
    width = 2 * shard_rows
    blocks = resize.shape[1] // width
    rest = PIXC - half

    def spans(low):
        copies = []
        for block in range(blocks):
            source = pl.ds(pl.multiple_of((2 * block + side) * width, 128), width)
            target = pl.ds(block * width, width)
            at = 2 * block
            if low:
                copies.append(
                    pltpu.make_async_copy(
                        coarse_ref.at[pl.ds(0, half), source],
                        resize.at[pl.ds(0, half), target],
                        sems.at[at],
                    )
                )
            else:
                copies.append(
                    pltpu.make_async_copy(
                        coarse_ref.at[pl.ds(half, rest), source],
                        resize.at[pl.ds(0, rest), target],
                        sems.at[at],
                    )
                )
                copies.append(
                    pltpu.make_async_copy(
                        fine_ref.at[:, source],
                        resize.at[pl.ds(rest, PIXF), target],
                        sems.at[at + 1],
                    )
                )
        return copies

    copies = []
    at = 2 * blocks
    small_at = 0
    for ref, places in zip(pieces, offsets):
        for index, place in enumerate(places):
            shard = jnp.bitwise_xor(me, place)
            spot = lax.shift_right_logical(shard, 2) * 2 + jnp.bitwise_and(shard, 1)
            first = pl.multiple_of(spot * shard_rows, shard_rows)
            copies.append(
                pltpu.make_async_copy(
                    ref.at[index, pl.ds(0, shard_rows)],
                    base.at[pl.ds(first, shard_rows)],
                    sems.at[at],
                )
            )
            copies.append(
                pltpu.make_async_copy(
                    ref.at[index, pl.ds(shard_rows, 2 * SMALL_PAD)],
                    small.at[small_at],
                    sems.at[at + 1],
                )
            )
            at += 2
            small_at += 1
    begin(copies)

    @pl.when(core == 0)
    def _():
        low = spans(True)
        begin(low)
        finish(low)

    @pl.when(core != 0)
    def _():
        resize[pl.ds(rest + PIXF, half - rest - PIXF)] = jnp.zeros(
            (half - rest - PIXF, resize.shape[1]), BF
        )
        high = spans(False)
        begin(high)
        finish(high)

    finish(copies)
    out_ref[:half] = dot_nn(resize[...], base[...]).astype(BF)
    joined = small[0].astype(F32)
    for index in range(1, small_at):
        joined = joined + small[index].astype(F32)
    out_ref[half:] = joined.astype(BF)


def resize_part(ids, coarse, fine, arrays, offsets, shard_rows):
    half = PIXALL // 2
    count = sum(len(places) for places in offsets)
    blocks = count // 2
    return pl.pallas_call(
        functools.partial(
            resize_kernel, offsets=offsets, arrays=len(arrays), shard_rows=shard_rows
        ),
        grid_spec=pltpu.PrefetchScalarGridSpec(
            num_scalar_prefetch=1,
            grid=(1,),
            in_specs=anys(2 + len(arrays)),
            out_specs=full_spec((half + 2 * SMALL_PAD, D // 2)),
            scratch_shapes=[
                pltpu.VMEM((half, count * shard_rows), BF),
                pltpu.VMEM((count * shard_rows, D // 2), BF),
                pltpu.VMEM((count, 2 * SMALL_PAD, D // 2), BF),
                pltpu.SemaphoreType.DMA((2 * blocks + 2 * count,)),
            ],
        ),
        out_shape=jax.ShapeDtypeStruct((half + 2 * SMALL_PAD, D // 2), BF),
        compiler_params=params(),
        cost_estimate=cost(0),
        name="resize_part",
    )(ids, coarse, fine, *arrays)


def spread_pixels(pixels, fine_col):
    rough = jnp.where(fine_col > 0.5, jnp.zeros((), BF), pixels)
    wide = PIXALL - PIXC
    lane = lax.broadcasted_iota(jnp.int32, (pixels.shape[0], wide), 1)
    fine = jnp.where((lane < PIXF) & (fine_col > 0.5), pixels[:, :wide], jnp.zeros((), BF))
    return jnp.concatenate([rough, fine], axis=1)


def patch_kernel(ids_ref, pixels_ref, rows_ref, vectors_ref, *refs, places, arrays):
    pieces = refs[:arrays]
    state_ref, normed_ref, weight_ref, sems = refs[arrays:]

    @pl.when(pl.program_id(0) == 0)
    def _():
        copies = []
        for ref, spots in zip(pieces, places):
            for index, spot in enumerate(spots):
                rows, width = ref.shape[1:]
                first, column = (0, 0) if spot is None else spot
                if spot is not None:
                    first = jnp.bitwise_xor(jnp.bitwise_and(ids_ref[0], 1), first) * rows
                    column = jnp.bitwise_xor(ids_ref[1], column) * width
                    first = pl.multiple_of(first, rows)
                    column = pl.multiple_of(column, 128)
                copies.append(
                    pltpu.make_async_copy(
                        ref.at[index],
                        weight_ref.at[pl.ds(first, rows), pl.ds(column, width)],
                        sems.at[len(copies)],
                    )
                )
        begin(copies)
        finish(copies)

    pixels = spread_pixels(pixels_ref[...], rows_ref[:, 2:3])
    vectors = vectors_ref[...]
    state = dot_nn(pixels, weight_ref[...]) + vectors[0:1]
    unit, _ = norm_parts(state)
    state_ref[...] = state
    normed_ref[...] = (unit * vectors[1:2] + vectors[2:3]).astype(BF)


def patch(ids, pixels, rows, vectors, arrays, places, deps=()):
    count = pixels.shape[0]
    total = sum(len(spots) for spots in places)
    return pl.pallas_call(
        functools.partial(patch_kernel, places=places, arrays=len(arrays)),
        grid_spec=pltpu.PrefetchScalarGridSpec(
            num_scalar_prefetch=1,
            grid=(count // ROWS,),
            in_specs=[row_spec(PIXC), row_spec(8), full_spec(vectors.shape)]
            + anys(len(arrays)),
            out_specs=[row_spec(D), row_spec(D), full_spec((PIXALL, D))],
            scratch_shapes=[pltpu.SemaphoreType.DMA((total,))],
        ),
        out_shape=[
            jax.ShapeDtypeStruct((count, D), F32),
            jax.ShapeDtypeStruct((count, D), BF),
            jax.ShapeDtypeStruct((PIXALL, D), BF),
        ],
        compiler_params=params(52 * 2**20),
        cost_estimate=cost(0),
        name="patch",
    )(tie(ids, *deps), pixels, rows, vectors, *arrays)


def qkv_kernel(ids_ref, normed_ref, *refs, offsets, arrays):
    pieces = refs[:arrays]
    out_ref, weight, sems = refs[arrays:]

    @pl.when(pl.program_id(0) == 0)
    def _():
        copies = fetch(ids_ref, pieces, offsets, weight, sems)
        begin(copies)
        finish(copies)

    out_ref[...] = dot_nn(normed_ref[...], weight[...]).astype(BF)


def project_qkv(ids, normed, weight, deps=()):
    arrays, offsets = weight
    count = normed.shape[0]
    return pl.pallas_call(
        functools.partial(qkv_kernel, offsets=offsets, arrays=len(arrays)),
        grid_spec=pltpu.PrefetchScalarGridSpec(
            num_scalar_prefetch=1,
            grid=(count // ROWS,),
            in_specs=[row_spec(D)] + anys(len(arrays)),
            out_specs=row_spec(3 * D),
            scratch_shapes=[
                pltpu.VMEM((D, 3 * D), BF),
                pltpu.SemaphoreType.DMA((piece_count(weight),)),
            ],
        ),
        out_shape=jax.ShapeDtypeStruct((count, 3 * D), BF),
        compiler_params=params(),
        cost_estimate=cost(0),
        name="project_qkv",
    )(tie(ids, *deps), normed, *arrays)


def lane_plan(rows, side, seg):
    lane = lax.broadcasted_iota(jnp.int32, (rows, 2 * HEAD_DIM), 1)
    mine = (lane < HEAD_DIM) if side == 0 else (lane >= HEAD_DIM)
    first = HEAD_DIM if side == 0 else 0
    hot = lane - first == seg
    slots = (lane >= first) & (lane < first + SLOTS)
    return lane, mine, hot, slots


def attend_kernel(ids_ref, seg_ref, q_ref, k_ref, v_ref, mixed_ref, log_ref, *, step, start):
    pair = pl.program_id(0) + start
    rows = q_ref.shape[0]
    seg = seg_ref[...]
    one = jnp.ones((), BF)
    logs = jnp.where(pair == start, 0.0, log_ref[...])
    outs = []
    for side in range(2):
        lane, mine, hot, slots = lane_plan(rows, side, seg)
        keys = jnp.where(
            mine, k_ref[...], jnp.where(slots & ~hot, FAR, 0.0).astype(BF)
        )
        values = jnp.where(mine, v_ref[...], one)
        queries = jnp.where(mine, q_ref[...] * BF(0.125), hot.astype(BF))
        parts, part_logs = [], []
        for at in range(0, rows, step):
            scores = lax.dot_general(
                queries[at : at + step],
                keys,
                (((1,), (1,)), ((), ())),
                preferred_element_type=F32,
            )
            top = jnp.max(scores, axis=1, keepdims=True) * LOG2E
            raised = jnp.exp2(scores * LOG2E - top).astype(BF)
            sums = jnp.dot(raised, values, preferred_element_type=F32)
            turned = pltpu.roll(sums, HEAD_DIM, 1)
            inside = mine[at : at + step]
            parts.append(sums / turned)
            part_logs.append(top + jnp.log2(jnp.where(inside, turned, sums)))
        outs.append(jnp.concatenate(parts, axis=0))
        logs = jnp.where(lane == 2 * pair + side, jnp.concatenate(part_logs, axis=0), logs)
    lane = lax.broadcasted_iota(jnp.int32, (rows, 2 * HEAD_DIM), 1)
    mixed_ref[...] = jnp.where(lane < HEAD_DIM, outs[0], outs[1]).astype(BF)
    log_ref[...] = logs


def attend(ids, qkv, seg, start, many, deps=()):
    rows = qkv.shape[0]
    wide = 2 * HEAD_DIM
    pairs = D // wide
    step = min(ATT_ROWS, rows)

    def block(first):
        return pl.BlockSpec((rows, wide), lambda pair, ids: (0, first + start + pair))

    return pl.pallas_call(
        functools.partial(attend_kernel, step=step, start=start),
        grid_spec=pltpu.PrefetchScalarGridSpec(
            num_scalar_prefetch=1,
            grid=(many,),
            in_specs=[full_spec((rows, 1)), block(0), block(pairs), block(2 * pairs)],
            out_specs=[
                pl.BlockSpec((rows, wide), lambda pair, ids: (0, pair)),
                full_spec((rows, wide)),
            ],
        ),
        out_shape=[
            jax.ShapeDtypeStruct((rows, many * wide), BF),
            jax.ShapeDtypeStruct((rows, wide), F32),
        ],
        compiler_params=params(),
        cost_estimate=cost(0),
        name="attend",
    )(tie(ids, *deps), seg, qkv, qkv, qkv)


def attend_back_kernel(
    ids_ref,
    seg_ref,
    q_ref,
    k_ref,
    v_ref,
    mixed_ref,
    grad_ref,
    log_ref,
    out_ref,
    *,
    step,
    start,
):
    pair = pl.program_id(0) + start
    rows = q_ref.shape[0]
    seg = seg_ref[...]
    zero = jnp.zeros((), BF)
    product = grad_ref[...].astype(F32) * mixed_ref[...].astype(F32)
    plain_keys = k_ref[...]
    values = v_ref[...]
    scaled = q_ref[...] * BF(0.125)
    results = []
    for side in range(2):
        lane, mine, hot, slots = lane_plan(rows, side, seg)
        keys = jnp.where(
            mine, plain_keys, jnp.where(slots & ~hot, FAR, 0.0).astype(BF)
        )
        queries = jnp.where(mine, scaled, hot.astype(BF))
        grads = jnp.where(mine, grad_ref[...], zero)
        queries_t = jnp.where(mine, scaled, zero).T
        grads_t = grads.T
        drop = jnp.sum(jnp.where(mine, product, 0.0), axis=1, keepdims=True)
        logs = jnp.sum(
            jnp.where(lane == 2 * pair + side, log_ref[...], 0.0), axis=1, keepdims=True
        )
        dq_parts, dk_t, dv_t = [], 0.0, 0.0
        for at in range(0, rows, step):
            part = slice(at, at + step)
            scores = lax.dot_general(
                queries[part],
                keys,
                (((1,), (1,)), ((), ())),
                preferred_element_type=F32,
            )
            probs = jnp.exp2(scores * LOG2E - logs[part])
            grad_probs = lax.dot_general(
                grads[part],
                values,
                (((1,), (1,)), ((), ())),
                preferred_element_type=F32,
            )
            grad_scores = (probs * (grad_probs - drop[part])).astype(BF)
            probs = probs.astype(BF)
            dq_parts.append(jnp.dot(grad_scores, plain_keys, preferred_element_type=F32))
            dv_t = dv_t + jnp.dot(grads_t[:, part], probs, preferred_element_type=F32)
            dk_t = dk_t + jnp.dot(
                queries_t[:, part], grad_scores, preferred_element_type=F32
            )
        results.append((jnp.concatenate(dq_parts, axis=0) * 0.125, dk_t.T, dv_t.T))
    lane = lax.broadcasted_iota(jnp.int32, (rows, 2 * HEAD_DIM), 1)
    for kind, (low, high) in enumerate(zip(results[0], results[1])):
        out_ref[kind] = jnp.where(lane < HEAD_DIM, low, high).astype(BF)


def attend_back(ids, qkv, seg, mixed, grad_mixed, logs, start, many, deps=()):
    rows = qkv.shape[0]
    wide = 2 * HEAD_DIM
    pairs = D // wide
    step = min(ATT_ROWS, rows)

    def block(first):
        return pl.BlockSpec((rows, wide), lambda pair, ids: (0, first + start + pair))

    kernel = functools.partial(attend_back_kernel, step=step, start=start)
    return pl.pallas_call(
        kernel,
        grid_spec=pltpu.PrefetchScalarGridSpec(
            num_scalar_prefetch=1,
            grid=(many,),
            in_specs=[
                full_spec((rows, 1)),
                block(0),
                block(pairs),
                block(2 * pairs),
                block(0),
                block(0),
                full_spec((rows, wide)),
            ],
            out_specs=pl.BlockSpec((3, rows, wide), lambda pair, ids: (0, 0, pair)),
        ),
        out_shape=jax.ShapeDtypeStruct((3, rows, many * wide), BF),
        compiler_params=params(),
        cost_estimate=cost(0),
        name="attend_back",
    )(tie(ids, *deps), seg, qkv, qkv, qkv, mixed, grad_mixed, logs)


def up_kernel(
    ids_ref, mixed_ref, state_ref, vectors_ref, bias_ref, *refs, offsets, arrays, columns
):
    pieces = refs[:arrays]
    one_ref, normed_ref, hidden_ref, slope_ref, proj, up, sems = refs[arrays:]

    @pl.when(pl.program_id(0) == 0)
    def _():
        copies = fetch_halves(ids_ref, pieces, offsets, (proj, up), sems)
        begin(copies)
        finish(copies)

    vectors = vectors_ref[...]
    state = state_ref[...] + dot_nn(mixed_ref[...], proj[...]) + vectors[3:4]
    one_ref[...] = state
    unit, _ = norm_parts(state)
    normed = (unit * vectors[4:5] + vectors[5:6]).astype(BF)
    normed_ref[...] = normed
    for at in range(0, FF, columns):
        part = slice(at, at + columns)
        before = dot_nn(normed, up[:, part]) + bias_ref[:, part]
        share = 0.5 + 0.5 * lax.erf(before * math.sqrt(0.5))
        bell = jnp.exp2(before * before * (-0.5 * LOG2E)) * (1.0 / math.sqrt(2.0 * math.pi))
        hidden_ref[:, part] = (before * share).astype(BF)
        slope_ref[:, part] = (share + before * bell).astype(BF)


def feed_up(ids, mixed, state, vectors, bias, weight, deps=()):
    arrays, offsets = weight
    count = mixed.shape[0]
    total = halves_count(weight)
    return pl.pallas_call(
        functools.partial(up_kernel, offsets=offsets, arrays=len(arrays), columns=512),
        grid_spec=pltpu.PrefetchScalarGridSpec(
            num_scalar_prefetch=1,
            grid=(count // ROWS,),
            in_specs=[
                row_spec(D),
                row_spec(D),
                full_spec(vectors.shape),
                full_spec(bias.shape),
            ]
            + anys(len(arrays)),
            out_specs=[row_spec(D), row_spec(D), row_spec(FF), row_spec(FF)],
            scratch_shapes=[
                pltpu.VMEM((D, D), BF),
                pltpu.VMEM((D, FF), BF),
                pltpu.SemaphoreType.DMA((total,)),
            ],
        ),
        out_shape=[
            jax.ShapeDtypeStruct((count, D), F32),
            jax.ShapeDtypeStruct((count, D), BF),
            jax.ShapeDtypeStruct((count, FF), BF),
            jax.ShapeDtypeStruct((count, FF), BF),
        ],
        compiler_params=params(),
        cost_estimate=cost(0),
        name="feed_up",
    )(tie(ids, *deps), mixed, state, vectors, bias, *arrays)


def down_kernel(
    ids_ref,
    hidden_ref,
    slope_ref,
    state_ref,
    cotangent_ref,
    rows_ref,
    vectors_ref,
    *refs,
    offsets,
    arrays,
    columns,
):
    pieces = refs[:arrays]
    out_ref, branch_ref, before_ref, sums_ref, weight, sems = refs[arrays:]

    @pl.when(pl.program_id(0) == 0)
    def _():
        copies = fetch(ids_ref, pieces, offsets, weight, sems)
        begin(copies)
        sums_ref[...] = jnp.zeros_like(sums_ref)
        finish(copies)

    alive = rows_ref[:, 1:2]
    state = state_ref[...] + dot_nn(hidden_ref[...], weight[...]) + vectors_ref[6:7]
    out_ref[...] = (state * alive).astype(BF)
    grad = cotangent_ref[...].astype(F32) * alive
    branch = grad.astype(BF)
    branch_ref[...] = branch
    sums_ref[0:1, :D] += column_sum(grad)
    for at in range(0, FF, columns):
        part = slice(at, at + columns)
        before = dot_nt(branch, weight[part]) * slope_ref[:, part].astype(F32)
        before = before.astype(BF)
        before_ref[:, part] = before
        sums_ref[1:2, part] += column_sum(before.astype(F32))


def feed_down(ids, hidden, slope, state, cotangent, rows, vectors, weight, deps=()):
    arrays, offsets = weight
    count = hidden.shape[0]
    return pl.pallas_call(
        functools.partial(down_kernel, offsets=offsets, arrays=len(arrays), columns=768),
        grid_spec=pltpu.PrefetchScalarGridSpec(
            num_scalar_prefetch=1,
            grid=(count // ROWS,),
            in_specs=[
                row_spec(FF),
                row_spec(FF),
                row_spec(D),
                row_spec(D),
                row_spec(8),
                full_spec(vectors.shape),
            ]
            + anys(len(arrays)),
            out_specs=[row_spec(D), row_spec(D), row_spec(FF), full_spec((8, FF))],
            scratch_shapes=[
                pltpu.VMEM((FF, D), BF),
                pltpu.SemaphoreType.DMA((piece_count(weight),)),
            ],
        ),
        out_shape=[
            jax.ShapeDtypeStruct((count, D), BF),
            jax.ShapeDtypeStruct((count, D), BF),
            jax.ShapeDtypeStruct((count, FF), BF),
            jax.ShapeDtypeStruct((8, FF), F32),
        ],
        compiler_params=params(),
        cost_estimate=cost(0),
        name="feed_down",
    )(tie(ids, *deps), hidden, slope, state, cotangent, rows, vectors, *arrays)


def middle_kernel(
    ids_ref, before_ref, state_ref, branch_ref, vectors_ref, *refs, offsets, arrays
):
    pieces = refs[:arrays]
    grad_ref, attn_ref, mixed_ref, sums_ref, proj, up, sems = refs[arrays:]

    @pl.when(pl.program_id(0) == 0)
    def _():
        copies = fetch_halves(ids_ref, pieces, offsets, (proj, up), sems)
        begin(copies)
        sums_ref[...] = jnp.zeros_like(sums_ref)
        finish(copies)

    vectors = vectors_ref[...]
    normed = dot_nt(before_ref[...], up[...])
    unit, scale = norm_parts(state_ref[...])
    grad = branch_ref[...].astype(F32) + norm_back(normed, vectors[4:5], unit, scale)
    grad_ref[...] = grad
    attn = grad.astype(BF)
    attn_ref[...] = attn
    mixed_ref[...] = dot_nt(attn, proj[...]).astype(BF)
    sums_ref[0:1] += column_sum(grad)
    sums_ref[1:2] += column_sum(normed * unit)
    sums_ref[2:3] += column_sum(normed)


def middle_back(ids, before, state, branch, vectors, weight, deps=()):
    arrays, offsets = weight
    count = before.shape[0]
    total = halves_count(weight)
    return pl.pallas_call(
        functools.partial(middle_kernel, offsets=offsets, arrays=len(arrays)),
        grid_spec=pltpu.PrefetchScalarGridSpec(
            num_scalar_prefetch=1,
            grid=(count // ROWS,),
            in_specs=[row_spec(FF), row_spec(D), row_spec(D), full_spec(vectors.shape)]
            + anys(len(arrays)),
            out_specs=[row_spec(D), row_spec(D), row_spec(D), full_spec((8, D))],
            scratch_shapes=[
                pltpu.VMEM((D, D), BF),
                pltpu.VMEM((D, FF), BF),
                pltpu.SemaphoreType.DMA((total,)),
            ],
        ),
        out_shape=[
            jax.ShapeDtypeStruct((count, D), F32),
            jax.ShapeDtypeStruct((count, D), BF),
            jax.ShapeDtypeStruct((count, D), BF),
            jax.ShapeDtypeStruct((8, D), F32),
        ],
        compiler_params=params(52 * 2**20),
        cost_estimate=cost(0),
        name="middle_back",
    )(tie(ids, *deps), before, state, branch, vectors, *arrays)


def place_pieces(ids_ref, values, kept_ref, sent_ref, shards, rows, first, lead=0):
    count = values.shape[0] // rows
    flat = len(kept_ref.shape) == 2
    if sent_ref is None:
        if flat:
            kept_ref[lead:] = values
        else:
            kept_ref[pl.ds(first, count)] = values.reshape((count, rows) + values.shape[1:])
        return
    me = ids_ref[0]
    for index in range(count):
        apart = jnp.bitwise_xor(me, first + index)
        spot = 0
        for bit in range(1, bits_of(shards)):
            spot = spot * 2 + jnp.bitwise_and(lax.shift_right_logical(apart, bit), 1)
        piece = values[index * rows : (index + 1) * rows]
        same = jnp.bitwise_and(apart, 1) == 0

        def put(ref, piece=piece, spot=spot):
            if flat:
                ref[pl.ds(pl.multiple_of(lead + spot * rows, 16), rows)] = piece
            else:
                ref[spot] = piece

        pl.when(same)(functools.partial(put, kept_ref))
        pl.when(jnp.logical_not(same))(functools.partial(put, sent_ref))


def weight_kernel(ids_ref, left_ref, right_ref, *refs, shards, rows, first_step, extra):
    out_refs = refs[2 * extra :]
    sent_ref = out_refs[1] if len(out_refs) > 1 else None
    step = pl.program_id(0)

    def put(left_ref, right_ref):
        right = right_ref[0] if len(right_ref.shape) == 3 else right_ref[...]
        values = dot_tn(left_ref[...], right).astype(BF)
        place_pieces(
            ids_ref, values, out_refs[0], sent_ref, shards, rows, step * first_step
        )

    if extra:
        last = pl.num_programs(0) - extra * (refs[1].shape[1] // right_ref.shape[2])
        pl.when(step < last)(lambda: put(left_ref, right_ref))

        @pl.when(step >= last)
        def _():
            wide = right_ref.shape[2]
            for index in range(refs[1].shape[1] // wide):
                part = pl.ds(index * wide, wide)

                @pl.when(step == last + index)
                def _(part=part):
                    put(refs[0], refs[1].at[:, part])

    else:
        put(left_ref, right_ref)


def weight_grad(ids, left, right, shards, split, name, deps=(), extra=()):
    count, tall = left.shape
    stacked = right.ndim == 3
    wide = right.shape[-1]
    step = wide if stacked else min(768, max(tall, wide))
    narrow = tall > wide and not stacked
    rows = tall // shards
    outs = 2 if split else 1
    pieces = shards // outs
    more_specs = []
    if narrow:
        grid, first_step, out_wide = tall // step, step // rows, wide
        specs = [
            pl.BlockSpec((count, step), lambda i, ids: (0, i)),
            pl.BlockSpec((count, wide), lambda i, ids: (0, 0)),
        ]
        out_spec = pl.BlockSpec((pieces, rows, wide), lambda i, ids: (0, 0, 0))
    else:
        first_step = 0
        if stacked:
            kinds = right.shape[0]
            grid, out_wide = kinds, kinds * wide
            if extra:
                grid, out_wide = grid + extra[1].shape[1] // wide, out_wide + extra[1].shape[1]
                more_specs = [full_spec(value.shape) for value in extra]
            right_spec = pl.BlockSpec(
                (1, count, step), lambda i, ids: (jnp.minimum(i, kinds - 1), 0, 0)
            )
        else:
            grid, out_wide = wide // step, wide
            right_spec = pl.BlockSpec((count, step), lambda i, ids: (0, i))
        specs = [pl.BlockSpec((count, tall), lambda i, ids: (0, 0)), right_spec]
        out_spec = pl.BlockSpec((pieces, rows, step), lambda i, ids: (0, 0, i))
    kernel = functools.partial(
        weight_kernel,
        shards=shards,
        rows=rows,
        first_step=first_step,
        extra=1 if extra else 0,
    )
    return pl.pallas_call(
        kernel,
        grid_spec=pltpu.PrefetchScalarGridSpec(
            num_scalar_prefetch=1,
            grid=(grid,),
            in_specs=specs + more_specs,
            out_specs=[out_spec] * outs,
        ),
        out_shape=[jax.ShapeDtypeStruct((pieces, rows, out_wide), BF)] * outs,
        compiler_params=params(),
        cost_estimate=cost(0),
        name=name,
    )(tie(ids, *deps), left, right, *extra)


def embed_kernel(
    ids_ref,
    state_ref,
    grad_ref,
    vectors_ref,
    down_sums_ref,
    middle_sums_ref,
    *refs,
    offsets,
    arrays,
    chunks,
):
    grad_refs = refs[:chunks]
    pieces = refs[chunks : chunks + arrays]
    patch_ref, small_ref, weight, sums, sems = refs[chunks + arrays :]
    step = pl.program_id(0)

    @pl.when(step == 0)
    def _():
        copies = fetch(ids_ref, pieces, offsets, weight, sems)
        begin(copies)
        sums[...] = jnp.zeros_like(sums)
        finish(copies)

    normed = 0.0
    at = 0
    for ref in grad_refs:
        wide = ref.shape[2]
        for kind in range(3):
            first = kind * D + at
            normed = normed + dot_nt(ref[kind], weight[:, first : first + wide])
        at += wide
    unit, scale = norm_parts(state_ref[...])
    grad = grad_ref[...] + norm_back(normed, vectors_ref[1:2], unit, scale)
    patch_ref[...] = grad.astype(BF)
    sums[0:1] += column_sum(grad)
    sums[1:2] += column_sum(normed * unit)
    sums[2:3] += column_sum(normed)

    @pl.when(step == pl.num_programs(0) - 1)
    def _():
        small = [sums[0:3], middle_sums_ref[0:3], down_sums_ref[0:1, :D]]
        small += [
            down_sums_ref[1:2, index * D : (index + 1) * D] for index in range(FF // D)
        ]
        small += [jnp.zeros((SMALL_PAD - SMALL, D), F32)]
        small_ref[:, :D] = jnp.concatenate(small, axis=0).astype(BF)
        small_ref[:, D:] = jnp.zeros((SMALL_PAD, PIXALL - D), BF)


def embed_back(
    ids, grads, state, grad, vectors, down_sums, middle_sums, weight, deps=()
):
    arrays, offsets = weight
    count = state.shape[0]
    kernel = functools.partial(
        embed_kernel, offsets=offsets, arrays=len(arrays), chunks=len(grads)
    )
    return pl.pallas_call(
        kernel,
        grid_spec=pltpu.PrefetchScalarGridSpec(
            num_scalar_prefetch=1,
            grid=(count // ROWS,),
            in_specs=[
                row_spec(D),
                row_spec(D),
                full_spec(vectors.shape),
                full_spec(down_sums.shape),
                full_spec(middle_sums.shape),
            ]
            + [
                pl.BlockSpec((3, ROWS, part.shape[2]), lambda i, ids: (0, i, 0))
                for part in grads
            ]
            + anys(len(arrays)),
            out_specs=[row_spec(D), full_spec((SMALL_PAD, PIXALL))],
            scratch_shapes=[
                pltpu.VMEM((D, 3 * D), BF),
                pltpu.VMEM((8, D), F32),
                pltpu.SemaphoreType.DMA((piece_count(weight),)),
            ],
        ),
        out_shape=[
            jax.ShapeDtypeStruct((count, D), BF),
            jax.ShapeDtypeStruct((SMALL_PAD, PIXALL), BF),
        ],
        compiler_params=params(),
        cost_estimate=cost(0),
        name="embed_back",
    )(tie(ids, *deps), state, grad, vectors, down_sums, middle_sums, *grads, *arrays)


def patch_back_kernel(ids_ref, patch_ref, pixels_ref, rows_ref, small_ref, *out_refs, shards):
    sent_ref = out_refs[1] if len(out_refs) > 1 else None
    spread = spread_pixels(pixels_ref[...], rows_ref[:, 2:3])
    values = dot_tn(patch_ref[...], spread).astype(BF)
    place_pieces(
        ids_ref, values, out_refs[0], sent_ref, shards, D // shards, 0, SMALL_PAD
    )
    for ref in out_refs:
        ref[:SMALL_PAD] = small_ref[...]


def patch_back(ids, patch_grad, pixels, rows, small, shards, split, deps=()):
    count = pixels.shape[0]
    outs = 2 if split else 1
    held = (SMALL_PAD + D // outs, PIXALL)
    return pl.pallas_call(
        functools.partial(patch_back_kernel, shards=shards),
        grid_spec=pltpu.PrefetchScalarGridSpec(
            num_scalar_prefetch=1,
            grid=(1,),
            in_specs=[
                full_spec((count, D)),
                full_spec((count, PIXC)),
                full_spec(rows.shape),
                full_spec(small.shape),
            ],
            out_specs=[full_spec(held)] * outs,
        ),
        out_shape=[jax.ShapeDtypeStruct(held, BF)] * outs,
        compiler_params=params(),
        cost_estimate=cost(0),
        name="patch_back",
    )(tie(ids, *deps), patch_grad, pixels, rows, small)


def pixel_kernel(ids_ref, patch_ref, rows_ref, weight_ref, out_ref):
    fine = rows_ref[:, 2:3]
    both = dot_nt(patch_ref[...], weight_ref[...])
    wide = PIXALL - PIXC
    rough = both[:, :PIXC] * (1.0 - fine)
    first = rough[:, :wide] + both[:, PIXC:] * fine
    out_ref[...] = jnp.concatenate([first, rough[:, wide:]], axis=1).astype(BF)


def pixel_back(ids, patch_grad, rows, weight, deps=()):
    count = patch_grad.shape[0]
    return pl.pallas_call(
        pixel_kernel,
        grid_spec=pltpu.PrefetchScalarGridSpec(
            num_scalar_prefetch=1,
            grid=(count // ROWS,),
            in_specs=[row_spec(D), row_spec(8), full_spec(weight.shape)],
            out_specs=row_spec(PIXC),
        ),
        out_shape=jax.ShapeDtypeStruct((count, PIXC), BF),
        compiler_params=params(),
        cost_estimate=cost(4),
        name="pixel_back",
    )(tie(ids, *deps), patch_grad, rows, weight)


def base_kernel(ids_ref, turned_ref, coarse_ref, fine_ref, out_ref, square_ref):
    turned = turned_ref[...]
    grad = dot_nn(turned[:, :PIXC], coarse_ref[...])
    grad = grad + dot_nn(turned[:, PIXC : PIXC + PIXF], fine_ref[...])

    @pl.when(pl.program_id(0) == 0)
    def _():
        square_ref[...] = jnp.zeros_like(square_ref)

    square_ref[...] += jnp.sum(grad * grad, axis=0, keepdims=True)
    low = grad.astype(BF)
    rows = out_ref.shape[2]
    for index in range(out_ref.shape[0]):
        out_ref[index] = low[:, index * rows : (index + 1) * rows]


def base_back(ids, turned, coarse, fine, shards, deps=()):
    count, wide = turned.shape[0], coarse.shape[1]
    step = 768
    rows = wide // shards
    return pl.pallas_call(
        base_kernel,
        grid_spec=pltpu.PrefetchScalarGridSpec(
            num_scalar_prefetch=1,
            grid=(wide // step,),
            in_specs=[
                full_spec(turned.shape),
                pl.BlockSpec((PIXC, step), lambda i, ids: (0, i)),
                pl.BlockSpec((PIXF, step), lambda i, ids: (0, i)),
            ],
            out_specs=[
                pl.BlockSpec((step // rows, count, rows), lambda i, ids: (i, 0, 0)),
                full_spec((1, step)),
            ],
        ),
        out_shape=[
            jax.ShapeDtypeStruct((shards, count, rows), BF),
            jax.ShapeDtypeStruct((1, step), F32),
        ],
        compiler_params=params(),
        cost_estimate=cost(0),
        name="base_back",
    )(tie(ids, *deps), turned, coarse, fine)


def bits_of(count):
    bits = count.bit_length() - 1
    assert count == 1 << bits
    return bits


def swap(value, axis, count, mask):
    return lax.ppermute(value, axis, [(i, i ^ mask) for i in range(count)])


def add_low(left, right):
    return (left.astype(F32) + right.astype(F32)).astype(BF)


class Gather:
    def __init__(self, shard, count):
        self.held, self.places, self.count = shard[None], [0], count
        self.bits = list(reversed(range(2, bits_of(count))))
        self.other = None

    def land(self, *after):
        if self.other is not None:
            self.held = jnp.concatenate([self.held, tie(self.other, *after)])
            self.other = None
        return self.held

    def step(self, *after):
        bit = self.bits.pop(0)
        held = tie(self.land(*after), *after)
        self.other = swap(held, "fsdp", self.count, 1 << bit)
        self.places = self.places + [place ^ (1 << bit) for place in self.places]
        return self.other

    def high(self, *after):
        held = tie(self.held, *after)
        masks = [0]
        while self.bits:
            masks = masks + [mask ^ (1 << self.bits[0]) for mask in masks]
            self.bits.pop(0)
        self.rest = [swap(held, "fsdp", self.count, mask) for mask in masks[1:]]
        self.places = masks
        return self.rest

    def join(self, *after):
        self.held = jnp.concatenate([self.held] + [tie(part, *after) for part in self.rest])

    def far(self, *after):
        held = tie(self.land(*after), *after)
        self.other = swap(held, "fsdp", self.count, 2)
        self.held_core = swap(held, "fsdp", self.count, 1)
        return self.other

    def far_halves(self, there, *after):
        held = tie(self.land(*after), *after)
        half = held.shape[2] // 2
        sent = lax.dynamic_slice_in_dim(held, there * half, half, axis=2)
        self.mine = swap(sent, "fsdp", self.count, 2)
        self.held_core = swap(held, "fsdp", self.count, 1)
        return self.mine

    def near_halves(self, *after):
        mine = tie(self.mine, *after)
        rest = swap(mine, "rep", 2, 1)
        mine_core = swap(mine, "fsdp", self.count, 1)
        rest_core = swap(rest, "fsdp", self.count, 1)
        arrays = (self.held, self.held_core, self.mine, mine_core, rest, rest_core)
        offsets = [tuple(p ^ mask for p in self.places) for mask in (0, 1)]
        offsets += [
            tuple((p ^ mask, side) for p in self.places) for side in (0, 1) for mask in (2, 3)
        ]
        return (arrays, tuple(offsets)), rest

    def near(self, *after):
        other_core = swap(tie(self.other, *after), "fsdp", self.count, 1)
        offsets = tuple(tuple(p ^ mask for p in self.places) for mask in (0, 1, 2, 3))
        return (self.held, self.held_core, self.other, other_core), offsets


def halves_of(value, side):
    wide = value.shape[1] // 2
    return value[:, side * wide : (side + 1) * wide]


def gather_whole(shard, count):
    here = lax.axis_index("fsdp")
    held = shard[None]
    for bit in reversed(range(bits_of(count))):
        other = swap(held, "fsdp", count, 1 << bit)
        upper = (here >> bit) & 1 == 1
        both = jnp.where(
            upper, jnp.stack([other, held], axis=1), jnp.stack([held, other], axis=1)
        )
        held = both.reshape((-1,) + shard.shape)
    return held.reshape((-1,) + shard.shape[1:])


def as_piece(whole):
    return (whole[None],), ((None,),)


def scatter_whole(blocks, count):
    here = lax.axis_index("fsdp")
    held = blocks
    for bit in range(bits_of(count)):
        side = (here >> bit) & 1
        halves = held.reshape((held.shape[0] // 2, 2) + held.shape[1:])
        sent = lax.dynamic_index_in_dim(halves, 1 - side, axis=1, keepdims=False)
        kept = lax.dynamic_index_in_dim(halves, side, axis=1, keepdims=False)
        held = add_low(kept, swap(sent, "fsdp", count, 1 << bit))
    return held[0]


class Scatter:
    def __init__(self, parts, shards, reps, plan, lead=0):
        self.kept, self.ready = parts
        self.shards, self.reps, self.lead = shards, reps, lead
        self.plan = plan
        self.at = 0

    def step(self, *after):
        kind = self.plan[self.at]
        value = tie(self.ready, *after)
        if isinstance(kind, int):
            self.other = swap(value, "fsdp", self.shards, 1 << kind)
        else:
            self.other = swap(value, "rep", self.reps, 1)
        self.at += 1

    def land(self, *after):
        kept, other = self.kept, tie(self.other, *after)
        following = self.plan[self.at] if self.at < len(self.plan) else None
        there = lax.axis_index("rep")
        if following == "half":
            wide = kept.shape[-1] // 2

            def columns(side):
                return add_low(
                    lax.dynamic_slice_in_dim(kept, side * wide, wide, axis=2),
                    lax.dynamic_slice_in_dim(other, side * wide, wide, axis=2),
                )

            self.kept, self.ready = columns(there), columns(1 - there)
        elif isinstance(following, int):
            half = (kept.shape[0] - self.lead) // 2 + self.lead
            low, high = add_low(kept[:half], other[:half]), add_low(kept[half:], other[half:])
            self.kept, self.ready = low, high
            if self.lead:
                self.ready = jnp.concatenate([low[: self.lead], high])
        else:
            self.kept = self.ready = add_low(kept, other)
        return self.ready


def merged(parts, more, shards, reps, plan):
    kept = jnp.concatenate([part.kept for part in (parts, more)], axis=2)
    ready = jnp.concatenate([part.ready for part in (parts, more)], axis=2)
    return Scatter((kept, ready), shards, reps, plan)


def rows_of(value):
    return [value[:, at : at + D] for at in range(0, value.shape[1], D)]


def replicas(value, count):
    for bit in range(bits_of(count)):
        value = add_low(value, swap(value, "rep", count, 1 << bit))
    return value


def total_of(value, count):
    for bit in range(bits_of(count)):
        value = value + swap(value, "fsdp", count, 1 << bit)
    return value


def body(
    shards,
    reps,
    pixels,
    image_tokens,
    patch_class,
    resize_coarse,
    resize_fine,
    w_base,
    w_qkv,
    w_proj,
    w_fc1,
    w_fc2,
    small_params,
    first_base,
    first_qkv,
    first_proj,
    first_fc1,
    first_fc2,
    first_small,
    second_base,
    second_qkv,
    second_proj,
    second_fc1,
    second_fc2,
    second_small,
    cotangent,
):
    rows_here = pixels.shape[0]
    here = lax.axis_index("fsdp")
    there = lax.axis_index("rep")
    ids = jnp.stack([here, there]).astype(jnp.int32)
    base_rows = w_base.shape[0]
    pieced = shards == 16 and reps == 2 and w_qkv.shape[0] % 16 == 0

    segment, alive, finer = rows_plan(image_tokens[0], patch_class[0], rows_here)
    segment_col = segment[:, None]
    nothing = jnp.zeros_like(alive)
    rows = jnp.stack([nothing, alive, finer] + [nothing] * 5, axis=1)

    low_qkv = w_qkv.astype(BF)
    low_both = jnp.concatenate(
        [part for side in (0, 1) for part in (halves_of(w_proj, side), halves_of(w_fc1, side))],
        axis=1,
    ).astype(BF)
    low_fc2 = w_fc2.astype(BF)
    small_cols = small_params.shape[1]
    if pieced:
        half_cols = D // 2
        lanes = jnp.arange(D, dtype=jnp.int32)[None, :] // small_cols
        placed = jnp.where(lanes == here, jnp.tile(small_params, (1, shards)), 0.0)
        placed = jnp.pad(placed, ((0, SMALL_PAD - SMALL), (0, 0))).astype(BF)
        mine = lax.dynamic_slice_in_dim(w_base, there * half_cols, half_cols, axis=1)
        message = jnp.concatenate(
            [mine.astype(BF), placed[:, :half_cols], placed[:, half_cols:]], axis=0
        )
        gather_base = Gather(message, shards)
        gather_base.step()
        base_done = gather_base.step()
        held, places = gather_base.land(), gather_base.places
        other = swap(held, "fsdp", shards, 1)
        offsets = (tuple(places), tuple(place ^ 1 for place in places))
        part = resize_part(ids, resize_coarse, resize_fine, (held, other), offsets, base_rows)
        gather_qkv = Gather(low_qkv, shards)
        gather_qkv.step(base_done)
        qkv_done = gather_qkv.step(part)
        part = add_low(part, swap(part, "fsdp", shards, 2))
        half_rows = PIXALL // 2
        quarter = part[:half_rows][None]
        small_low = part[half_rows:]
        vectors = jnp.concatenate([small_low[:SMALL_PAD], small_low[SMALL_PAD:]], axis=1)
        quarter_rep = swap(quarter, "rep", reps, 1)
        quarter_core = swap(quarter, "fsdp", shards, 1)
        quarter_both = swap(quarter_rep, "fsdp", shards, 1)
        patch_arrays = (quarter, quarter_core, quarter_rep, quarter_both)
        patch_places = (((0, 0),), ((1, 0),), ((0, 1),), ((1, 1),))
        gather_qkv.far(quarter)
        gather_both = Gather(low_both, shards)
        gather_both.step(qkv_done, quarter)
    else:
        base = gather_whole(w_base.astype(BF), shards)
        coarse = dot_nn(resize_coarse, base).astype(BF)
        fine = dot_nn(resize_fine, base).astype(BF)
        whole = jnp.concatenate([coarse, fine, jnp.zeros((PIXALL - PIXC - PIXF, D), BF)])
        patch_arrays = (whole[None],)
        patch_places = ((None,),)
        vectors = gather_whole(small_params.astype(BF).T, shards).T
        vectors = jnp.pad(vectors, ((0, SMALL_PAD - SMALL), (0, 0)))
        weight_qkv = as_piece(gather_whole(low_qkv, shards))
        weight_both = as_piece(gather_whole(low_both, shards))
        weight_fc2 = as_piece(gather_whole(low_fc2, shards))
    vectors = vectors.astype(F32)
    bias = vectors[7:11].reshape(1, FF)

    state_zero, normed_one, patch_weight = patch(
        ids, pixels, rows, vectors, patch_arrays, patch_places
    )
    if pieced:
        weight_qkv = gather_qkv.near(state_zero)
        both_done = gather_both.step(state_zero)
    qkv = project_qkv(ids, normed_one, weight_qkv)
    chunks = 3
    pairs = HEADS // 2
    many = pairs // chunks
    if pieced:
        gather_fc2 = Gather(low_fc2, shards)
        gather_fc2.high(qkv)
    outs = [attend(ids, qkv, segment_col, 0, many)]
    after = ()
    if pieced:
        both_held = gather_both.land(outs[0][0])
        both_mine = gather_both.far_halves(there, both_held)
        after = (both_held,)
    for index in range(1, chunks):
        outs.append(attend(ids, qkv, segment_col, index * many, many, after))
        after = (outs[-1][0],)
    if pieced:
        weight_both, both_rest = gather_both.near_halves(outs[-1][0])
        gather_fc2.join(both_mine, outs[-1][0])
        gather_fc2.far()
    mixed = jnp.concatenate([out[0] for out in outs], axis=1)
    logs = [out[1] for out in outs]
    state_one, normed_two, hidden, slope = feed_up(
        ids, mixed, state_zero, vectors, bias, weight_both
    )
    if pieced:
        weight_fc2 = gather_fc2.near(state_one)
    activations, branch, grad_before, down_sums = feed_down(
        ids, hidden, slope, state_one, cotangent, rows, vectors, weight_fc2
    )

    def qkv_chunk(index, *after):
        many = pairs // chunks
        return attend_back(
            ids, qkv, segment_col, mixed, grad_mixed, logs[index], index * many, many, after
        )

    def chunk_grad(part, *after, extra=()):
        return weight_grad(
            ids, normed_one, part, shards, pieced, "grad_qkv", after, extra
        )

    def finish_embed(grads, *after):
        return embed_back(
            ids,
            grads,
            state_zero,
            grad_one,
            vectors,
            down_sums,
            middle_sums,
            weight_qkv,
            after,
        )

    part_fc2 = weight_grad(ids, hidden, branch, shards, pieced, "grad_fc2")
    if pieced:
        every = list(range(bits_of(shards)))
        near, far = every[:2], every[2:]
        sum_fc2 = Scatter(part_fc2, shards, reps, every)
        sum_fc2.step()
        part_fc1 = weight_grad(
            ids, normed_two, grad_before, shards, pieced, "grad_fc1", part_fc2
        )
        sum_fc1 = Scatter(part_fc1, shards, reps, [0, "half"] + every[1:])
        sum_fc2.land(part_fc1[0])
        sum_fc2.step()
        sum_fc1.step()
        grad_one, grad_attn, grad_mixed, middle_sums = middle_back(
            ids,
            grad_before,
            state_one,
            branch,
            vectors,
            weight_both,
            (sum_fc2.ready, part_fc1[0]),
        )
        sum_fc1.land(grad_one)
        sum_fc1.step()
        first = qkv_chunk(0, sum_fc1.ready)
        part_first = chunk_grad(first, extra=(mixed, grad_attn))
        sum_first = Scatter(part_first, shards, reps, [0, "half"] + every[1:])
        sum_fc2.land(part_first[0])
        sum_fc2.step()
        sum_first.step()
        second = qkv_chunk(1, sum_fc2.ready, part_first[0])
        sum_first.land(second)
        sum_first.step()
        sum_fc1.land(second)
        sum_fc1.step(sum_first.ready)
        part_second = chunk_grad(second, sum_first.ready, sum_fc1.ready)
        sum_second = Scatter(part_second, shards, reps, every)
        sum_fc2.land(part_second[0])
        sum_fc2.step()
        sum_second.step()
        third = qkv_chunk(2, sum_fc2.ready, part_second[0])
        sum_first.land(third)
        sum_first.step()
        sum_second.land(third)
        sum_second.step(sum_first.ready)
        part_third = chunk_grad(third, sum_second.ready, sum_first.ready)
        sum_third = Scatter(part_third, shards, reps, every)
        sum_third.step()
        sum_fc1.land(part_third[0])
        sum_fc1.step()
        patch_grad, small_part = finish_embed(
            (first, second, third), part_third[0], sum_fc1.ready
        )
        sum_third.land(patch_grad)
        sum_third.step()
        sum_first.land(patch_grad)
        sum_second.land(patch_grad)
        sum_both = merged(sum_first, sum_second, shards, reps, far)
        sum_both.step(sum_third.ready)
        patch_parts = patch_back(
            ids,
            patch_grad,
            pixels,
            rows,
            small_part,
            shards,
            pieced,
            (sum_third.ready, sum_both.ready),
        )
        sum_patch = Scatter(patch_parts, shards, reps, every, SMALL_PAD)
        sum_patch.step()
        sum_fc1.land(patch_parts[0])
        sum_fc1.step()
        sum_fc2.land(patch_parts[0])
        fc2_other = swap(sum_fc2.kept, "rep", reps, 1)
        sum_patch.land(sum_fc1.ready, sum_fc2.kept)
        sum_patch.step()
        mark = sum_patch.ready
        pixel_grad = pixel_back(ids, patch_grad, rows, patch_weight, (mark,))
        sum_third.land(pixel_grad)
        sum_third.step()
        sum_both.land(sum_third.ready)
        sum_both.step()
        sum_patch.land(sum_both.ready)
        sum_patch.step()
        mark = sum_patch.ready
        sum_fc1.land(mark)
        sum_third.land(mark)
        sum_third.step()
        sum_patch.land(sum_third.ready, sum_fc1.ready)
        sum_patch.step()
        mark = sum_patch.ready
        sum_both.land(mark)
        ends = jnp.concatenate([*rows_of(sum_fc1.kept[0]), *rows_of(sum_both.kept[0])])
        ends_other = swap(ends, "rep", reps, 1)
        sum_third.land(ends)
        grad_fc2 = add_low(sum_fc2.kept[0], tie(fc2_other, ends)[0])
        sum_patch.land(sum_third.kept)
        tail = jnp.pad(sum_third.kept[0], ((0, 0), (0, PIXALL - D)))
        tail = jnp.concatenate([sum_patch.kept, tail])
        tail = add_low(tail, swap(tail, "rep", reps, 1))
        few = w_qkv.shape[0]
        parts = [ends[at * few :][:few] for at in range(4)]
        others = [ends_other[at * few :][:few] for at in range(4)]
        low = [jnp.where(there == 0, a, b) for a, b in zip(parts, others)]
        high = [jnp.where(there == 0, b, a) for a, b in zip(parts, others)]
        grad_fc1 = jnp.concatenate(low[:2] + high[:2], axis=1)
        grad_first, grad_proj = low[2], high[2]
        grad_second = add_low(parts[3], others[3])
        split_at = SMALL_PAD + D // shards
        turned, grad_third = tail[:split_at], tail[split_at:, :D]
    else:

        def owned(parts):
            return replicas(scatter_whole(parts[0], shards), reps)

        grad_fc2 = owned(part_fc2)
        grad_fc1 = owned(
            weight_grad(ids, normed_two, grad_before, shards, pieced, "grad_fc1")
        )
        grad_one, grad_attn, grad_mixed, middle_sums = middle_back(
            ids, grad_before, state_one, branch, vectors, weight_both
        )
        grad_proj = owned(weight_grad(ids, mixed, grad_attn, shards, pieced, "grad_proj"))
        grads = [qkv_chunk(index) for index in range(chunks)]
        grad_first, grad_second, grad_third = [owned(chunk_grad(part)) for part in grads]
        patch_grad, small_part = finish_embed(grads)
        patch_parts = patch_back(ids, patch_grad, pixels, rows, small_part, shards, pieced)
        pixel_grad = pixel_back(ids, patch_grad, rows, patch_weight)
        small_all = small_part
        for bit in range(bits_of(shards)):
            small_all = add_low(small_all, swap(small_all, "fsdp", shards, 1 << bit))
        patch_all = patch_parts[0][SMALL_PAD:].reshape(shards, D // shards, PIXALL)
        turned = jnp.concatenate([replicas(small_all, reps), owned((patch_all,))])

    small_total = turned[:SMALL, :D].astype(F32)
    turned = turned[SMALL_PAD:]
    grad_small = lax.dynamic_slice_in_dim(small_total, here * small_cols, small_cols, axis=1)
    if pieced:
        pieces, square_parts = base_back(ids, turned, resize_coarse, resize_fine, shards)
        squares = jnp.sum(square_parts)
    else:
        base_cols = dot_nn(turned[:, :PIXC], resize_coarse)
        base_cols = base_cols + dot_nn(turned[:, PIXC : PIXC + PIXF], resize_fine)
        squares = jnp.sum(base_cols * base_cols)
        pieces = base_cols.astype(BF).reshape(base_cols.shape[0], shards, base_rows)
        pieces = pieces.transpose(1, 0, 2)
    pieces = lax.all_to_all(pieces, "fsdp", 0, 0)
    grad_base = pieces.reshape(D, base_rows).T
    wide = grad_first.shape[1] // 3
    grad_qkv = jnp.concatenate(
        [
            part[:, kind * wide : (kind + 1) * wide]
            for kind in range(3)
            for part in (grad_first, grad_second, grad_third)
        ],
        axis=1,
    )

    shards_of = [
        value.astype(F32) for value in (grad_base, grad_qkv, grad_proj, grad_fc1, grad_fc2)
    ] + [grad_small]
    for shard in shards_of[1:5]:
        squares = squares + jnp.sum(shard * shard)
    squares = total_of(squares, shards) + jnp.sum(small_total * small_total)
    grad_norm = jnp.sqrt(squares)
    clip = jnp.minimum(1.0, CLIP_NORM / grad_norm)
    masters = (w_base, w_qkv, w_proj, w_fc1, w_fc2, small_params)
    firsts = (first_base, first_qkv, first_proj, first_fc1, first_fc2, first_small)
    seconds = (second_base, second_qkv, second_proj, second_fc1, second_fc2, second_small)
    rates = (RATE, RATE, RATE, RATE, RATE, RATE_SMALL)
    results = [
        adamw(masters[index], shards_of[index], firsts[index], seconds[index], clip, rates[index])
        for index in range(6)
    ]
    return (activations, pixel_grad, grad_norm) + tuple(
        results[index][kind] for kind in range(3) for index in range(6)
    )


def solution(mesh):
    tokens = P(("fsdp", "rep"), None)
    split_rows = P("fsdp", None)
    states = (split_rows,) * 5 + (P(None, "fsdp"),)
    in_specs = (tokens, tokens, tokens, P(), P()) + states * 3 + (tokens,)
    out_specs = (tokens, tokens, P()) + states * 3
    step = functools.partial(body, mesh.shape["fsdp"], mesh.shape["rep"])
    return jax.shard_map(
        step, mesh=mesh, in_specs=in_specs, out_specs=out_specs, check_vma=False
    )
```

```python
import functools
import math

import jax
import jax.numpy as jnp
from jax import lax
from jax.experimental import pallas as pl
from jax.experimental.pallas import tpu as pltpu
from jax.sharding import PartitionSpec as P

D = 768
HEADS = 12
HEAD_DIM = 64
FF = 3072
PIXC = 768
PIXF = 192
PIXALL = 1024
STEP = 10
SLOTS = 5
SMALL = 11
SMALL_PAD = 16


EPS_NORM = 1e-06
RATE = 0.05
RATE_SMALL = 0.5
BETA_ONE = 0.9
BETA_TWO = 0.95
ADAM_EPS = 1e-08
DECAY = 0.05
CLIP_NORM = 1.0

LOG2E = math.log2(math.e)
FAR = -1e30
ATT_ROWS = 512
ROWS = 256
VMEM = 16 * 2**20
BF = jnp.bfloat16
F32 = jnp.float32
ANY = pltpu.HBM


def rows_plan(lengths, classes, count):
    ends = jnp.cumsum(lengths)
    positions = jnp.arange(count, dtype=jnp.int32)
    segment = jnp.sum((positions[:, None] >= ends[None, :]).astype(jnp.int32), axis=1)
    alive = (positions < ends[-1]).astype(F32)
    slots = jnp.arange(lengths.shape[0], dtype=jnp.int32)
    member = (segment[:, None] == slots[None, :]).astype(F32)
    finer = jnp.sum(member * classes[None, :].astype(F32), axis=1)
    return (segment, alive, finer)


def adamw(weight, grad, first, second, clip, rate):
    scaled = grad * clip
    first_new = BETA_ONE * first + (1.0 - BETA_ONE) * scaled
    second_new = BETA_TWO * second + (1.0 - BETA_TWO) * scaled * scaled
    update = (
        first_new
        / (1.0 - BETA_ONE**STEP)
        / (jnp.sqrt(second_new / (1.0 - BETA_TWO**STEP)) + ADAM_EPS)
    )
    return (weight - rate * (update + DECAY * weight), first_new, second_new)


def dot_nn(left, right):
    return jnp.dot(left, right, preferred_element_type=F32)


def dot_nt(left, right):
    return lax.dot_general(left, right, (((1,), (1,)), ((), ())), preferred_element_type=F32)


def dot_tn(left, right):
    return lax.dot_general(left, right, (((0,), (0,)), ((), ())), preferred_element_type=F32)


def norm_parts(values):
    average = jnp.mean(values, axis=-1, keepdims=True)
    centre = values - average
    spread = jnp.mean(centre * centre, axis=-1, keepdims=True)
    scale = lax.rsqrt(spread + EPS_NORM)
    return centre * scale, scale


def norm_back(grad, gain, unit, scale):
    inner = grad * gain
    mean_inner = jnp.mean(inner, axis=-1, keepdims=True)
    mean_unit = jnp.mean(inner * unit, axis=-1, keepdims=True)
    return scale * (inner - mean_inner - unit * mean_unit)


def column_sum(values):
    return jnp.sum(values, axis=0, keepdims=True)


def fetch(ids_ref, refs, offsets, target, sems, column=0, width=None):
    me = ids_ref[0]
    copies = []
    for ref, places in zip(refs, offsets):
        rows = ref.shape[1]
        for index, place in enumerate(places):
            source = ref.at[index]
            if width is not None and width != ref.shape[2]:
                source = ref.at[index, :, pl.ds(column, width)]
            first = 0 if place is None else jnp.bitwise_xor(me, place) * rows
            if place is not None:
                first = pl.multiple_of(first, rows)
            copies.append(
                pltpu.make_async_copy(
                    source, target.at[pl.ds(first, rows)], sems.at[len(copies)]
                )
            )
    return copies


def fetch_halves(ids_ref, refs, offsets, targets, sems):
    me = ids_ref[0]
    copies = []
    for ref, places in zip(refs, offsets):
        rows = ref.shape[1]
        for index, place in enumerate(places):
            if place is None:
                first, sides = 0, (0, 1)
            elif isinstance(place, tuple):
                first = pl.multiple_of(jnp.bitwise_xor(me, place[0]) * rows, rows)
                sides = (jnp.bitwise_xor(ids_ref[1], place[1]),)
            else:
                first = pl.multiple_of(jnp.bitwise_xor(me, place) * rows, rows)
                sides = (0, 1)
            at = 0
            for side in sides:
                for target in targets:
                    half = target.shape[1] // 2
                    column = side * half
                    if len(sides) == 1:
                        column = pl.multiple_of(column, 128)
                    copies.append(
                        pltpu.make_async_copy(
                            ref.at[index, :, pl.ds(at, half)],
                            target.at[pl.ds(first, rows), pl.ds(column, half)],
                            sems.at[len(copies)],
                        )
                    )
                    at += half
    return copies


def halves_count(weight):
    return sum(
        2 if isinstance(place, tuple) else 4 for places in weight[1] for place in places
    )


def begin(copies):
    for copy in copies:
        copy.start()


def finish(copies):
    for copy in copies:
        copy.wait()


def piece_count(weight):
    return sum(len(places) for places in weight[1])


def anys(count):
    return [pl.BlockSpec(memory_space=ANY)] * count


def params(limit=VMEM):
    return pltpu.CompilerParams(vmem_limit_bytes=limit)


def cost(micros):
    return pl.CostEstimate(
        flops=int(micros * 1.15e9), bytes_accessed=0, transcendentals=0
    )


def tie(value, *others):
    return lax.optimization_barrier((value,) + others)[0] if others else value


def row_spec(width, step=ROWS):
    return pl.BlockSpec((step, width), lambda i, ids: (i, 0))


def full_spec(shape):
    return pl.BlockSpec(shape, lambda i, ids: (0,) * len(shape))


def resize_kernel(ids_ref, *refs, offsets, arrays, shard_rows):
    coarse_ref, fine_ref = refs[:2]
    pieces = refs[2 : 2 + arrays]
    out_ref, resize, base, small, sems = refs[2 + arrays :]
    me = ids_ref[0]
    core = jnp.bitwise_and(me, 1)
    side = jnp.bitwise_and(lax.shift_right_logical(me, 1), 1)
    half = PIXALL // 2
    width = 2 * shard_rows
    blocks = resize.shape[1] // width
    rest = PIXC - half

    def spans(low):
        copies = []
        for block in range(blocks):
            source = pl.ds(pl.multiple_of((2 * block + side) * width, 128), width)
            target = pl.ds(block * width, width)
            at = 2 * block
            if low:
                copies.append(
                    pltpu.make_async_copy(
                        coarse_ref.at[pl.ds(0, half), source],
                        resize.at[pl.ds(0, half), target],
                        sems.at[at],
                    )
                )
            else:
                copies.append(
                    pltpu.make_async_copy(
                        coarse_ref.at[pl.ds(half, rest), source],
                        resize.at[pl.ds(0, rest), target],
                        sems.at[at],
                    )
                )
                copies.append(
                    pltpu.make_async_copy(
                        fine_ref.at[:, source],
                        resize.at[pl.ds(rest, PIXF), target],
                        sems.at[at + 1],
                    )
                )
        return copies

    copies = []
    at = 2 * blocks
    small_at = 0
    for ref, places in zip(pieces, offsets):
        for index, place in enumerate(places):
            shard = jnp.bitwise_xor(me, place)
            spot = lax.shift_right_logical(shard, 2) * 2 + jnp.bitwise_and(shard, 1)
            first = pl.multiple_of(spot * shard_rows, shard_rows)
            copies.append(
                pltpu.make_async_copy(
                    ref.at[index, pl.ds(0, shard_rows)],
                    base.at[pl.ds(first, shard_rows)],
                    sems.at[at],
                )
            )
            copies.append(
                pltpu.make_async_copy(
                    ref.at[index, pl.ds(shard_rows, 2 * SMALL_PAD)],
                    small.at[small_at],
                    sems.at[at + 1],
                )
            )
            at += 2
            small_at += 1
    begin(copies)

    @pl.when(core == 0)
    def _():
        low = spans(True)
        begin(low)
        finish(low)

    @pl.when(core != 0)
    def _():
        resize[pl.ds(rest + PIXF, half - rest - PIXF)] = jnp.zeros(
            (half - rest - PIXF, resize.shape[1]), BF
        )
        high = spans(False)
        begin(high)
        finish(high)

    finish(copies)
    out_ref[:half] = dot_nn(resize[...], base[...]).astype(BF)
    joined = small[0].astype(F32)
    for index in range(1, small_at):
        joined = joined + small[index].astype(F32)
    out_ref[half:] = joined.astype(BF)


def resize_part(ids, coarse, fine, arrays, offsets, shard_rows):
    half = PIXALL // 2
    count = sum(len(places) for places in offsets)
    blocks = count // 2
    return pl.pallas_call(
        functools.partial(
            resize_kernel, offsets=offsets, arrays=len(arrays), shard_rows=shard_rows
        ),
        grid_spec=pltpu.PrefetchScalarGridSpec(
            num_scalar_prefetch=1,
            grid=(1,),
            in_specs=anys(2 + len(arrays)),
            out_specs=full_spec((half + 2 * SMALL_PAD, D // 2)),
            scratch_shapes=[
                pltpu.VMEM((half, count * shard_rows), BF),
                pltpu.VMEM((count * shard_rows, D // 2), BF),
                pltpu.VMEM((count, 2 * SMALL_PAD, D // 2), BF),
                pltpu.SemaphoreType.DMA((2 * blocks + 2 * count,)),
            ],
        ),
        out_shape=jax.ShapeDtypeStruct((half + 2 * SMALL_PAD, D // 2), BF),
        compiler_params=params(),
        cost_estimate=cost(0),
        name="resize_part",
    )(ids, coarse, fine, *arrays)


def spread_pixels(pixels, fine_col):
    rough = jnp.where(fine_col > 0.5, jnp.zeros((), BF), pixels)
    wide = PIXALL - PIXC
    lane = lax.broadcasted_iota(jnp.int32, (pixels.shape[0], wide), 1)
    fine = jnp.where((lane < PIXF) & (fine_col > 0.5), pixels[:, :wide], jnp.zeros((), BF))
    return jnp.concatenate([rough, fine], axis=1)


def patch_kernel(ids_ref, pixels_ref, rows_ref, vectors_ref, *refs, places, arrays):
    pieces = refs[:arrays]
    state_ref, normed_ref, weight_ref, sems = refs[arrays:]

    @pl.when(pl.program_id(0) == 0)
    def _():
        copies = []
        for ref, spots in zip(pieces, places):
            for index, spot in enumerate(spots):
                rows, width = ref.shape[1:]
                first, column = (0, 0) if spot is None else spot
                if spot is not None:
                    first = jnp.bitwise_xor(jnp.bitwise_and(ids_ref[0], 1), first) * rows
                    column = jnp.bitwise_xor(ids_ref[1], column) * width
                    first = pl.multiple_of(first, rows)
                    column = pl.multiple_of(column, 128)
                copies.append(
                    pltpu.make_async_copy(
                        ref.at[index],
                        weight_ref.at[pl.ds(first, rows), pl.ds(column, width)],
                        sems.at[len(copies)],
                    )
                )
        begin(copies)
        finish(copies)

    pixels = spread_pixels(pixels_ref[...], rows_ref[:, 2:3])
    vectors = vectors_ref[...]
    state = dot_nn(pixels, weight_ref[...]) + vectors[0:1]
    unit, _ = norm_parts(state)
    state_ref[...] = state
    normed_ref[...] = (unit * vectors[1:2] + vectors[2:3]).astype(BF)


def patch(ids, pixels, rows, vectors, arrays, places, deps=()):
    count = pixels.shape[0]
    total = sum(len(spots) for spots in places)
    return pl.pallas_call(
        functools.partial(patch_kernel, places=places, arrays=len(arrays)),
        grid_spec=pltpu.PrefetchScalarGridSpec(
            num_scalar_prefetch=1,
            grid=(count // ROWS,),
            in_specs=[row_spec(PIXC), row_spec(8), full_spec(vectors.shape)]
            + anys(len(arrays)),
            out_specs=[row_spec(D), row_spec(D), full_spec((PIXALL, D))],
            scratch_shapes=[pltpu.SemaphoreType.DMA((total,))],
        ),
        out_shape=[
            jax.ShapeDtypeStruct((count, D), F32),
            jax.ShapeDtypeStruct((count, D), BF),
            jax.ShapeDtypeStruct((PIXALL, D), BF),
        ],
        compiler_params=params(52 * 2**20),
        cost_estimate=cost(0),
        name="patch",
    )(tie(ids, *deps), pixels, rows, vectors, *arrays)


def qkv_kernel(ids_ref, normed_ref, *refs, offsets, arrays):
    pieces = refs[:arrays]
    out_ref, weight, sems = refs[arrays:]

    @pl.when(pl.program_id(0) == 0)
    def _():
        copies = fetch(ids_ref, pieces, offsets, weight, sems)
        begin(copies)
        finish(copies)

    out_ref[...] = dot_nn(normed_ref[...], weight[...]).astype(BF)


def project_qkv(ids, normed, weight, deps=()):
    arrays, offsets = weight
    count = normed.shape[0]
    return pl.pallas_call(
        functools.partial(qkv_kernel, offsets=offsets, arrays=len(arrays)),
        grid_spec=pltpu.PrefetchScalarGridSpec(
            num_scalar_prefetch=1,
            grid=(count // ROWS,),
            in_specs=[row_spec(D)] + anys(len(arrays)),
            out_specs=row_spec(3 * D),
            scratch_shapes=[
                pltpu.VMEM((D, 3 * D), BF),
                pltpu.SemaphoreType.DMA((piece_count(weight),)),
            ],
        ),
        out_shape=jax.ShapeDtypeStruct((count, 3 * D), BF),
        compiler_params=params(),
        cost_estimate=cost(0),
        name="project_qkv",
    )(tie(ids, *deps), normed, *arrays)


def lane_plan(rows, side, seg):
    lane = lax.broadcasted_iota(jnp.int32, (rows, 2 * HEAD_DIM), 1)
    mine = (lane < HEAD_DIM) if side == 0 else (lane >= HEAD_DIM)
    first = HEAD_DIM if side == 0 else 0
    hot = lane - first == seg
    slots = (lane >= first) & (lane < first + SLOTS)
    return lane, mine, hot, slots


def attend_kernel(ids_ref, seg_ref, q_ref, k_ref, v_ref, mixed_ref, log_ref, *, step, start):
    pair = pl.program_id(0) + start
    rows = q_ref.shape[0]
    seg = seg_ref[...]
    one = jnp.ones((), BF)
    logs = jnp.where(pair == start, 0.0, log_ref[...])
    outs = []
    for side in range(2):
        lane, mine, hot, slots = lane_plan(rows, side, seg)
        keys = jnp.where(
            mine, k_ref[...], jnp.where(slots & ~hot, FAR, 0.0).astype(BF)
        )
        values = jnp.where(mine, v_ref[...], one)
        queries = jnp.where(mine, q_ref[...] * BF(0.125), hot.astype(BF))
        parts, part_logs = [], []
        for at in range(0, rows, step):
            scores = lax.dot_general(
                queries[at : at + step],
                keys,
                (((1,), (1,)), ((), ())),
                preferred_element_type=F32,
            )
            top = jnp.max(scores, axis=1, keepdims=True) * LOG2E
            raised = jnp.exp2(scores * LOG2E - top).astype(BF)
            sums = jnp.dot(raised, values, preferred_element_type=F32)
            turned = pltpu.roll(sums, HEAD_DIM, 1)
            inside = mine[at : at + step]
            parts.append(sums / turned)
            part_logs.append(top + jnp.log2(jnp.where(inside, turned, sums)))
        outs.append(jnp.concatenate(parts, axis=0))
        logs = jnp.where(lane == 2 * pair + side, jnp.concatenate(part_logs, axis=0), logs)
    lane = lax.broadcasted_iota(jnp.int32, (rows, 2 * HEAD_DIM), 1)
    mixed_ref[...] = jnp.where(lane < HEAD_DIM, outs[0], outs[1]).astype(BF)
    log_ref[...] = logs


def attend(ids, qkv, seg, start, many, deps=()):
    rows = qkv.shape[0]
    wide = 2 * HEAD_DIM
    pairs = D // wide
    step = min(ATT_ROWS, rows)

    def block(first):
        return pl.BlockSpec((rows, wide), lambda pair, ids: (0, first + start + pair))

    return pl.pallas_call(
        functools.partial(attend_kernel, step=step, start=start),
        grid_spec=pltpu.PrefetchScalarGridSpec(
            num_scalar_prefetch=1,
            grid=(many,),
            in_specs=[full_spec((rows, 1)), block(0), block(pairs), block(2 * pairs)],
            out_specs=[
                pl.BlockSpec((rows, wide), lambda pair, ids: (0, pair)),
                full_spec((rows, wide)),
            ],
        ),
        out_shape=[
            jax.ShapeDtypeStruct((rows, many * wide), BF),
            jax.ShapeDtypeStruct((rows, wide), F32),
        ],
        compiler_params=params(),
        cost_estimate=cost(0),
        name="attend",
    )(tie(ids, *deps), seg, qkv, qkv, qkv)


def attend_back_kernel(
    ids_ref,
    seg_ref,
    q_ref,
    k_ref,
    v_ref,
    mixed_ref,
    grad_ref,
    log_ref,
    out_ref,
    *,
    step,
    start,
):
    pair = pl.program_id(0) + start
    rows = q_ref.shape[0]
    seg = seg_ref[...]
    zero = jnp.zeros((), BF)
    product = grad_ref[...].astype(F32) * mixed_ref[...].astype(F32)
    plain_keys = k_ref[...]
    values = v_ref[...]
    scaled = q_ref[...] * BF(0.125)
    results = []
    for side in range(2):
        lane, mine, hot, slots = lane_plan(rows, side, seg)
        keys = jnp.where(
            mine, plain_keys, jnp.where(slots & ~hot, FAR, 0.0).astype(BF)
        )
        queries = jnp.where(mine, scaled, hot.astype(BF))
        grads = jnp.where(mine, grad_ref[...], zero)
        queries_t = jnp.where(mine, scaled, zero).T
        grads_t = grads.T
        drop = jnp.sum(jnp.where(mine, product, 0.0), axis=1, keepdims=True)
        logs = jnp.sum(
            jnp.where(lane == 2 * pair + side, log_ref[...], 0.0), axis=1, keepdims=True
        )
        dq_parts, dk_t, dv_t = [], 0.0, 0.0
        for at in range(0, rows, step):
            part = slice(at, at + step)
            scores = lax.dot_general(
                queries[part],
                keys,
                (((1,), (1,)), ((), ())),
                preferred_element_type=F32,
            )
            probs = jnp.exp2(scores * LOG2E - logs[part])
            grad_probs = lax.dot_general(
                grads[part],
                values,
                (((1,), (1,)), ((), ())),
                preferred_element_type=F32,
            )
            grad_scores = (probs * (grad_probs - drop[part])).astype(BF)
            probs = probs.astype(BF)
            dq_parts.append(jnp.dot(grad_scores, plain_keys, preferred_element_type=F32))
            dv_t = dv_t + jnp.dot(grads_t[:, part], probs, preferred_element_type=F32)
            dk_t = dk_t + jnp.dot(
                queries_t[:, part], grad_scores, preferred_element_type=F32
            )
        results.append((jnp.concatenate(dq_parts, axis=0) * 0.125, dk_t.T, dv_t.T))
    lane = lax.broadcasted_iota(jnp.int32, (rows, 2 * HEAD_DIM), 1)
    for kind, (low, high) in enumerate(zip(results[0], results[1])):
        out_ref[kind] = jnp.where(lane < HEAD_DIM, low, high).astype(BF)


def attend_back(ids, qkv, seg, mixed, grad_mixed, logs, start, many, deps=()):
    rows = qkv.shape[0]
    wide = 2 * HEAD_DIM
    pairs = D // wide
    step = min(ATT_ROWS, rows)

    def block(first):
        return pl.BlockSpec((rows, wide), lambda pair, ids: (0, first + start + pair))

    kernel = functools.partial(attend_back_kernel, step=step, start=start)
    return pl.pallas_call(
        kernel,
        grid_spec=pltpu.PrefetchScalarGridSpec(
            num_scalar_prefetch=1,
            grid=(many,),
            in_specs=[
                full_spec((rows, 1)),
                block(0),
                block(pairs),
                block(2 * pairs),
                block(0),
                block(0),
                full_spec((rows, wide)),
            ],
            out_specs=pl.BlockSpec((3, rows, wide), lambda pair, ids: (0, 0, pair)),
        ),
        out_shape=jax.ShapeDtypeStruct((3, rows, many * wide), BF),
        compiler_params=params(),
        cost_estimate=cost(0),
        name="attend_back",
    )(tie(ids, *deps), seg, qkv, qkv, qkv, mixed, grad_mixed, logs)


def up_kernel(
    ids_ref, mixed_ref, state_ref, vectors_ref, bias_ref, *refs, offsets, arrays, columns
):
    pieces = refs[:arrays]
    one_ref, normed_ref, hidden_ref, slope_ref, proj, up, sems = refs[arrays:]

    @pl.when(pl.program_id(0) == 0)
    def _():
        copies = fetch_halves(ids_ref, pieces, offsets, (proj, up), sems)
        begin(copies)
        finish(copies)

    vectors = vectors_ref[...]
    state = state_ref[...] + dot_nn(mixed_ref[...], proj[...]) + vectors[3:4]
    one_ref[...] = state
    unit, _ = norm_parts(state)
    normed = (unit * vectors[4:5] + vectors[5:6]).astype(BF)
    normed_ref[...] = normed
    for at in range(0, FF, columns):
        part = slice(at, at + columns)
        before = dot_nn(normed, up[:, part]) + bias_ref[:, part]
        share = 0.5 + 0.5 * lax.erf(before * math.sqrt(0.5))
        bell = jnp.exp2(before * before * (-0.5 * LOG2E)) * (1.0 / math.sqrt(2.0 * math.pi))
        hidden_ref[:, part] = (before * share).astype(BF)
        slope_ref[:, part] = (share + before * bell).astype(BF)


def feed_up(ids, mixed, state, vectors, bias, weight, deps=()):
    arrays, offsets = weight
    count = mixed.shape[0]
    total = halves_count(weight)
    return pl.pallas_call(
        functools.partial(up_kernel, offsets=offsets, arrays=len(arrays), columns=512),
        grid_spec=pltpu.PrefetchScalarGridSpec(
            num_scalar_prefetch=1,
            grid=(count // ROWS,),
            in_specs=[
                row_spec(D),
                row_spec(D),
                full_spec(vectors.shape),
                full_spec(bias.shape),
            ]
            + anys(len(arrays)),
            out_specs=[row_spec(D), row_spec(D), row_spec(FF), row_spec(FF)],
            scratch_shapes=[
                pltpu.VMEM((D, D), BF),
                pltpu.VMEM((D, FF), BF),
                pltpu.SemaphoreType.DMA((total,)),
            ],
        ),
        out_shape=[
            jax.ShapeDtypeStruct((count, D), F32),
            jax.ShapeDtypeStruct((count, D), BF),
            jax.ShapeDtypeStruct((count, FF), BF),
            jax.ShapeDtypeStruct((count, FF), BF),
        ],
        compiler_params=params(),
        cost_estimate=cost(0),
        name="feed_up",
    )(tie(ids, *deps), mixed, state, vectors, bias, *arrays)


def down_kernel(
    ids_ref,
    hidden_ref,
    slope_ref,
    state_ref,
    cotangent_ref,
    rows_ref,
    vectors_ref,
    *refs,
    offsets,
    arrays,
    columns,
):
    pieces = refs[:arrays]
    out_ref, branch_ref, before_ref, sums_ref, weight, sems = refs[arrays:]

    @pl.when(pl.program_id(0) == 0)
    def _():
        copies = fetch(ids_ref, pieces, offsets, weight, sems)
        begin(copies)
        sums_ref[...] = jnp.zeros_like(sums_ref)
        finish(copies)

    alive = rows_ref[:, 1:2]
    state = state_ref[...] + dot_nn(hidden_ref[...], weight[...]) + vectors_ref[6:7]
    out_ref[...] = (state * alive).astype(BF)
    grad = cotangent_ref[...].astype(F32) * alive
    branch = grad.astype(BF)
    branch_ref[...] = branch
    sums_ref[0:1, :D] += column_sum(grad)
    for at in range(0, FF, columns):
        part = slice(at, at + columns)
        before = dot_nt(branch, weight[part]) * slope_ref[:, part].astype(F32)
        before = before.astype(BF)
        before_ref[:, part] = before
        sums_ref[1:2, part] += column_sum(before.astype(F32))


def feed_down(ids, hidden, slope, state, cotangent, rows, vectors, weight, deps=()):
    arrays, offsets = weight
    count = hidden.shape[0]
    return pl.pallas_call(
        functools.partial(down_kernel, offsets=offsets, arrays=len(arrays), columns=768),
        grid_spec=pltpu.PrefetchScalarGridSpec(
            num_scalar_prefetch=1,
            grid=(count // ROWS,),
            in_specs=[
                row_spec(FF),
                row_spec(FF),
                row_spec(D),
                row_spec(D),
                row_spec(8),
                full_spec(vectors.shape),
            ]
            + anys(len(arrays)),
            out_specs=[row_spec(D), row_spec(D), row_spec(FF), full_spec((8, FF))],
            scratch_shapes=[
                pltpu.VMEM((FF, D), BF),
                pltpu.SemaphoreType.DMA((piece_count(weight),)),
            ],
        ),
        out_shape=[
            jax.ShapeDtypeStruct((count, D), BF),
            jax.ShapeDtypeStruct((count, D), BF),
            jax.ShapeDtypeStruct((count, FF), BF),
            jax.ShapeDtypeStruct((8, FF), F32),
        ],
        compiler_params=params(),
        cost_estimate=cost(0),
        name="feed_down",
    )(tie(ids, *deps), hidden, slope, state, cotangent, rows, vectors, *arrays)


def middle_kernel(
    ids_ref, before_ref, state_ref, branch_ref, vectors_ref, *refs, offsets, arrays
):
    pieces = refs[:arrays]
    grad_ref, attn_ref, mixed_ref, sums_ref, proj, up, sems = refs[arrays:]

    @pl.when(pl.program_id(0) == 0)
    def _():
        copies = fetch_halves(ids_ref, pieces, offsets, (proj, up), sems)
        begin(copies)
        sums_ref[...] = jnp.zeros_like(sums_ref)
        finish(copies)

    vectors = vectors_ref[...]
    normed = dot_nt(before_ref[...], up[...])
    unit, scale = norm_parts(state_ref[...])
    grad = branch_ref[...].astype(F32) + norm_back(normed, vectors[4:5], unit, scale)
    grad_ref[...] = grad
    attn = grad.astype(BF)
    attn_ref[...] = attn
    mixed_ref[...] = dot_nt(attn, proj[...]).astype(BF)
    sums_ref[0:1] += column_sum(grad)
    sums_ref[1:2] += column_sum(normed * unit)
    sums_ref[2:3] += column_sum(normed)


def middle_back(ids, before, state, branch, vectors, weight, deps=()):
    arrays, offsets = weight
    count = before.shape[0]
    total = halves_count(weight)
    return pl.pallas_call(
        functools.partial(middle_kernel, offsets=offsets, arrays=len(arrays)),
        grid_spec=pltpu.PrefetchScalarGridSpec(
            num_scalar_prefetch=1,
            grid=(count // ROWS,),
            in_specs=[row_spec(FF), row_spec(D), row_spec(D), full_spec(vectors.shape)]
            + anys(len(arrays)),
            out_specs=[row_spec(D), row_spec(D), row_spec(D), full_spec((8, D))],
            scratch_shapes=[
                pltpu.VMEM((D, D), BF),
                pltpu.VMEM((D, FF), BF),
                pltpu.SemaphoreType.DMA((total,)),
            ],
        ),
        out_shape=[
            jax.ShapeDtypeStruct((count, D), F32),
            jax.ShapeDtypeStruct((count, D), BF),
            jax.ShapeDtypeStruct((count, D), BF),
            jax.ShapeDtypeStruct((8, D), F32),
        ],
        compiler_params=params(52 * 2**20),
        cost_estimate=cost(0),
        name="middle_back",
    )(tie(ids, *deps), before, state, branch, vectors, *arrays)


def place_pieces(ids_ref, values, kept_ref, sent_ref, shards, rows, first, lead=0):
    count = values.shape[0] // rows
    flat = len(kept_ref.shape) == 2
    if sent_ref is None:
        if flat:
            kept_ref[lead:] = values
        else:
            kept_ref[pl.ds(first, count)] = values.reshape((count, rows) + values.shape[1:])
        return
    me = ids_ref[0]
    for index in range(count):
        apart = jnp.bitwise_xor(me, first + index)
        spot = 0
        for bit in range(1, bits_of(shards)):
            spot = spot * 2 + jnp.bitwise_and(lax.shift_right_logical(apart, bit), 1)
        piece = values[index * rows : (index + 1) * rows]
        same = jnp.bitwise_and(apart, 1) == 0

        def put(ref, piece=piece, spot=spot):
            if flat:
                ref[pl.ds(pl.multiple_of(lead + spot * rows, 16), rows)] = piece
            else:
                ref[spot] = piece

        pl.when(same)(functools.partial(put, kept_ref))
        pl.when(jnp.logical_not(same))(functools.partial(put, sent_ref))


def weight_kernel(ids_ref, left_ref, right_ref, *refs, shards, rows, first_step, extra):
    out_refs, turned = refs[2 * extra : -1], refs[-1]
    sent_ref = out_refs[1] if len(out_refs) > 1 else None
    step = pl.program_id(0)

    def put(left_ref, right_ref, start=0):
        right = right_ref[0] if len(right_ref.shape) == 3 else right_ref[...]
        if first_step:
            values = dot_tn(left_ref[...], right).astype(BF)
        else:

            @pl.when(step == start)
            def _():
                turned[...] = left_ref[...].T

            values = dot_nn(turned[...], right).astype(BF)
        place_pieces(
            ids_ref, values, out_refs[0], sent_ref, shards, rows, step * first_step
        )

    if extra:
        last = pl.num_programs(0) - extra * (refs[1].shape[1] // right_ref.shape[2])
        pl.when(step < last)(lambda: put(left_ref, right_ref))

        @pl.when(step >= last)
        def _():
            wide = right_ref.shape[2]
            for index in range(refs[1].shape[1] // wide):
                part = pl.ds(index * wide, wide)

                @pl.when(step == last + index)
                def _(part=part):
                    put(refs[0], refs[1].at[:, part], last)

    else:
        put(left_ref, right_ref)


def weight_grad(ids, left, right, shards, split, name, deps=(), extra=()):
    count, tall = left.shape
    stacked = right.ndim == 3
    wide = right.shape[-1]
    step = wide if stacked else min(768, max(tall, wide))
    narrow = tall > wide and not stacked
    rows = tall // shards
    outs = 2 if split else 1
    pieces = shards // outs
    more_specs = []
    if narrow:
        grid, first_step, out_wide = tall // step, step // rows, wide
        specs = [
            pl.BlockSpec((count, step), lambda i, ids: (0, i)),
            pl.BlockSpec((count, wide), lambda i, ids: (0, 0)),
        ]
        out_spec = pl.BlockSpec((pieces, rows, wide), lambda i, ids: (0, 0, 0))
    else:
        first_step = 0
        if stacked:
            kinds = right.shape[0]
            grid, out_wide = kinds, kinds * wide
            if extra:
                grid, out_wide = grid + extra[1].shape[1] // wide, out_wide + extra[1].shape[1]
                more_specs = [full_spec(value.shape) for value in extra]
            right_spec = pl.BlockSpec(
                (1, count, step), lambda i, ids: (jnp.minimum(i, kinds - 1), 0, 0)
            )
        else:
            grid, out_wide = wide // step, wide
            right_spec = pl.BlockSpec((count, step), lambda i, ids: (0, i))
        specs = [pl.BlockSpec((count, tall), lambda i, ids: (0, 0)), right_spec]
        out_spec = pl.BlockSpec((pieces, rows, step), lambda i, ids: (0, 0, i))
    kernel = functools.partial(
        weight_kernel,
        shards=shards,
        rows=rows,
        first_step=first_step,
        extra=1 if extra else 0,
    )
    return pl.pallas_call(
        kernel,
        grid_spec=pltpu.PrefetchScalarGridSpec(
            num_scalar_prefetch=1,
            grid=(grid,),
            in_specs=specs + more_specs,
            out_specs=[out_spec] * outs,
            scratch_shapes=[pltpu.VMEM((16, 128) if narrow else (tall, count), BF)],
        ),
        out_shape=[jax.ShapeDtypeStruct((pieces, rows, out_wide), BF)] * outs,
        compiler_params=params(),
        cost_estimate=cost(0),
        name=name,
    )(tie(ids, *deps), left, right, *extra)


def embed_kernel(
    ids_ref,
    state_ref,
    grad_ref,
    vectors_ref,
    down_sums_ref,
    middle_sums_ref,
    *refs,
    offsets,
    arrays,
    chunks,
):
    grad_refs = refs[:chunks]
    pieces = refs[chunks : chunks + arrays]
    patch_ref, small_ref, weight, sums, sems = refs[chunks + arrays :]
    step = pl.program_id(0)

    @pl.when(step == 0)
    def _():
        copies = fetch(ids_ref, pieces, offsets, weight, sems)
        begin(copies)
        sums[...] = jnp.zeros_like(sums)
        finish(copies)

    normed = 0.0
    at = 0
    for ref in grad_refs:
        wide = ref.shape[2]
        for kind in range(3):
            first = kind * D + at
            normed = normed + dot_nt(ref[kind], weight[:, first : first + wide])
        at += wide
    unit, scale = norm_parts(state_ref[...])
    grad = grad_ref[...] + norm_back(normed, vectors_ref[1:2], unit, scale)
    patch_ref[...] = grad.astype(BF)
    sums[0:1] += column_sum(grad)
    sums[1:2] += column_sum(normed * unit)
    sums[2:3] += column_sum(normed)

    @pl.when(step == pl.num_programs(0) - 1)
    def _():
        small = [sums[0:3], middle_sums_ref[0:3], down_sums_ref[0:1, :D]]
        small += [
            down_sums_ref[1:2, index * D : (index + 1) * D] for index in range(FF // D)
        ]
        small += [jnp.zeros((SMALL_PAD - SMALL, D), F32)]
        small_ref[:, :D] = jnp.concatenate(small, axis=0).astype(BF)
        small_ref[:, D:] = jnp.zeros((SMALL_PAD, PIXALL - D), BF)


def embed_back(
    ids, grads, state, grad, vectors, down_sums, middle_sums, weight, deps=()
):
    arrays, offsets = weight
    count = state.shape[0]
    kernel = functools.partial(
        embed_kernel, offsets=offsets, arrays=len(arrays), chunks=len(grads)
    )
    return pl.pallas_call(
        kernel,
        grid_spec=pltpu.PrefetchScalarGridSpec(
            num_scalar_prefetch=1,
            grid=(count // ROWS,),
            in_specs=[
                row_spec(D),
                row_spec(D),
                full_spec(vectors.shape),
                full_spec(down_sums.shape),
                full_spec(middle_sums.shape),
            ]
            + [
                pl.BlockSpec((3, ROWS, part.shape[2]), lambda i, ids: (0, i, 0))
                for part in grads
            ]
            + anys(len(arrays)),
            out_specs=[row_spec(D), full_spec((SMALL_PAD, PIXALL))],
            scratch_shapes=[
                pltpu.VMEM((D, 3 * D), BF),
                pltpu.VMEM((8, D), F32),
                pltpu.SemaphoreType.DMA((piece_count(weight),)),
            ],
        ),
        out_shape=[
            jax.ShapeDtypeStruct((count, D), BF),
            jax.ShapeDtypeStruct((SMALL_PAD, PIXALL), BF),
        ],
        compiler_params=params(),
        cost_estimate=cost(0),
        name="embed_back",
    )(tie(ids, *deps), state, grad, vectors, down_sums, middle_sums, *grads, *arrays)


def patch_back_kernel(ids_ref, patch_ref, pixels_ref, rows_ref, small_ref, *out_refs, shards):
    sent_ref = out_refs[1] if len(out_refs) > 1 else None
    spread = spread_pixels(pixels_ref[...], rows_ref[:, 2:3])
    values = dot_tn(patch_ref[...], spread).astype(BF)
    place_pieces(
        ids_ref, values, out_refs[0], sent_ref, shards, D // shards, 0, SMALL_PAD
    )
    for ref in out_refs:
        ref[:SMALL_PAD] = small_ref[...]


def patch_back(ids, patch_grad, pixels, rows, small, shards, split, deps=()):
    count = pixels.shape[0]
    outs = 2 if split else 1
    held = (SMALL_PAD + D // outs, PIXALL)
    return pl.pallas_call(
        functools.partial(patch_back_kernel, shards=shards),
        grid_spec=pltpu.PrefetchScalarGridSpec(
            num_scalar_prefetch=1,
            grid=(1,),
            in_specs=[
                full_spec((count, D)),
                full_spec((count, PIXC)),
                full_spec(rows.shape),
                full_spec(small.shape),
            ],
            out_specs=[full_spec(held)] * outs,
        ),
        out_shape=[jax.ShapeDtypeStruct(held, BF)] * outs,
        compiler_params=params(),
        cost_estimate=cost(0),
        name="patch_back",
    )(tie(ids, *deps), patch_grad, pixels, rows, small)


def pixel_kernel(ids_ref, patch_ref, rows_ref, weight_ref, out_ref):
    fine = rows_ref[:, 2:3]
    both = dot_nt(patch_ref[...], weight_ref[...])
    wide = PIXALL - PIXC
    rough = both[:, :PIXC] * (1.0 - fine)
    first = rough[:, :wide] + both[:, PIXC:] * fine
    out_ref[...] = jnp.concatenate([first, rough[:, wide:]], axis=1).astype(BF)


def pixel_back(ids, patch_grad, rows, weight, deps=()):
    count = patch_grad.shape[0]
    return pl.pallas_call(
        pixel_kernel,
        grid_spec=pltpu.PrefetchScalarGridSpec(
            num_scalar_prefetch=1,
            grid=(count // ROWS,),
            in_specs=[row_spec(D), row_spec(8), full_spec(weight.shape)],
            out_specs=row_spec(PIXC),
        ),
        out_shape=jax.ShapeDtypeStruct((count, PIXC), BF),
        compiler_params=params(),
        cost_estimate=cost(4),
        name="pixel_back",
    )(tie(ids, *deps), patch_grad, rows, weight)


def base_kernel(ids_ref, turned_ref, coarse_ref, fine_ref, out_ref, square_ref):
    turned = turned_ref[...]
    grad = dot_nn(turned[:, :PIXC], coarse_ref[...])
    grad = grad + dot_nn(turned[:, PIXC : PIXC + PIXF], fine_ref[...])

    @pl.when(pl.program_id(0) == 0)
    def _():
        square_ref[...] = jnp.zeros_like(square_ref)

    square_ref[...] += jnp.sum(grad * grad, axis=0, keepdims=True)
    low = grad.astype(BF)
    rows = out_ref.shape[2]
    for index in range(out_ref.shape[0]):
        out_ref[index] = low[:, index * rows : (index + 1) * rows]


def base_back(ids, turned, coarse, fine, shards, deps=()):
    count, wide = turned.shape[0], coarse.shape[1]
    step = 768
    rows = wide // shards
    return pl.pallas_call(
        base_kernel,
        grid_spec=pltpu.PrefetchScalarGridSpec(
            num_scalar_prefetch=1,
            grid=(wide // step,),
            in_specs=[
                full_spec(turned.shape),
                pl.BlockSpec((PIXC, step), lambda i, ids: (0, i)),
                pl.BlockSpec((PIXF, step), lambda i, ids: (0, i)),
            ],
            out_specs=[
                pl.BlockSpec((step // rows, count, rows), lambda i, ids: (i, 0, 0)),
                full_spec((1, step)),
            ],
        ),
        out_shape=[
            jax.ShapeDtypeStruct((shards, count, rows), BF),
            jax.ShapeDtypeStruct((1, step), F32),
        ],
        compiler_params=params(),
        cost_estimate=cost(0),
        name="base_back",
    )(tie(ids, *deps), turned, coarse, fine)


def bits_of(count):
    bits = count.bit_length() - 1
    assert count == 1 << bits
    return bits


def swap(value, axis, count, mask):
    return lax.ppermute(value, axis, [(i, i ^ mask) for i in range(count)])


def add_low(left, right):
    return (left.astype(F32) + right.astype(F32)).astype(BF)


class Gather:
    def __init__(self, shard, count):
        self.held, self.places, self.count = shard[None], [0], count
        self.bits = list(reversed(range(2, bits_of(count))))
        self.other = None

    def land(self, *after):
        if self.other is not None:
            self.held = jnp.concatenate([self.held, tie(self.other, *after)])
            self.other = None
        return self.held

    def step(self, *after):
        bit = self.bits.pop(0)
        held = tie(self.land(*after), *after)
        self.other = swap(held, "fsdp", self.count, 1 << bit)
        self.places = self.places + [place ^ (1 << bit) for place in self.places]
        return self.other

    def high(self, *after):
        held = tie(self.held, *after)
        masks = [0]
        while self.bits:
            masks = masks + [mask ^ (1 << self.bits[0]) for mask in masks]
            self.bits.pop(0)
        self.rest = [swap(held, "fsdp", self.count, mask) for mask in masks[1:]]
        self.places = masks
        return self.rest

    def join(self, *after):
        self.held = jnp.concatenate([self.held] + [tie(part, *after) for part in self.rest])

    def far(self, *after):
        held = tie(self.land(*after), *after)
        self.other = swap(held, "fsdp", self.count, 2)
        self.held_core = swap(held, "fsdp", self.count, 1)
        return self.other

    def far_halves(self, there, *after):
        held = tie(self.land(*after), *after)
        half = held.shape[2] // 2
        sent = lax.dynamic_slice_in_dim(held, there * half, half, axis=2)
        self.mine = swap(sent, "fsdp", self.count, 2)
        self.held_core = swap(held, "fsdp", self.count, 1)
        return self.mine

    def near_halves(self, *after):
        mine = tie(self.mine, *after)
        rest = swap(mine, "rep", 2, 1)
        mine_core = swap(mine, "fsdp", self.count, 1)
        rest_core = swap(rest, "fsdp", self.count, 1)
        arrays = (self.held, self.held_core, self.mine, mine_core, rest, rest_core)
        offsets = [tuple(p ^ mask for p in self.places) for mask in (0, 1)]
        offsets += [
            tuple((p ^ mask, side) for p in self.places) for side in (0, 1) for mask in (2, 3)
        ]
        return (arrays, tuple(offsets)), rest

    def near(self, *after):
        other_core = swap(tie(self.other, *after), "fsdp", self.count, 1)
        offsets = tuple(tuple(p ^ mask for p in self.places) for mask in (0, 1, 2, 3))
        return (self.held, self.held_core, self.other, other_core), offsets


def halves_of(value, side):
    wide = value.shape[1] // 2
    return value[:, side * wide : (side + 1) * wide]


def gather_whole(shard, count):
    here = lax.axis_index("fsdp")
    held = shard[None]
    for bit in reversed(range(bits_of(count))):
        other = swap(held, "fsdp", count, 1 << bit)
        upper = (here >> bit) & 1 == 1
        both = jnp.where(
            upper, jnp.stack([other, held], axis=1), jnp.stack([held, other], axis=1)
        )
        held = both.reshape((-1,) + shard.shape)
    return held.reshape((-1,) + shard.shape[1:])


def as_piece(whole):
    return (whole[None],), ((None,),)


def scatter_whole(blocks, count):
    here = lax.axis_index("fsdp")
    held = blocks
    for bit in range(bits_of(count)):
        side = (here >> bit) & 1
        halves = held.reshape((held.shape[0] // 2, 2) + held.shape[1:])
        sent = lax.dynamic_index_in_dim(halves, 1 - side, axis=1, keepdims=False)
        kept = lax.dynamic_index_in_dim(halves, side, axis=1, keepdims=False)
        held = add_low(kept, swap(sent, "fsdp", count, 1 << bit))
    return held[0]


class Scatter:
    def __init__(self, parts, shards, reps, plan, lead=0):
        self.kept, self.ready = parts
        self.shards, self.reps, self.lead = shards, reps, lead
        self.plan = plan
        self.at = 0

    def step(self, *after):
        kind = self.plan[self.at]
        value = tie(self.ready, *after)
        if isinstance(kind, int):
            self.other = swap(value, "fsdp", self.shards, 1 << kind)
        else:
            self.other = swap(value, "rep", self.reps, 1)
        self.at += 1

    def land(self, *after):
        kept, other = self.kept, tie(self.other, *after)
        following = self.plan[self.at] if self.at < len(self.plan) else None
        there = lax.axis_index("rep")
        if following == "half":
            wide = kept.shape[-1] // 2

            def columns(side):
                return add_low(
                    lax.dynamic_slice_in_dim(kept, side * wide, wide, axis=2),
                    lax.dynamic_slice_in_dim(other, side * wide, wide, axis=2),
                )

            self.kept, self.ready = columns(there), columns(1 - there)
        elif isinstance(following, int):
            half = (kept.shape[0] - self.lead) // 2 + self.lead
            low, high = add_low(kept[:half], other[:half]), add_low(kept[half:], other[half:])
            self.kept, self.ready = low, high
            if self.lead:
                self.ready = jnp.concatenate([low[: self.lead], high])
        else:
            self.kept = self.ready = add_low(kept, other)
        return self.ready


def merged(parts, more, shards, reps, plan):
    kept = jnp.concatenate([part.kept for part in (parts, more)], axis=2)
    ready = jnp.concatenate([part.ready for part in (parts, more)], axis=2)
    return Scatter((kept, ready), shards, reps, plan)


def rows_of(value):
    return [value[:, at : at + D] for at in range(0, value.shape[1], D)]


def replicas(value, count):
    for bit in range(bits_of(count)):
        value = add_low(value, swap(value, "rep", count, 1 << bit))
    return value


def total_of(value, count):
    for bit in range(bits_of(count)):
        value = value + swap(value, "fsdp", count, 1 << bit)
    return value


def body(
    shards,
    reps,
    pixels,
    image_tokens,
    patch_class,
    resize_coarse,
    resize_fine,
    w_base,
    w_qkv,
    w_proj,
    w_fc1,
    w_fc2,
    small_params,
    first_base,
    first_qkv,
    first_proj,
    first_fc1,
    first_fc2,
    first_small,
    second_base,
    second_qkv,
    second_proj,
    second_fc1,
    second_fc2,
    second_small,
    cotangent,
):
    rows_here = pixels.shape[0]
    here = lax.axis_index("fsdp")
    there = lax.axis_index("rep")
    ids = jnp.stack([here, there]).astype(jnp.int32)
    base_rows = w_base.shape[0]
    pieced = shards == 16 and reps == 2 and w_qkv.shape[0] % 16 == 0

    segment, alive, finer = rows_plan(image_tokens[0], patch_class[0], rows_here)
    segment_col = segment[:, None]
    nothing = jnp.zeros_like(alive)
    rows = jnp.stack([nothing, alive, finer] + [nothing] * 5, axis=1)

    low_qkv = w_qkv.astype(BF)
    low_both = jnp.concatenate(
        [part for side in (0, 1) for part in (halves_of(w_proj, side), halves_of(w_fc1, side))],
        axis=1,
    ).astype(BF)
    low_fc2 = w_fc2.astype(BF)
    small_cols = small_params.shape[1]
    if pieced:
        half_cols = D // 2
        lanes = jnp.arange(D, dtype=jnp.int32)[None, :] // small_cols
        placed = jnp.where(lanes == here, jnp.tile(small_params, (1, shards)), 0.0)
        placed = jnp.pad(placed, ((0, SMALL_PAD - SMALL), (0, 0))).astype(BF)
        mine = lax.dynamic_slice_in_dim(w_base, there * half_cols, half_cols, axis=1)
        message = jnp.concatenate(
            [mine.astype(BF), placed[:, :half_cols], placed[:, half_cols:]], axis=0
        )
        gather_base = Gather(message, shards)
        gather_base.step()
        base_done = gather_base.step()
        held, places = gather_base.land(), gather_base.places
        other = swap(held, "fsdp", shards, 1)
        offsets = (tuple(places), tuple(place ^ 1 for place in places))
        part = resize_part(ids, resize_coarse, resize_fine, (held, other), offsets, base_rows)
        gather_qkv = Gather(low_qkv, shards)
        gather_qkv.step(base_done)
        qkv_done = gather_qkv.step(part)
        part = add_low(part, swap(part, "fsdp", shards, 2))
        half_rows = PIXALL // 2
        quarter = part[:half_rows][None]
        small_low = part[half_rows:]
        vectors = jnp.concatenate([small_low[:SMALL_PAD], small_low[SMALL_PAD:]], axis=1)
        quarter_rep = swap(quarter, "rep", reps, 1)
        quarter_core = swap(quarter, "fsdp", shards, 1)
        quarter_both = swap(quarter_rep, "fsdp", shards, 1)
        patch_arrays = (quarter, quarter_core, quarter_rep, quarter_both)
        patch_places = (((0, 0),), ((1, 0),), ((0, 1),), ((1, 1),))
        gather_qkv.far(quarter)
        gather_both = Gather(low_both, shards)
        gather_both.step(qkv_done, quarter)
    else:
        base = gather_whole(w_base.astype(BF), shards)
        coarse = dot_nn(resize_coarse, base).astype(BF)
        fine = dot_nn(resize_fine, base).astype(BF)
        whole = jnp.concatenate([coarse, fine, jnp.zeros((PIXALL - PIXC - PIXF, D), BF)])
        patch_arrays = (whole[None],)
        patch_places = ((None,),)
        vectors = gather_whole(small_params.astype(BF).T, shards).T
        vectors = jnp.pad(vectors, ((0, SMALL_PAD - SMALL), (0, 0)))
        weight_qkv = as_piece(gather_whole(low_qkv, shards))
        weight_both = as_piece(gather_whole(low_both, shards))
        weight_fc2 = as_piece(gather_whole(low_fc2, shards))
    vectors = vectors.astype(F32)
    bias = vectors[7:11].reshape(1, FF)

    state_zero, normed_one, patch_weight = patch(
        ids, pixels, rows, vectors, patch_arrays, patch_places
    )
    if pieced:
        weight_qkv = gather_qkv.near(state_zero)
        both_done = gather_both.step(state_zero)
    qkv = project_qkv(ids, normed_one, weight_qkv)
    chunks = 3
    pairs = HEADS // 2
    many = pairs // chunks
    if pieced:
        gather_fc2 = Gather(low_fc2, shards)
        gather_fc2.high(qkv)
    outs = [attend(ids, qkv, segment_col, 0, many)]
    after = ()
    if pieced:
        both_held = gather_both.land(outs[0][0])
        both_mine = gather_both.far_halves(there, both_held)
        after = (both_held,)
    for index in range(1, chunks):
        outs.append(attend(ids, qkv, segment_col, index * many, many, after))
        after = (outs[-1][0],)
    if pieced:
        weight_both, both_rest = gather_both.near_halves(outs[-1][0])
        gather_fc2.join(both_mine, outs[-1][0])
        gather_fc2.far()
    mixed = jnp.concatenate([out[0] for out in outs], axis=1)
    logs = [out[1] for out in outs]
    state_one, normed_two, hidden, slope = feed_up(
        ids, mixed, state_zero, vectors, bias, weight_both
    )
    if pieced:
        weight_fc2 = gather_fc2.near(state_one)
    activations, branch, grad_before, down_sums = feed_down(
        ids, hidden, slope, state_one, cotangent, rows, vectors, weight_fc2
    )

    def qkv_chunk(index, *after):
        many = pairs // chunks
        return attend_back(
            ids, qkv, segment_col, mixed, grad_mixed, logs[index], index * many, many, after
        )

    def chunk_grad(part, *after, extra=()):
        return weight_grad(
            ids, normed_one, part, shards, pieced, "grad_qkv", after, extra
        )

    def finish_embed(grads, *after):
        return embed_back(
            ids,
            grads,
            state_zero,
            grad_one,
            vectors,
            down_sums,
            middle_sums,
            weight_qkv,
            after,
        )

    part_fc2 = weight_grad(ids, hidden, branch, shards, pieced, "grad_fc2")
    if pieced:
        every = list(range(bits_of(shards)))
        near, far = every[:2], every[2:]
        sum_fc2 = Scatter(part_fc2, shards, reps, every)
        sum_fc2.step()
        part_fc1 = weight_grad(
            ids, normed_two, grad_before, shards, pieced, "grad_fc1", part_fc2
        )
        sum_fc1 = Scatter(part_fc1, shards, reps, [0, "half"] + every[1:])
        sum_fc2.land(part_fc1[0])
        sum_fc2.step()
        sum_fc1.step()
        grad_one, grad_attn, grad_mixed, middle_sums = middle_back(
            ids,
            grad_before,
            state_one,
            branch,
            vectors,
            weight_both,
            (sum_fc2.ready, part_fc1[0]),
        )
        sum_fc1.land(grad_one)
        sum_fc1.step()
        first = qkv_chunk(0, sum_fc1.ready)
        part_first = chunk_grad(first, extra=(mixed, grad_attn))
        sum_first = Scatter(part_first, shards, reps, [0, "half"] + every[1:])
        sum_fc2.land(part_first[0])
        sum_fc2.step()
        sum_first.step()
        second = qkv_chunk(1, sum_fc2.ready, part_first[0])
        sum_first.land(second)
        sum_first.step()
        sum_fc1.land(second)
        sum_fc1.step(sum_first.ready)
        part_second = chunk_grad(second, sum_first.ready, sum_fc1.ready)
        sum_second = Scatter(part_second, shards, reps, every)
        sum_fc2.land(part_second[0])
        sum_fc2.step()
        sum_second.step()
        third = qkv_chunk(2, sum_fc2.ready, part_second[0])
        sum_first.land(third)
        sum_first.step()
        sum_second.land(third)
        sum_second.step(sum_first.ready)
        part_third = chunk_grad(third, sum_second.ready, sum_first.ready)
        sum_third = Scatter(part_third, shards, reps, every)
        sum_third.step()
        sum_fc1.land(part_third[0])
        sum_fc1.step()
        patch_grad, small_part = finish_embed(
            (first, second, third), part_third[0], sum_fc1.ready
        )
        sum_third.land(patch_grad)
        sum_third.step()
        sum_first.land(patch_grad)
        sum_second.land(patch_grad)
        sum_both = merged(sum_first, sum_second, shards, reps, far)
        sum_both.step(sum_third.ready)
        patch_parts = patch_back(
            ids,
            patch_grad,
            pixels,
            rows,
            small_part,
            shards,
            pieced,
            (sum_third.ready, sum_both.ready),
        )
        sum_patch = Scatter(patch_parts, shards, reps, every, SMALL_PAD)
        sum_patch.step()
        sum_fc1.land(patch_parts[0])
        sum_fc1.step()
        sum_fc2.land(patch_parts[0])
        fc2_other = swap(sum_fc2.kept, "rep", reps, 1)
        sum_patch.land(sum_fc1.ready, sum_fc2.kept)
        sum_patch.step()
        mark = sum_patch.ready
        pixel_grad = pixel_back(ids, patch_grad, rows, patch_weight, (mark,))
        sum_third.land(pixel_grad)
        sum_third.step()
        sum_both.land(sum_third.ready)
        sum_both.step()
        sum_patch.land(sum_both.ready)
        sum_patch.step()
        mark = sum_patch.ready
        sum_fc1.land(mark)
        sum_third.land(mark)
        sum_third.step()
        sum_patch.land(sum_third.ready, sum_fc1.ready)
        sum_patch.step()
        mark = sum_patch.ready
        sum_both.land(mark)
        ends = jnp.concatenate([*rows_of(sum_fc1.kept[0]), *rows_of(sum_both.kept[0])])
        ends_other = swap(ends, "rep", reps, 1)
        sum_third.land(ends)
        grad_fc2 = add_low(sum_fc2.kept[0], tie(fc2_other, ends)[0])
        sum_patch.land(sum_third.kept)
        tail = jnp.pad(sum_third.kept[0], ((0, 0), (0, PIXALL - D)))
        tail = jnp.concatenate([sum_patch.kept, tail])
        tail = add_low(tail, swap(tail, "rep", reps, 1))
        few = w_qkv.shape[0]
        parts = [ends[at * few :][:few] for at in range(4)]
        others = [ends_other[at * few :][:few] for at in range(4)]
        low = [jnp.where(there == 0, a, b) for a, b in zip(parts, others)]
        high = [jnp.where(there == 0, b, a) for a, b in zip(parts, others)]
        grad_fc1 = jnp.concatenate(low[:2] + high[:2], axis=1)
        grad_first, grad_proj = low[2], high[2]
        grad_second = add_low(parts[3], others[3])
        split_at = SMALL_PAD + D // shards
        turned, grad_third = tail[:split_at], tail[split_at:, :D]
    else:

        def owned(parts):
            return replicas(scatter_whole(parts[0], shards), reps)

        grad_fc2 = owned(part_fc2)
        grad_fc1 = owned(
            weight_grad(ids, normed_two, grad_before, shards, pieced, "grad_fc1")
        )
        grad_one, grad_attn, grad_mixed, middle_sums = middle_back(
            ids, grad_before, state_one, branch, vectors, weight_both
        )
        grad_proj = owned(weight_grad(ids, mixed, grad_attn, shards, pieced, "grad_proj"))
        grads = [qkv_chunk(index) for index in range(chunks)]
        grad_first, grad_second, grad_third = [owned(chunk_grad(part)) for part in grads]
        patch_grad, small_part = finish_embed(grads)
        patch_parts = patch_back(ids, patch_grad, pixels, rows, small_part, shards, pieced)
        pixel_grad = pixel_back(ids, patch_grad, rows, patch_weight)
        small_all = small_part
        for bit in range(bits_of(shards)):
            small_all = add_low(small_all, swap(small_all, "fsdp", shards, 1 << bit))
        patch_all = patch_parts[0][SMALL_PAD:].reshape(shards, D // shards, PIXALL)
        turned = jnp.concatenate([replicas(small_all, reps), owned((patch_all,))])

    small_total = turned[:SMALL, :D].astype(F32)
    turned = turned[SMALL_PAD:]
    grad_small = lax.dynamic_slice_in_dim(small_total, here * small_cols, small_cols, axis=1)
    if pieced:
        pieces, square_parts = base_back(ids, turned, resize_coarse, resize_fine, shards)
        squares = jnp.sum(square_parts)
    else:
        base_cols = dot_nn(turned[:, :PIXC], resize_coarse)
        base_cols = base_cols + dot_nn(turned[:, PIXC : PIXC + PIXF], resize_fine)
        squares = jnp.sum(base_cols * base_cols)
        pieces = base_cols.astype(BF).reshape(base_cols.shape[0], shards, base_rows)
        pieces = pieces.transpose(1, 0, 2)
    pieces = lax.all_to_all(pieces, "fsdp", 0, 0)
    grad_base = pieces.reshape(D, base_rows).T
    wide = grad_first.shape[1] // 3
    grad_qkv = jnp.concatenate(
        [
            part[:, kind * wide : (kind + 1) * wide]
            for kind in range(3)
            for part in (grad_first, grad_second, grad_third)
        ],
        axis=1,
    )

    shards_of = [
        value.astype(F32) for value in (grad_base, grad_qkv, grad_proj, grad_fc1, grad_fc2)
    ] + [grad_small]
    for shard in shards_of[1:5]:
        squares = squares + jnp.sum(shard * shard)
    squares = total_of(squares, shards) + jnp.sum(small_total * small_total)
    grad_norm = jnp.sqrt(squares)
    clip = jnp.minimum(1.0, CLIP_NORM / grad_norm)
    masters = (w_base, w_qkv, w_proj, w_fc1, w_fc2, small_params)
    firsts = (first_base, first_qkv, first_proj, first_fc1, first_fc2, first_small)
    seconds = (second_base, second_qkv, second_proj, second_fc1, second_fc2, second_small)
    rates = (RATE, RATE, RATE, RATE, RATE, RATE_SMALL)
    results = [
        adamw(masters[index], shards_of[index], firsts[index], seconds[index], clip, rates[index])
        for index in range(6)
    ]
    return (activations, pixel_grad, grad_norm) + tuple(
        results[index][kind] for kind in range(3) for index in range(6)
    )


def solution(mesh):
    tokens = P(("fsdp", "rep"), None)
    split_rows = P("fsdp", None)
    states = (split_rows,) * 5 + (P(None, "fsdp"),)
    in_specs = (tokens, tokens, tokens, P(), P()) + states * 3 + (tokens,)
    out_specs = (tokens, tokens, P()) + states * 3
    step = functools.partial(body, mesh.shape["fsdp"], mesh.shape["rep"])
    return jax.shard_map(
        step, mesh=mesh, in_specs=in_specs, out_specs=out_specs, check_vma=False
    )
```
